128 devices in a mesh: outer: 8 (over y, core), inner: 16 (over x, z).
Axes of the slice: x: 4, y: 4, z: 4, core: 2. Of those that a mesh axis runs over, the one named last changes fastest.
Arguments:
- images: bfloat16 [20480, 768], P(('outer', 'inner')), may hold values from -16 to 16
- texts: bfloat16 [20480, 768], P(('outer', 'inner')), may hold values from -16 to 16
Outputs:
- image_grad: float32 [20480, 768], P(('outer', 'inner'))
- text_grad: float32 [20480, 768], P(('outer', 'inner'))
The draws below stay inside these ranges and needn't reach their ends.
All inputs are finite; a program needn't handle non-finite values.
Results may differ from the reference program's by a relative error of at most 0.0016.
Values may be sent and summed in bfloat16 or wider, within the bound.
No kernel may reach another device: no remote copies, remote signals or barrier semaphores. Data moves between devices by JAX's collectives and lax.ppermute only.
A program may use at most 64 MiB of HBM per device.

```python
import math
import jax
import jax.numpy as jnp
from jax import lax

EMBED = 768
PAIRS = 20480


def shared_parts(key):
    base_draw = jax.random.normal(jax.random.fold_in(key, 11), (PAIRS, EMBED), jnp.float32)
    return base_draw


def draw_images(key, part):
    base_draw = shared_parts(key)
    key = jax.random.fold_in(key, 1)
    noise = jax.random.normal(jax.random.fold_in(key, 2), (PAIRS, EMBED), jnp.float32)
    scales = jnp.exp(jax.random.uniform(jax.random.fold_in(key, 3), (PAIRS, 1), jnp.float32, math.log(0.8), math.log(1.25)))
    values = scales * (0.6 * base_draw + 0.8 * noise)
    return jnp.clip(values, -16.0, 16.0).astype(jnp.bfloat16)


def draw_texts(key, part):
    base_draw = shared_parts(key)
    key = jax.random.fold_in(key, 2)
    noise = jax.random.normal(jax.random.fold_in(key, 4), (PAIRS, EMBED), jnp.float32)
    scales = jnp.exp(jax.random.uniform(jax.random.fold_in(key, 5), (PAIRS, 1), jnp.float32, math.log(0.8), math.log(1.25)))
    values = scales * (0.225 * base_draw + 0.97 * noise)
    return jnp.clip(values, -16.0, 16.0).astype(jnp.bfloat16)


def setup_inputs(seed: int = 0) -> dict:
    splits = jax.random.split(jax.random.key(seed), 3)
    images = draw_images(jax.random.fold_in(splits[2], 71), 0)
    texts = draw_texts(jax.random.fold_in(splits[2], 71), 0)
    return dict(images=images, texts=texts)


def merge_pair(earlier, latter):
    highest = jnp.maximum(earlier[0], latter[0])
    return (highest, earlier[1] * jnp.exp(earlier[0] - highest) + latter[1] * jnp.exp(latter[0] - highest))

def reference(images, texts):
    score_scale = 4.0 / math.sqrt(EMBED)
    block_size = math.gcd(PAIRS, 1024)
    block_count = PAIRS // block_size
    image_blocks = images.reshape(block_count, block_size, EMBED)

    def forward(running, img_blk):
        scores = jnp.dot(img_blk, texts.T, preferred_element_type=jnp.float32) * score_scale
        row_max = lax.optimization_barrier(jnp.max(scores, axis=1))
        row_lse = row_max + jnp.log(lax.optimization_barrier(jnp.sum(jnp.exp(scores - row_max[:, None]), axis=1)))
        blk_max = lax.optimization_barrier(jnp.max(scores, axis=0))
        blk_sum = lax.optimization_barrier(jnp.sum(jnp.exp(scores - blk_max[None, :]), axis=0))
        return (merge_pair(running, (blk_max, blk_sum)), row_lse)
    initial = (jnp.full((PAIRS,), -jnp.inf, jnp.float32), jnp.zeros((PAIRS,), jnp.float32))
    column_state, row_lse = lax.scan(forward, initial, image_blocks)
    col_lse = column_state[0] + jnp.log(column_state[1])

    def backward(text_acc, inputs):
        img_blk, lse_blk = inputs
        scores = jnp.dot(img_blk, texts.T, preferred_element_type=jnp.float32) * score_scale
        weights = (jnp.exp(scores - lse_blk[:, None]) + jnp.exp(scores - col_lse[None, :])).astype(jnp.bfloat16)
        image_part = 0.5 * jnp.dot(weights, texts, preferred_element_type=jnp.float32)
        text_acc = text_acc + jnp.dot(weights.T, img_blk, preferred_element_type=jnp.float32)
        return (text_acc, image_part)
    text_acc, image_parts = lax.scan(backward, jnp.zeros((PAIRS, EMBED), jnp.float32), (image_blocks, row_lse))
    image_grad = image_parts.reshape(PAIRS, EMBED) - texts.astype(jnp.float32)
    text_grad = 0.5 * text_acc - images.astype(jnp.float32)
    return (image_grad, text_grad)
```

```python
import functools
import math

import jax
import jax.numpy as jnp
from jax import lax
from jax.experimental import pallas as pl
from jax.experimental.pallas import tpu as pltpu
from jax.sharding import Mesh, PartitionSpec as P

AXES = ("y", "core", "x", "z")
SIZES = (4, 2, 4, 4)
ORDER = (0, 1, 2, 4, 3, 5, 6, 7)
PLACE = tuple(ORDER.index(m) for m in range(8))
LOG2E = 1.4426950408889634
VMEM_LIMIT = 56 * 1024 * 1024


def flat(y, c, x, z):
    return ((y * 2 + c) * 4 + x) * 4 + z


def coords():
    for y in range(4):
        for c in range(2):
            for x in range(4):
                for z in range(4):
                    yield y, c, x, z


def partner(v, c):
    return v ^ 1 if c == 0 else 3 - v


def across(m):
    pairs = []
    for y, c, x, z in coords():
        target = (
            partner(y, c) if m & 2 else y,
            c,
            partner(x, c) if m & 1 else x,
            partner(z, c) if m & 4 else z,
        )
        pairs.append((flat(y, c, x, z), flat(*target)))
    return pairs


SWAP = [(flat(y, c, x, z), flat(y, 1 - c, x, z)) for y, c, x, z in coords()]


def cube_groups():
    groups = []
    seen = set()
    for y, c, x, z in coords():
        members = []
        for m in range(8):
            yy = partner(y, c) if m & 2 else y
            xx = partner(x, c) if m & 1 else x
            zz = partner(z, c) if m & 4 else z
            place = (xx & 1) | ((yy & 1) << 1) | ((zz & 1) << 2)
            members.append((place, flat(yy, c, xx, zz)))
        key = tuple(d for _, d in sorted(members))
        if key not in seen:
            seen.add(key)
            groups.append(list(key))
    return groups


GROUPS = cube_groups()


def to_cube(a, m):
    return lax.ppermute(a, AXES, across(m))


def swap(a):
    return lax.ppermute(a, AXES, SWAP)


def column_of(row, rows):
    padded = -(-rows // 128) * 128
    wide = jnp.broadcast_to(row, (128, rows))
    if padded != rows:
        wide = jnp.concatenate([wide, jnp.zeros((128, padded - rows), jnp.float32)], axis=1)
    return wide.T[:rows, :1]


def row_of(column, rows):
    padded = -(-rows // 128) * 128
    wide = jnp.broadcast_to(column, (rows, 128))
    if padded != rows:
        wide = jnp.concatenate([wide, jnp.zeros((padded - rows, 128), jnp.float32)], axis=0)
    return wide.T[:1, :rows]


def load_blocks(core, a_refs, b_refs, a_s, b_s, a_sem, b_sem):
    rows = a_refs[0].shape[0]
    for k in range(8):
        pltpu.make_async_copy(a_refs[k], a_s.at[pl.ds(k * rows, rows)], a_sem.at[k]).start()
        stage = (k // 4) ^ core
        start = pl.multiple_of((stage * 4 + k % 4) * rows, 16)
        pltpu.make_async_copy(b_refs[k], b_s.at[pl.ds(start, rows)], b_sem.at[stage * 4 + k % 4]).start()


def wait_half(h, a_refs, b_refs, a_s, b_s, a_sem, b_sem):
    rows = a_refs[0].shape[0]
    for j in range(4):
        k = h * 4 + j
        pltpu.make_async_copy(a_refs[k], a_s.at[pl.ds(k * rows, rows)], a_sem.at[k]).wait()
        pltpu.make_async_copy(b_refs[k], b_s.at[pl.ds(k * rows, rows)], b_sem.at[k]).wait()


def scores_kernel(scale, core_ref, *refs):
    a_refs, b_refs = refs[:8], refs[8:16]
    s_ref, a_stat, b_stat = refs[16:19]
    a_s, b_s, col_m, col_s, a_sem, b_sem = refs[19:]
    rows = a_refs[0].shape[0]
    half = 4 * rows
    core = core_ref[0]
    step = pl.program_id(0)

    @pl.when(step == 0)
    def _():
        load_blocks(core, a_refs, b_refs, a_s, b_s, a_sem, b_sem)
        wait_half(0, a_refs, b_refs, a_s, b_s, a_sem, b_sem)

    @pl.when(step == 4)
    def _():
        wait_half(1, a_refs, b_refs, a_s, b_s, a_sem, b_sem)

    quadrant = step // 4
    a_blk = a_s[pl.ds(pl.multiple_of(step * rows, 16), rows), :]
    b_half = b_s[pl.ds(pl.multiple_of(quadrant * half, 16), half), :]
    s = lax.dot_general(a_blk, b_half, (((1,), (1,)), ((), ())), preferred_element_type=jnp.float32) * scale
    s_ref[0] = s
    row_m = jnp.max(s, axis=1, keepdims=True)
    row_sum = jnp.sum(jnp.exp2(s - row_m), axis=1, keepdims=True)
    a_stat[pl.ds(step, 1), :] = row_of(row_m + jnp.log2(row_sum), rows)
    blk_m = jnp.max(s, axis=0, keepdims=True)
    blk_s = jnp.sum(jnp.exp2(s - blk_m), axis=0, keepdims=True)

    @pl.when(step % 4 == 0)
    def _():
        col_m[...] = blk_m
        col_s[...] = blk_s

    @pl.when(step % 4 != 0)
    def _():
        before = col_m[...]
        top = jnp.maximum(before, blk_m)
        col_s[...] = col_s[...] * jnp.exp2(before - top) + blk_s * jnp.exp2(blk_m - top)
        col_m[...] = top

    @pl.when(step % 4 == 3)
    def _():
        lse = col_m[...] + jnp.log2(col_s[...])
        for j in range(4):
            b_stat[pl.ds((quadrant ^ core) * 4 + j, 1), :] = lse[:, j * rows : (j + 1) * rows]


def any_spec():
    return pl.BlockSpec(memory_space=pl.ANY)


def scores_call(core, a_blocks, b_blocks, scale):
    rows, features = a_blocks[0].shape
    half = 4 * rows
    stat = jax.ShapeDtypeStruct((8, rows), jnp.float32)
    return pl.pallas_call(
        functools.partial(scores_kernel, scale),
        grid=(8,),
        in_specs=[pl.BlockSpec(memory_space=pltpu.SMEM)] + [any_spec()] * 16,
        out_specs=[
            pl.BlockSpec((1, rows, half), lambda i: (i, 0, 0)),
            pl.BlockSpec((8, rows), lambda i: (0, 0)),
            pl.BlockSpec((8, rows), lambda i: (0, 0)),
        ],
        out_shape=[jax.ShapeDtypeStruct((8, rows, half), jnp.float32), stat, stat],
        scratch_shapes=[
            pltpu.VMEM((8 * rows, features), jnp.bfloat16),
            pltpu.VMEM((8 * rows, features), jnp.bfloat16),
            pltpu.VMEM((1, half), jnp.float32),
            pltpu.VMEM((1, half), jnp.float32),
            pltpu.SemaphoreType.DMA((8,)),
            pltpu.SemaphoreType.DMA((8,)),
        ],
        compiler_params=pltpu.CompilerParams(vmem_limit_bytes=VMEM_LIMIT),
        cost_estimate=pl.CostEstimate(
            flops=2 * 8 * rows * half * features, bytes_accessed=32 * rows * half, transcendentals=16 * rows * half
        ),
        name="scores",
    )(core, *a_blocks, *b_blocks)


def merge_kernel(place_ref, got_ref, out_ref):
    me = place_ref[0]
    for m in range(8):
        parts = []
        for k in range(8):
            offset = (me ^ k) ^ m
            row = jnp.int32(0)
            for n in range(8):
                row = jnp.where(offset == n, PLACE[n], row)
            parts.append(got_ref[k, pl.ds(row, 1), :])
        top = functools.reduce(jnp.maximum, parts)
        total = functools.reduce(jnp.add, [jnp.exp2(p - top) for p in parts])
        out_ref[PLACE[m] : PLACE[m] + 1, :] = top + jnp.log2(total)


def merge_call(place, got):
    return pl.pallas_call(
        merge_kernel,
        in_specs=[pl.BlockSpec(memory_space=pltpu.SMEM), pl.BlockSpec(memory_space=pltpu.VMEM)],
        out_specs=pl.BlockSpec(memory_space=pltpu.VMEM),
        out_shape=jax.ShapeDtypeStruct(got.shape[1:], jnp.float32),
        name="merge",
    )(place, got)


def grads_kernel(core_ref, *refs):
    s_ref, a_lse, b_lse = refs[:3]
    a_refs, b_refs = refs[3:11], refs[11:19]
    ga, gb, gb0 = refs[19:22]
    a_s, b_s, w_s, col, a_sem, b_sem = refs[22:]
    rows = a_refs[0].shape[0]
    half = 4 * rows
    core = core_ref[0]
    step = pl.program_id(0)
    quadrant = step // 4

    @pl.when(step == 0)
    def _():
        load_blocks(core, a_refs, b_refs, a_s, b_s, a_sem, b_sem)
        wait_half(0, a_refs, b_refs, a_s, b_s, a_sem, b_sem)

    @pl.when(step == 4)
    def _():
        wait_half(1, a_refs, b_refs, a_s, b_s, a_sem, b_sem)

    @pl.when(step % 4 == 0)
    def _():
        col[...] = jnp.concatenate(
            [b_lse[pl.ds((quadrant ^ core) * 4 + j, 1), :] for j in range(4)], axis=1
        )

    s = s_ref[0]
    lse = column_of(a_lse[pl.ds(step, 1), :], rows)
    w = (jnp.exp2(s - lse) + jnp.exp2(s - col[...])).astype(jnp.bfloat16)
    w_s[pl.ds(pl.multiple_of((step % 4) * rows, 16), rows), :] = w
    b_half = b_s[pl.ds(pl.multiple_of(quadrant * half, 16), half), :]
    ga[0] = 0.5 * jnp.dot(w, b_half, preferred_element_type=jnp.float32)

    @pl.when(step % 4 == 3)
    def _():
        a_half = a_s[pl.ds(pl.multiple_of(quadrant * half, 16), half), :]
        for j in range(4):
            g = 0.5 * lax.dot_general(
                w_s[:, j * rows : (j + 1) * rows],
                a_half,
                (((0,), (0,)), ((), ())),
                preferred_element_type=jnp.float32,
            )
            gb[pl.ds((quadrant ^ core) * 4 + j, 1)] = g.astype(jnp.bfloat16)[None]
            if j == 0:

                @pl.when(quadrant == core)
                def _():
                    gb0[...] = g


def grads_call(core, s, a_lse, b_lse, a_blocks, b_blocks):
    rows, features = a_blocks[0].shape
    half = 4 * rows
    return pl.pallas_call(
        grads_kernel,
        grid=(8,),
        in_specs=[
            pl.BlockSpec(memory_space=pltpu.SMEM),
            pl.BlockSpec((1, rows, half), lambda i: (i, 0, 0)),
            pl.BlockSpec((8, rows), lambda i: (0, 0)),
            pl.BlockSpec((8, rows), lambda i: (0, 0)),
        ]
        + [any_spec()] * 16,
        out_specs=[
            pl.BlockSpec((1, rows, features), lambda i: (i, 0, 0)),
            pl.BlockSpec((8, rows, features), lambda i: (0, 0, 0)),
            pl.BlockSpec((rows, features), lambda i: (0, 0)),
        ],
        out_shape=[
            jax.ShapeDtypeStruct((8, rows, features), jnp.float32),
            jax.ShapeDtypeStruct((8, rows, features), jnp.bfloat16),
            jax.ShapeDtypeStruct((rows, features), jnp.float32),
        ],
        scratch_shapes=[
            pltpu.VMEM((8 * rows, features), jnp.bfloat16),
            pltpu.VMEM((8 * rows, features), jnp.bfloat16),
            pltpu.VMEM((half, half), jnp.bfloat16),
            pltpu.VMEM((1, half), jnp.float32),
            pltpu.SemaphoreType.DMA((8,)),
            pltpu.SemaphoreType.DMA((8,)),
        ],
        compiler_params=pltpu.CompilerParams(vmem_limit_bytes=VMEM_LIMIT),
        cost_estimate=pl.CostEstimate(
            flops=4 * 8 * rows * half * features, bytes_accessed=32 * rows * half, transcendentals=16 * rows * half
        ),
        name="grads",
    )(core, s, a_lse, b_lse, *a_blocks, *b_blocks)


def body(images, texts):
    rows, features = images.shape
    scale = 4.0 / math.sqrt(features) * LOG2E
    core = lax.axis_index("core")
    first = core == 0
    core_arr = core.astype(jnp.int32).reshape(1)
    place = (
        (lax.axis_index("x") & 1) | ((lax.axis_index("y") & 1) << 1) | ((lax.axis_index("z") & 1) << 2)
    ).astype(jnp.int32).reshape(1)

    mine = jnp.where(first, images, texts)
    other = swap(jnp.where(first, texts, images))
    own = jnp.concatenate([mine, other], axis=0)
    near = {m: to_cube(own, m) for m in (1, 2, 4)}
    blocks = {0: own, **near}
    blocks[3] = to_cube(near[2], 1)
    blocks[6] = to_cube(near[4], 2)
    blocks[5] = to_cube(near[1], 4)
    blocks[7] = to_cube(near[1], 6)
    a_blocks = [blocks[m] for m in ORDER]
    b_blocks = [swap(blocks[m]) for m in ORDER]

    s, a_stat, b_stat = scores_call(core_arr, a_blocks, b_blocks, scale)
    chip_stat = jnp.logaddexp2(a_stat, swap(b_stat))
    got = lax.all_to_all(
        jnp.broadcast_to(chip_stat[None], (8,) + chip_stat.shape), AXES, 0, 0, axis_index_groups=GROUPS
    )
    a_lse = merge_call(place, got)
    b_lse = swap(a_lse)

    ga, gb, gb0 = grads_call(core_arr, s, a_lse, b_lse, a_blocks, b_blocks)
    gb_other = {m: swap(gb[PLACE[m]]) for m in range(1, 8)}
    gb0_other = swap(gb0)

    def chip_part(m):
        return ga[PLACE[m]] + gb_other[m].astype(jnp.float32)

    def narrow(a):
        return a.astype(jnp.bfloat16)

    from_xy = to_cube(narrow(chip_part(3)), 1)
    from_yz = to_cube(narrow(chip_part(6)), 2)
    from_xz = to_cube(narrow(chip_part(5)), 4)
    from_xyz = to_cube(narrow(chip_part(7)), 6)
    wide = lambda a: a.astype(jnp.float32)
    from_x = to_cube(narrow(chip_part(1) + wide(from_xz) + wide(from_xyz)), 1)
    from_y = to_cube(narrow(chip_part(2) + wide(from_xy)), 2)
    from_z = to_cube(narrow(chip_part(4) + wide(from_yz)), 4)
    total = ga[0] + gb0_other + wide(from_x) + wide(from_y) + wide(from_z)
    kept, sent = total[:rows], total[rows:]
    got_sum = swap(sent)
    image_sum = jnp.where(first, kept, got_sum)
    text_sum = jnp.where(first, got_sum, kept)
    return (image_sum - wide(texts), text_sum - wide(images))


def solution(mesh):
    chips = Mesh(mesh.devices.reshape(SIZES), AXES)
    spec = P(AXES, None)
    return jax.shard_map(
        body,
        mesh=chips,
        in_specs=(spec, spec),
        out_specs=(spec, spec),
        check_vma=False,
    )
```

```python
import functools
import math

import jax
import jax.numpy as jnp
from jax import lax
from jax.experimental import pallas as pl
from jax.experimental.pallas import tpu as pltpu
from jax.sharding import Mesh, PartitionSpec as P

AXES = ("y", "core", "x", "z")
SIZES = (4, 2, 4, 4)
ORDER = (0, 1, 2, 4, 3, 5, 6, 7)
PLACE = tuple(ORDER.index(m) for m in range(8))
LOG2E = 1.4426950408889634
VMEM_LIMIT = 36 * 1024 * 1024
RANGE = 60.0


def flat(y, c, x, z):
    return ((y * 2 + c) * 4 + x) * 4 + z


def coords():
    for y in range(4):
        for c in range(2):
            for x in range(4):
                for z in range(4):
                    yield y, c, x, z


def partner(v, c):
    return v ^ 1 if c == 0 else 3 - v


def across(m):
    pairs = []
    for y, c, x, z in coords():
        target = (
            partner(y, c) if m & 2 else y,
            c,
            partner(x, c) if m & 1 else x,
            partner(z, c) if m & 4 else z,
        )
        pairs.append((flat(y, c, x, z), flat(*target)))
    return pairs


SWAP = [(flat(y, c, x, z), flat(y, 1 - c, x, z)) for y, c, x, z in coords()]


def cube_groups():
    groups = []
    seen = set()
    for y, c, x, z in coords():
        members = []
        for m in range(8):
            yy = partner(y, c) if m & 2 else y
            xx = partner(x, c) if m & 1 else x
            zz = partner(z, c) if m & 4 else z
            place = (xx & 1) | ((yy & 1) << 1) | ((zz & 1) << 2)
            members.append((place, flat(yy, c, xx, zz)))
        key = tuple(d for _, d in sorted(members))
        if key not in seen:
            seen.add(key)
            groups.append(list(key))
    return groups


GROUPS = cube_groups()


def to_cube(a, m):
    return lax.ppermute(a, AXES, across(m))


def swap(a):
    return lax.ppermute(a, AXES, SWAP)


def column_of(row, rows):
    padded = -(-rows // 128) * 128
    wide = jnp.broadcast_to(row, (128, rows))
    if padded != rows:
        wide = jnp.concatenate([wide, jnp.zeros((128, padded - rows), jnp.float32)], axis=1)
    return wide.T[:rows, :1]


def row_of(column, rows):
    padded = -(-rows // 128) * 128
    wide = jnp.broadcast_to(column, (rows, 128))
    if padded != rows:
        wide = jnp.concatenate([wide, jnp.zeros((padded - rows, 128), jnp.float32)], axis=0)
    return wide.T[:1, :rows]


def any_spec():
    return pl.BlockSpec(memory_space=pl.ANY)


def vmem_spec():
    return pl.BlockSpec(memory_space=pltpu.VMEM)


def smem_spec():
    return pl.BlockSpec(memory_space=pltpu.SMEM)


def cost(matmuls, rows, cols, depth, passes=0):
    return pl.CostEstimate(
        flops=2 * matmuls * rows * cols * depth, bytes_accessed=passes * rows * cols, transcendentals=0
    )


def params():
    return pltpu.CompilerParams(vmem_limit_bytes=VMEM_LIMIT)


def dot_nt(a, b):
    return lax.dot_general(a, b, (((1,), (1,)), ((), ())), preferred_element_type=jnp.float32)


def dot_tn(a, b):
    return lax.dot_general(a, b, (((0,), (0,)), ((), ())), preferred_element_type=jnp.float32)


def join_kernel(b0, b1, b2, b3, out, sem):
    rows = b0.shape[0]
    copies = [
        pltpu.make_async_copy(b, out.at[pl.ds(j * rows, rows)], sem.at[j]) for j, b in enumerate((b0, b1, b2, b3))
    ]
    for c in copies:
        c.start()
    for c in copies:
        c.wait()


def join_call(blocks):
    rows, features = blocks[0].shape
    return pl.pallas_call(
        join_kernel,
        in_specs=[any_spec()] * 4,
        out_specs=any_spec(),
        out_shape=jax.ShapeDtypeStruct((4 * rows, features), blocks[0].dtype),
        scratch_shapes=[pltpu.SemaphoreType.DMA((4,))],
        name="join",
    )(*blocks)


def scores_kernel(scale, core_ref, a_lo, b_lo, *refs):
    a_hi, b_hi = refs[:4], refs[4:8]
    e_ref, a_cat, b_cat, a_stat, b_stat, flags, col_m, col_s, sem = refs[8:]
    rows = a_hi[0].shape[0]
    half = 4 * rows
    core = core_ref[0]

    def copies_a(h):
        if h == 0:
            return [pltpu.make_async_copy(a_lo, a_cat.at[0], sem.at[0])]
        return [pltpu.make_async_copy(a_hi[j], a_cat.at[1, pl.ds(j * rows, rows)], sem.at[1 + j]) for j in range(4)]

    def copies_b(h):
        place = core if h == 0 else 1 - core
        if h == 0:
            return [pltpu.make_async_copy(b_lo, b_cat.at[place], sem.at[5])]
        return [
            pltpu.make_async_copy(b_hi[j], b_cat.at[place, pl.ds(j * rows, rows)], sem.at[6 + j]) for j in range(4)
        ]

    for c in copies_b(0) + copies_a(0) + copies_b(1) + copies_a(1):
        c.start()

    def quadrant(q):
        for c in copies_a(q):
            c.wait()
        for h in range(2):

            @pl.when((h ^ core) == q)
            def _():
                for c in copies_b(h):
                    c.wait()

        b_half = b_cat[q]
        sums = []
        col = None
        for r in range(4):
            sl = slice(r * rows, (r + 1) * rows)
            e = jnp.exp2(dot_nt(a_cat[q, sl, :], b_half) * scale)
            e_ref[q, sl, :] = e
            sums.append(jnp.sum(e, axis=1, keepdims=True))
            part = jnp.sum(e, axis=0, keepdims=True)
            col = part if col is None else col + part
        row_lse = jnp.log2(row_of(jnp.concatenate(sums, axis=0), half))
        col_lse = jnp.log2(col)
        for j in range(4):
            sl = slice(j * rows, (j + 1) * rows)
            a_stat[4 * q + j : 4 * q + j + 1, :] = row_lse[:, sl]
            b_stat[pl.ds((q ^ core) * 4 + j, 1), :] = col_lse[:, sl]
        reach = jnp.max(jnp.maximum(jnp.abs(row_lse), jnp.abs(col_lse)))
        bad = jnp.logical_not(reach <= RANGE)
        flags[q] = bad.astype(jnp.int32)

        @pl.when(bad)
        def _():
            col_m[...] = jnp.full_like(col_m, -jnp.inf)
            col_s[...] = jnp.zeros_like(col_s)

            @pl.loop(0, 4)
            def _(r):
                sl = pl.ds(pl.multiple_of(r * rows, 16), rows)
                s = dot_nt(a_cat[q, sl, :], b_cat[q]) * scale
                e_ref[q, sl, :] = s
                row_m = jnp.max(s, axis=1, keepdims=True)
                row_s = jnp.sum(jnp.exp2(s - row_m), axis=1, keepdims=True)
                a_stat[pl.ds(4 * q + r, 1), :] = row_of(row_m + jnp.log2(row_s), rows)
                blk_m = jnp.max(s, axis=0, keepdims=True)
                blk_s = jnp.sum(jnp.exp2(s - blk_m), axis=0, keepdims=True)
                before = col_m[...]
                top = jnp.maximum(before, blk_m)
                col_s[...] = col_s[...] * jnp.exp2(before - top) + blk_s * jnp.exp2(blk_m - top)
                col_m[...] = top

            lse = col_m[...] + jnp.log2(col_s[...])
            for j in range(4):
                b_stat[pl.ds((q ^ core) * 4 + j, 1), :] = lse[:, j * rows : (j + 1) * rows]

    quadrant(0)
    quadrant(1)


def scores_call(core, a_lo, b_lo, a_hi, b_hi, scale):
    rows, features = a_hi[0].shape
    half = 4 * rows
    stat = jax.ShapeDtypeStruct((8, rows), jnp.float32)
    return pl.pallas_call(
        functools.partial(scores_kernel, scale),
        in_specs=[smem_spec()] + [any_spec()] * 10,
        out_specs=[vmem_spec()] * 5 + [smem_spec()],
        out_shape=[
            pltpu.VMEM((2, half, half), jnp.float32),
            pltpu.VMEM((2, half, features), jnp.bfloat16),
            pltpu.VMEM((2, half, features), jnp.bfloat16),
            stat,
            stat,
            jax.ShapeDtypeStruct((2,), jnp.int32),
        ],
        scratch_shapes=[
            pltpu.VMEM((1, half), jnp.float32),
            pltpu.VMEM((1, half), jnp.float32),
            pltpu.SemaphoreType.DMA((10,)),
        ],
        compiler_params=params(),
        cost_estimate=cost(2, half, half, features),
        name="scores",
    )(core, a_lo, b_lo, *a_hi, *b_hi)


def merge_kernel(place_ref, got_ref, out_ref):
    me = place_ref[0]
    for m in range(8):
        parts = []
        for k in range(8):
            offset = (me ^ k) ^ m
            row = jnp.int32(0)
            for n in range(8):
                row = jnp.where(offset == n, PLACE[n], row)
            parts.append(got_ref[k, pl.ds(row, 1), :])
        top = functools.reduce(jnp.maximum, parts)
        total = functools.reduce(jnp.add, [jnp.exp2(p - top) for p in parts])
        out_ref[PLACE[m] : PLACE[m] + 1, :] = top + jnp.log2(total)


def merge_call(place, got):
    return pl.pallas_call(
        merge_kernel,
        in_specs=[pl.BlockSpec(memory_space=pltpu.SMEM), pl.BlockSpec(memory_space=pltpu.VMEM)],
        out_specs=pl.BlockSpec(memory_space=pltpu.VMEM),
        out_shape=jax.ShapeDtypeStruct(got.shape[1:], jnp.float32),
        name="merge",
    )(place, got)


def weights_kernel(core_ref, flags, e_ref, a_lse, b_lse, a_cat, w_ref, gb_hi):
    rows = a_lse.shape[1]
    half = 4 * rows
    core = core_ref[0]
    for q in range(2):
        a_row = jnp.concatenate([a_lse[4 * q + j : 4 * q + j + 1, :] for j in range(4)], axis=1)
        b_row = jnp.concatenate([b_lse[pl.ds((q ^ core) * 4 + j, 1), :] for j in range(4)], axis=1)

        @pl.when(flags[q] == 0)
        def _():
            a_col = column_of(jnp.exp2(-a_row), half)
            b_exp = jnp.exp2(-b_row)
            for r in range(4):
                sl = slice(r * rows, (r + 1) * rows)
                w_ref[q, sl, :] = (e_ref[q, sl, :] * (a_col[sl, :] + b_exp)).astype(jnp.bfloat16)

        @pl.when(flags[q] != 0)
        def _():
            a_col = column_of(a_row, half)
            for r in range(4):
                sl = slice(r * rows, (r + 1) * rows)
                s = e_ref[q, sl, :]
                w_ref[q, sl, :] = (jnp.exp2(s - a_col[sl, :]) + jnp.exp2(s - b_row)).astype(jnp.bfloat16)

    q = 1 - core
    gb_hi[...] = (0.5 * dot_tn(w_ref[q], a_cat[q])).astype(jnp.bfloat16)


def weights_call(core, flags, e, a_lse, b_lse, a_cat):
    _, half, features = a_cat.shape
    return pl.pallas_call(
        weights_kernel,
        in_specs=[smem_spec()] * 2 + [vmem_spec()] * 4,
        out_specs=[vmem_spec()] * 2,
        out_shape=[
            pltpu.VMEM((2, half, half), jnp.bfloat16),
            jax.ShapeDtypeStruct((half, features), jnp.bfloat16),
        ],
        compiler_params=params(),
        cost_estimate=cost(1, half, half, features, 12),
        name="weights",
    )(core, flags, e, a_lse, b_lse, a_cat)


def middle_kernel(core_ref, w_ref, a_cat, b_cat, ga_hi, gb0, gb_lo):
    rows = gb0.shape[0]
    q = core_ref[0]
    g = 0.5 * dot_tn(w_ref[q], a_cat[q])
    gb0[...] = g[:rows]
    gb_lo[...] = g[rows:].astype(jnp.bfloat16)
    ga_hi[...] = 0.5 * jnp.dot(w_ref[1], b_cat[1], preferred_element_type=jnp.float32)


def middle_call(core, w, a_cat, b_cat):
    _, half, features = a_cat.shape
    rows = half // 4
    return pl.pallas_call(
        middle_kernel,
        in_specs=[smem_spec()] + [vmem_spec()] * 3,
        out_specs=[vmem_spec()] * 3,
        out_shape=[
            pltpu.VMEM((half, features), jnp.float32),
            jax.ShapeDtypeStruct((rows, features), jnp.float32),
            jax.ShapeDtypeStruct((half - rows, features), jnp.bfloat16),
        ],
        compiler_params=params(),
        cost_estimate=cost(2, half, half, features),
        name="middle",
    )(core, w, a_cat, b_cat)


def far_kernel(ga_hi, got, *outs):
    rows = outs[0].shape[0]
    for j in range(4):
        sl = slice(j * rows, (j + 1) * rows)
        outs[j][...] = (ga_hi[sl, :] + got[sl, :].astype(jnp.float32)).astype(jnp.bfloat16)


def far_call(ga_hi, got):
    half, features = ga_hi.shape
    rows = half // 4
    return pl.pallas_call(
        far_kernel,
        in_specs=[vmem_spec()] * 2,
        out_specs=[vmem_spec()] * 4,
        out_shape=[jax.ShapeDtypeStruct((rows, features), jnp.bfloat16)] * 4,
        compiler_params=params(),
        cost_estimate=cost(0, half, features, 1, 8),
        name="far",
    )(ga_hi, got)


def last_kernel(w_ref, b_cat, ga_lo):
    ga_lo[...] = 0.5 * jnp.dot(w_ref[0], b_cat[0], preferred_element_type=jnp.float32)


def last_call(w, b_cat):
    _, half, features = b_cat.shape
    return pl.pallas_call(
        last_kernel,
        in_specs=[vmem_spec()] * 2,
        out_specs=vmem_spec(),
        out_shape=pltpu.VMEM((half, features), jnp.float32),
        compiler_params=params(),
        cost_estimate=cost(1, half, half, features),
        name="last",
    )(w, b_cat)


def near_kernel(ga_lo, got0, got_lo, r_xy, r_yz, r_xz, r_xyz, p0, p1, p2, p4):
    rows = p0.shape[0]
    wide = lambda ref: ref[...].astype(jnp.float32)
    p0[...] = ga_lo[:rows] + got0[...]
    part = lambda j: ga_lo[j * rows : (j + 1) * rows, :] + got_lo[(j - 1) * rows : j * rows, :].astype(jnp.float32)
    p1[...] = (part(1) + wide(r_xz) + wide(r_xyz)).astype(jnp.bfloat16)
    p2[...] = (part(2) + wide(r_xy)).astype(jnp.bfloat16)
    p4[...] = (part(3) + wide(r_yz)).astype(jnp.bfloat16)


def near_call(ga_lo, got0, got_lo, *received):
    rows, features = got0.shape
    narrow = jax.ShapeDtypeStruct((rows, features), jnp.bfloat16)
    return pl.pallas_call(
        near_kernel,
        in_specs=[vmem_spec()] * 7,
        out_specs=[vmem_spec()] * 4,
        out_shape=[pltpu.VMEM((rows, features), jnp.float32)] + [narrow] * 3,
        compiler_params=params(),
        cost_estimate=cost(0, 4 * rows, features, 1, 12),
        name="near",
    )(ga_lo, got0, got_lo, *received)


def body(images, texts):
    rows, features = images.shape
    scale = 4.0 / math.sqrt(features) * LOG2E
    core = lax.axis_index("core")
    first = core == 0
    core_arr = core.astype(jnp.int32).reshape(1)
    place = (
        (lax.axis_index("x") & 1) | ((lax.axis_index("y") & 1) << 1) | ((lax.axis_index("z") & 1) << 2)
    ).astype(jnp.int32).reshape(1)

    mine = jnp.where(first, images, texts)
    other = swap(jnp.where(first, texts, images))
    own = jnp.concatenate([mine, other], axis=0)
    near = {m: to_cube(own, m) for m in (1, 2, 4)}
    far = {3: to_cube(near[2], 1), 6: to_cube(near[4], 2), 5: to_cube(near[1], 4), 7: to_cube(near[1], 6)}
    a_lo = join_call([own, near[1], near[2], near[4]])
    b_lo = swap(a_lo)
    a_hi = [far[m] for m in ORDER[4:]]
    b_hi = [swap(a) for a in a_hi]

    e, a_cat, b_cat, a_stat, b_stat, flags = scores_call(core_arr, a_lo, b_lo, a_hi, b_hi, scale)
    chip_stat = jnp.logaddexp2(a_stat, swap(b_stat))
    got = lax.all_to_all(
        jnp.broadcast_to(chip_stat[None], (8,) + chip_stat.shape), AXES, 0, 0, axis_index_groups=GROUPS
    )
    a_lse = merge_call(place, got)
    b_lse = swap(a_lse)

    w, gb_hi = weights_call(core_arr, flags, e, a_lse, b_lse, a_cat)
    got_hi = swap(gb_hi)
    ga_hi, gb0, gb_lo = middle_call(core_arr, w, a_cat, b_cat)
    got0, got_lo = swap(gb0), swap(gb_lo)
    p = dict(zip(ORDER[4:], far_call(ga_hi, got_hi)))
    from_xyz = to_cube(p[7], 6)
    from_xy = to_cube(p[3], 1)
    from_yz = to_cube(p[6], 2)
    from_xz = to_cube(p[5], 4)
    ga_lo = last_call(w, b_cat)
    p0, p1, p2, p4 = near_call(ga_lo, got0, got_lo, from_xy, from_yz, from_xz, from_xyz)
    wide = lambda a: a.astype(jnp.float32)
    total = p0 + wide(to_cube(p1, 1)) + wide(to_cube(p2, 2)) + wide(to_cube(p4, 4))
    kept, sent = total[:rows], total[rows:]
    got_sum = swap(sent)
    image_sum = jnp.where(first, kept, got_sum)
    text_sum = jnp.where(first, got_sum, kept)
    return (image_sum - wide(texts), text_sum - wide(images))


def solution(mesh):
    chips = Mesh(mesh.devices.reshape(SIZES), AXES)
    spec = P(AXES, None)
    return jax.shard_map(
        body,
        mesh=chips,
        in_specs=(spec, spec),
        out_specs=(spec, spec),
        check_vma=False,
    )
```

```python
import functools
import math

import jax
import jax.numpy as jnp
from jax import lax
from jax.experimental import pallas as pl
from jax.experimental.pallas import tpu as pltpu
from jax.sharding import Mesh, PartitionSpec as P

AXES = ("y", "core", "x", "z")
SIZES = (4, 2, 4, 4)
ORDER = (0, 1, 2, 4, 3, 5, 6, 7)
PLACE = tuple(ORDER.index(m) for m in range(8))
LOG2E = 1.4426950408889634
VMEM_LIMIT = 20 * 1024 * 1024
RANGE = 60.0


def flat(y, c, x, z):
    return ((y * 2 + c) * 4 + x) * 4 + z


def coords():
    for y in range(4):
        for c in range(2):
            for x in range(4):
                for z in range(4):
                    yield y, c, x, z


def partner(v, c):
    return v ^ 1 if c == 0 else 3 - v


def across(m):
    pairs = []
    for y, c, x, z in coords():
        target = (
            partner(y, c) if m & 2 else y,
            c,
            partner(x, c) if m & 1 else x,
            partner(z, c) if m & 4 else z,
        )
        pairs.append((flat(y, c, x, z), flat(*target)))
    return pairs


SWAP = [(flat(y, c, x, z), flat(y, 1 - c, x, z)) for y, c, x, z in coords()]


def cube_groups():
    groups = []
    seen = set()
    for y, c, x, z in coords():
        members = []
        for m in range(8):
            yy = partner(y, c) if m & 2 else y
            xx = partner(x, c) if m & 1 else x
            zz = partner(z, c) if m & 4 else z
            place = (xx & 1) | ((yy & 1) << 1) | ((zz & 1) << 2)
            members.append((place, flat(yy, c, xx, zz)))
        key = tuple(d for _, d in sorted(members))
        if key not in seen:
            seen.add(key)
            groups.append(list(key))
    return groups


GROUPS = cube_groups()


def to_cube(a, m):
    return lax.ppermute(a, AXES, across(m))


def swap(a):
    return lax.ppermute(a, AXES, SWAP)


def column_of(row, rows):
    padded = -(-rows // 128) * 128
    wide = jnp.broadcast_to(row, (128, rows))
    if padded != rows:
        wide = jnp.concatenate([wide, jnp.zeros((128, padded - rows), jnp.float32)], axis=1)
    return wide.T[:rows, :1]


def row_of(column, rows):
    padded = -(-rows // 128) * 128
    wide = jnp.broadcast_to(column, (rows, 128))
    if padded != rows:
        wide = jnp.concatenate([wide, jnp.zeros((padded - rows, 128), jnp.float32)], axis=0)
    return wide.T[:1, :rows]


def any_spec():
    return pl.BlockSpec(memory_space=pl.ANY)


def vmem_spec():
    return pl.BlockSpec(memory_space=pltpu.VMEM)


def smem_spec():
    return pl.BlockSpec(memory_space=pltpu.SMEM)


def cost(matmuls, rows, cols, depth, passes=0):
    return pl.CostEstimate(
        flops=2 * matmuls * rows * cols * depth, bytes_accessed=passes * rows * cols, transcendentals=0
    )


def params():
    return pltpu.CompilerParams(vmem_limit_bytes=VMEM_LIMIT)


def dot_nt(a, b):
    return lax.dot_general(a, b, (((1,), (1,)), ((), ())), preferred_element_type=jnp.float32)


def dot_tn(a, b):
    return lax.dot_general(a, b, (((0,), (0,)), ((), ())), preferred_element_type=jnp.float32)


def scores_kernel(scale, core_ref, *refs):
    a_refs, b_refs = refs[:8], refs[8:16]
    e_ref, a_stat, b_stat, flags, a_cat, b_cat, col_m, col_s, sem = refs[16:]
    rows = a_refs[0].shape[0]
    half = 4 * rows
    core = core_ref[0]

    def copies_a(h):
        return [
            pltpu.make_async_copy(a_refs[4 * h + j], a_cat.at[h, pl.ds(j * rows, rows)], sem.at[4 * h + j])
            for j in range(4)
        ]

    def copies_b(h):
        place = h ^ core
        return [
            pltpu.make_async_copy(b_refs[4 * h + j], b_cat.at[place, pl.ds(j * rows, rows)], sem.at[8 + 4 * h + j])
            for j in range(4)
        ]

    for c in copies_b(0) + copies_a(0) + copies_b(1) + copies_a(1):
        c.start()

    def quadrant(q):
        for c in copies_a(q):
            c.wait()
        for h in range(2):

            @pl.when((h ^ core) == q)
            def _():
                for c in copies_b(h):
                    c.wait()

        b_half = b_cat[q]
        sums = []
        col = None
        for r in range(4):
            sl = slice(r * rows, (r + 1) * rows)
            e = jnp.exp2(dot_nt(a_cat[q, sl, :], b_half) * scale)
            e_ref[q, sl, :] = e
            sums.append(jnp.sum(e, axis=1, keepdims=True))
            part = jnp.sum(e, axis=0, keepdims=True)
            col = part if col is None else col + part
        row_lse = jnp.log2(row_of(jnp.concatenate(sums, axis=0), half))
        col_lse = jnp.log2(col)
        for j in range(4):
            sl = slice(j * rows, (j + 1) * rows)
            a_stat[4 * q + j : 4 * q + j + 1, :] = row_lse[:, sl]
            b_stat[pl.ds((q ^ core) * 4 + j, 1), :] = col_lse[:, sl]
        reach = jnp.max(jnp.maximum(jnp.abs(row_lse), jnp.abs(col_lse)))
        bad = jnp.logical_not(reach <= RANGE)
        flags[q] = bad.astype(jnp.int32)

        @pl.when(bad)
        def _():
            col_m[...] = jnp.full_like(col_m, -jnp.inf)
            col_s[...] = jnp.zeros_like(col_s)

            @pl.loop(0, 4)
            def _(r):
                sl = pl.ds(pl.multiple_of(r * rows, 16), rows)
                s = dot_nt(a_cat[q, sl, :], b_cat[q]) * scale
                e_ref[q, sl, :] = s
                row_m = jnp.max(s, axis=1, keepdims=True)
                row_s = jnp.sum(jnp.exp2(s - row_m), axis=1, keepdims=True)
                a_stat[pl.ds(4 * q + r, 1), :] = row_of(row_m + jnp.log2(row_s), rows)
                blk_m = jnp.max(s, axis=0, keepdims=True)
                blk_s = jnp.sum(jnp.exp2(s - blk_m), axis=0, keepdims=True)
                before = col_m[...]
                top = jnp.maximum(before, blk_m)
                col_s[...] = col_s[...] * jnp.exp2(before - top) + blk_s * jnp.exp2(blk_m - top)
                col_m[...] = top

            lse = col_m[...] + jnp.log2(col_s[...])
            for j in range(4):
                b_stat[pl.ds((q ^ core) * 4 + j, 1), :] = lse[:, j * rows : (j + 1) * rows]

    quadrant(0)
    quadrant(1)


def scores_call(core, a_blocks, b_blocks, scale):
    rows, features = a_blocks[0].shape
    half = 4 * rows
    stat = jax.ShapeDtypeStruct((8, rows), jnp.float32)
    return pl.pallas_call(
        functools.partial(scores_kernel, scale),
        in_specs=[smem_spec()] + [any_spec()] * 16,
        out_specs=[vmem_spec()] * 3 + [smem_spec()],
        out_shape=[
            pltpu.VMEM((2, half, half), jnp.float32),
            stat,
            stat,
            jax.ShapeDtypeStruct((2,), jnp.int32),
        ],
        scratch_shapes=[
            pltpu.VMEM((2, half, features), jnp.bfloat16),
            pltpu.VMEM((2, half, features), jnp.bfloat16),
            pltpu.VMEM((1, half), jnp.float32),
            pltpu.VMEM((1, half), jnp.float32),
            pltpu.SemaphoreType.DMA((16,)),
        ],
        compiler_params=params(),
        cost_estimate=cost(2, half, half, features),
        name="scores",
    )(core, *a_blocks, *b_blocks)


def merge_kernel(place_ref, got_ref, out_ref):
    me = place_ref[0]
    for m in range(8):
        parts = []
        for k in range(8):
            offset = (me ^ k) ^ m
            row = jnp.int32(0)
            for n in range(8):
                row = jnp.where(offset == n, PLACE[n], row)
            parts.append(got_ref[k, pl.ds(row, 1), :])
        top = functools.reduce(jnp.maximum, parts)
        total = functools.reduce(jnp.add, [jnp.exp2(p - top) for p in parts])
        out_ref[PLACE[m] : PLACE[m] + 1, :] = top + jnp.log2(total)


def merge_call(place, got):
    return pl.pallas_call(
        merge_kernel,
        in_specs=[pl.BlockSpec(memory_space=pltpu.SMEM), pl.BlockSpec(memory_space=pltpu.VMEM)],
        out_specs=pl.BlockSpec(memory_space=pltpu.VMEM),
        out_shape=jax.ShapeDtypeStruct(got.shape[1:], jnp.float32),
        name="merge",
    )(place, got)


def half_copies(refs, h, out, sem):
    rows = refs[0].shape[0]
    return [
        pltpu.make_async_copy(refs[4 * h + j], out.at[pl.ds(j * rows, rows)], sem.at[j]) for j in range(4)
    ]


def start_half(core, refs, shift, out, sem):
    for c in range(2):

        @pl.when(core == c)
        def _():
            for copy in half_copies(refs, c ^ shift, out, sem):
                copy.start()


def wait_half(refs, out, sem):
    for copy in half_copies(refs, 0, out, sem):
        copy.wait()


def half_scratch(block):
    return [pltpu.VMEM((4 * block.shape[0], block.shape[1]), block.dtype), pltpu.SemaphoreType.DMA((4,))]


def weights_kernel(core_ref, flags, e_ref, a_lse, b_lse, *refs):
    a_refs, (w_ref, gb_hi, a_half, a_sem) = refs[:8], refs[8:]
    rows = a_lse.shape[1]
    half = 4 * rows
    core = core_ref[0]
    start_half(core, a_refs, 1, a_half, a_sem)
    for q in range(2):
        a_row = jnp.concatenate([a_lse[4 * q + j : 4 * q + j + 1, :] for j in range(4)], axis=1)
        b_row = jnp.concatenate([b_lse[pl.ds((q ^ core) * 4 + j, 1), :] for j in range(4)], axis=1)

        @pl.when(flags[q] == 0)
        def _():
            a_col = column_of(jnp.exp2(-a_row), half)
            b_exp = jnp.exp2(-b_row)
            for r in range(4):
                sl = slice(r * rows, (r + 1) * rows)
                w_ref[q, sl, :] = (e_ref[q, sl, :] * (a_col[sl, :] + b_exp)).astype(jnp.bfloat16)

        @pl.when(flags[q] != 0)
        def _():
            a_col = column_of(a_row, half)
            for r in range(4):
                sl = slice(r * rows, (r + 1) * rows)
                s = e_ref[q, sl, :]
                w_ref[q, sl, :] = (jnp.exp2(s - a_col[sl, :]) + jnp.exp2(s - b_row)).astype(jnp.bfloat16)

    wait_half(a_refs, a_half, a_sem)
    gb_hi[...] = (0.5 * dot_tn(w_ref[1 - core], a_half[...])).astype(jnp.bfloat16)


def weights_call(core, flags, e, a_lse, b_lse, a_blocks):
    rows, features = a_blocks[0].shape
    half = 4 * rows
    return pl.pallas_call(
        weights_kernel,
        in_specs=[smem_spec()] * 2 + [vmem_spec()] * 3 + [any_spec()] * 8,
        out_specs=[vmem_spec()] * 2,
        out_shape=[
            pltpu.VMEM((2, half, half), jnp.bfloat16),
            jax.ShapeDtypeStruct((half, features), jnp.bfloat16),
        ],
        scratch_shapes=half_scratch(a_blocks[0]),
        compiler_params=params(),
        cost_estimate=cost(1, half, half, features, 12),
        name="weights",
    )(core, flags, e, a_lse, b_lse, *a_blocks)


def middle_kernel(core_ref, w_ref, *refs):
    a_refs, b_refs = refs[:8], refs[8:16]
    ga_hi, gb0, gb_lo, a_half, a_sem, b_half, b_sem = refs[16:]
    rows = gb0.shape[0]
    core = core_ref[0]
    start_half(core, a_refs, 0, a_half, a_sem)
    start_half(core, b_refs, 1, b_half, b_sem)
    wait_half(a_refs, a_half, a_sem)
    g = 0.5 * dot_tn(w_ref[core], a_half[...])
    gb0[...] = g[:rows]
    gb_lo[...] = g[rows:].astype(jnp.bfloat16)
    wait_half(b_refs, b_half, b_sem)
    ga_hi[...] = 0.5 * jnp.dot(w_ref[1], b_half[...], preferred_element_type=jnp.float32)


def middle_call(core, w, a_blocks, b_blocks):
    rows, features = a_blocks[0].shape
    half = 4 * rows
    return pl.pallas_call(
        middle_kernel,
        in_specs=[smem_spec(), vmem_spec()] + [any_spec()] * 16,
        out_specs=[vmem_spec()] * 3,
        out_shape=[
            pltpu.VMEM((half, features), jnp.float32),
            jax.ShapeDtypeStruct((rows, features), jnp.float32),
            jax.ShapeDtypeStruct((half - rows, features), jnp.bfloat16),
        ],
        scratch_shapes=half_scratch(a_blocks[0]) + half_scratch(b_blocks[0]),
        compiler_params=params(),
        cost_estimate=cost(2, half, half, features),
        name="middle",
    )(core, w, *a_blocks, *b_blocks)


def far_kernel(ga_hi, got, *outs):
    rows = outs[0].shape[0]
    for j in range(4):
        sl = slice(j * rows, (j + 1) * rows)
        outs[j][...] = (ga_hi[sl, :] + got[sl, :].astype(jnp.float32)).astype(jnp.bfloat16)


def far_call(ga_hi, got):
    half, features = ga_hi.shape
    rows = half // 4
    return pl.pallas_call(
        far_kernel,
        in_specs=[vmem_spec()] * 2,
        out_specs=[vmem_spec()] * 4,
        out_shape=[jax.ShapeDtypeStruct((rows, features), jnp.bfloat16)] * 4,
        compiler_params=params(),
        cost_estimate=cost(0, half, features, 1, 8),
        name="far",
    )(ga_hi, got)


def last_kernel(core_ref, w_ref, *refs):
    b_refs, (ga_lo, b_half, b_sem) = refs[:8], refs[8:]
    start_half(core_ref[0], b_refs, 0, b_half, b_sem)
    wait_half(b_refs, b_half, b_sem)
    ga_lo[...] = 0.5 * jnp.dot(w_ref[0], b_half[...], preferred_element_type=jnp.float32)


def last_call(core, w, b_blocks):
    rows, features = b_blocks[0].shape
    half = 4 * rows
    return pl.pallas_call(
        last_kernel,
        in_specs=[smem_spec(), vmem_spec()] + [any_spec()] * 8,
        out_specs=vmem_spec(),
        out_shape=pltpu.VMEM((half, features), jnp.float32),
        scratch_shapes=half_scratch(b_blocks[0]),
        compiler_params=params(),
        cost_estimate=cost(1, half, half, features),
        name="last",
    )(core, w, *b_blocks)


def near_kernel(ga_lo, got0, got_lo, r_xy, r_yz, r_xz, p0, p1, p2, p4):
    rows = p0.shape[0]
    wide = lambda ref: ref[...].astype(jnp.float32)
    p0[...] = ga_lo[:rows] + got0[...]
    part = lambda j: ga_lo[j * rows : (j + 1) * rows, :] + got_lo[(j - 1) * rows : j * rows, :].astype(jnp.float32)
    p1[...] = (part(1) + wide(r_xz)).astype(jnp.bfloat16)
    p2[...] = (part(2) + wide(r_xy)).astype(jnp.bfloat16)
    p4[...] = (part(3) + wide(r_yz)).astype(jnp.bfloat16)


def near_call(ga_lo, got0, got_lo, *received):
    rows, features = got0.shape
    narrow = jax.ShapeDtypeStruct((rows, features), jnp.bfloat16)
    return pl.pallas_call(
        near_kernel,
        in_specs=[vmem_spec()] * 6,
        out_specs=[vmem_spec()] * 4,
        out_shape=[pltpu.VMEM((rows, features), jnp.float32)] + [narrow] * 3,
        compiler_params=params(),
        cost_estimate=cost(0, 4 * rows, features, 1, 12),
        name="near",
    )(ga_lo, got0, got_lo, *received)


def body(images, texts):
    rows, features = images.shape
    scale = 4.0 / math.sqrt(features) * LOG2E
    core = lax.axis_index("core")
    first = core == 0
    core_arr = core.astype(jnp.int32).reshape(1)
    place = (
        (lax.axis_index("x") & 1) | ((lax.axis_index("y") & 1) << 1) | ((lax.axis_index("z") & 1) << 2)
    ).astype(jnp.int32).reshape(1)

    mine = jnp.where(first, images, texts)
    other = swap(jnp.where(first, texts, images))
    own = jnp.concatenate([mine, other], axis=0)
    blocks = {0: own, 1: to_cube(own, 1), 2: to_cube(own, 2), 4: to_cube(own, 4), 7: to_cube(own, 7)}
    blocks[5] = to_cube(blocks[1], 4)
    blocks[3] = to_cube(blocks[2], 1)
    blocks[6] = to_cube(blocks[4], 2)
    a_blocks = [blocks[m] for m in ORDER]
    b_blocks = [swap(a) for a in a_blocks]

    e, a_stat, b_stat, flags = scores_call(core_arr, a_blocks, b_blocks, scale)
    chip_stat = jnp.logaddexp2(a_stat, swap(b_stat))
    got = lax.all_to_all(
        jnp.broadcast_to(chip_stat[None], (8,) + chip_stat.shape), AXES, 0, 0, axis_index_groups=GROUPS
    )
    a_lse = merge_call(place, got)
    b_lse = swap(a_lse)

    w, gb_hi = weights_call(core_arr, flags, e, a_lse, b_lse, a_blocks)
    got_hi = swap(gb_hi)
    ga_hi, gb0, gb_lo = middle_call(core_arr, w, a_blocks, b_blocks)
    got0, got_lo = swap(gb0), swap(gb_lo)
    p = dict(zip(ORDER[4:], far_call(ga_hi, got_hi)))
    from_xy = to_cube(p[3], 1)
    from_yz = to_cube(p[6], 2)
    from_xz = to_cube(p[5], 4)
    from_xyz = to_cube(p[7], 7)
    ga_lo = last_call(core_arr, w, b_blocks)
    p0, p1, p2, p4 = near_call(ga_lo, got0, got_lo, from_xy, from_yz, from_xz)
    wide = lambda a: a.astype(jnp.float32)
    total = p0 + wide(from_xyz) + wide(to_cube(p1, 1)) + wide(to_cube(p2, 2)) + wide(to_cube(p4, 4))
    kept, sent = total[:rows], total[rows:]
    got_sum = swap(sent)
    image_sum = jnp.where(first, kept, got_sum)
    text_sum = jnp.where(first, got_sum, kept)
    return (image_sum - wide(texts), text_sum - wide(images))


def solution(mesh):
    chips = Mesh(mesh.devices.reshape(SIZES), AXES)
    spec = P(AXES, None)
    return jax.shard_map(
        body,
        mesh=chips,
        in_specs=(spec, spec),
        out_specs=(spec, spec),
        check_vma=False,
    )
```

```python
import functools
import math

import jax
import jax.numpy as jnp
from jax import lax
from jax.experimental import pallas as pl
from jax.experimental.pallas import tpu as pltpu
from jax.sharding import Mesh, PartitionSpec as P

AXES = ("y", "core", "x", "z")
SIZES = (4, 2, 4, 4)
ORDER = (0, 1, 2, 4, 3, 5, 6, 7)
PLACE = tuple(ORDER.index(m) for m in range(8))
LOG2E = 1.4426950408889634
VMEM_LIMIT = 12 * 1024 * 1024
RANGE = 60.0


def flat(y, c, x, z):
    return ((y * 2 + c) * 4 + x) * 4 + z


def coords():
    for y in range(4):
        for c in range(2):
            for x in range(4):
                for z in range(4):
                    yield y, c, x, z


def partner(v, c):
    return v ^ 1 if c == 0 else 3 - v


def across(m):
    pairs = []
    for y, c, x, z in coords():
        target = (
            partner(y, c) if m & 2 else y,
            c,
            partner(x, c) if m & 1 else x,
            partner(z, c) if m & 4 else z,
        )
        pairs.append((flat(y, c, x, z), flat(*target)))
    return pairs


SWAP = [(flat(y, c, x, z), flat(y, 1 - c, x, z)) for y, c, x, z in coords()]


def cube_groups():
    groups = []
    seen = set()
    for y, c, x, z in coords():
        members = []
        for m in range(8):
            yy = partner(y, c) if m & 2 else y
            xx = partner(x, c) if m & 1 else x
            zz = partner(z, c) if m & 4 else z
            place = (xx & 1) | ((yy & 1) << 1) | ((zz & 1) << 2)
            members.append((place, flat(yy, c, xx, zz)))
        key = tuple(d for _, d in sorted(members))
        if key not in seen:
            seen.add(key)
            groups.append(list(key))
    return groups


GROUPS = cube_groups()


def to_cube(a, m):
    return lax.ppermute(a, AXES, across(m))


def swap(a):
    return lax.ppermute(a, AXES, SWAP)


def column_of(row, rows):
    padded = -(-rows // 128) * 128
    wide = jnp.broadcast_to(row, (128, rows))
    if padded != rows:
        wide = jnp.concatenate([wide, jnp.zeros((128, padded - rows), jnp.float32)], axis=1)
    return wide.T[:rows, :1]


def row_of(column, rows):
    padded = -(-rows // 128) * 128
    wide = jnp.broadcast_to(column, (rows, 128))
    if padded != rows:
        wide = jnp.concatenate([wide, jnp.zeros((padded - rows, 128), jnp.float32)], axis=0)
    return wide.T[:1, :rows]


def any_spec():
    return pl.BlockSpec(memory_space=pl.ANY)


def vmem_spec():
    return pl.BlockSpec(memory_space=pltpu.VMEM)


def smem_spec():
    return pl.BlockSpec(memory_space=pltpu.SMEM)


def cost(matmuls, rows, cols, depth, passes=0):
    return pl.CostEstimate(
        flops=2 * matmuls * rows * cols * depth, bytes_accessed=passes * rows * cols, transcendentals=0
    )


def params():
    return pltpu.CompilerParams(vmem_limit_bytes=VMEM_LIMIT)


def dot_nt(a, b):
    return lax.dot_general(a, b, (((1,), (1,)), ((), ())), preferred_element_type=jnp.float32)


def dot_tn(a, b):
    return lax.dot_general(a, b, (((0,), (0,)), ((), ())), preferred_element_type=jnp.float32)


def scores_kernel(scale, core_ref, *refs):
    a_refs, b_refs = refs[:8], refs[8:16]
    e_ref, a_stat, b_stat, flags, a_cat, b_cat, col_m, col_s, sem = refs[16:]
    rows = a_refs[0].shape[0]
    half = 4 * rows
    core = core_ref[0]

    def copies_a(h):
        return [
            pltpu.make_async_copy(a_refs[4 * h + j], a_cat.at[h, pl.ds(j * rows, rows)], sem.at[4 * h + j])
            for j in range(4)
        ]

    def copies_b(h):
        place = h ^ core
        return [
            pltpu.make_async_copy(b_refs[4 * h + j], b_cat.at[place, pl.ds(j * rows, rows)], sem.at[8 + 4 * h + j])
            for j in range(4)
        ]

    for c in copies_b(0) + copies_a(0) + copies_b(1) + copies_a(1):
        c.start()

    def quadrant(q):
        for c in copies_a(q):
            c.wait()
        for h in range(2):

            @pl.when((h ^ core) == q)
            def _():
                for c in copies_b(h):
                    c.wait()

        b_half = b_cat[q]
        sums = []
        col = None
        for r in range(4):
            sl = slice(r * rows, (r + 1) * rows)
            e = jnp.exp2(dot_nt(a_cat[q, sl, :], b_half) * scale)
            e_ref[q, sl, :] = e
            sums.append(jnp.sum(e, axis=1, keepdims=True))
            part = jnp.sum(e, axis=0, keepdims=True)
            col = part if col is None else col + part
        row_lse = jnp.log2(row_of(jnp.concatenate(sums, axis=0), half))
        col_lse = jnp.log2(col)
        for j in range(4):
            sl = slice(j * rows, (j + 1) * rows)
            a_stat[4 * q + j : 4 * q + j + 1, :] = row_lse[:, sl]
            b_stat[pl.ds((q ^ core) * 4 + j, 1), :] = col_lse[:, sl]
        reach = jnp.max(jnp.maximum(jnp.abs(row_lse), jnp.abs(col_lse)))
        bad = jnp.logical_not(reach <= RANGE)
        flags[q] = bad.astype(jnp.int32)

        @pl.when(bad)
        def _():
            col_m[...] = jnp.full_like(col_m, -jnp.inf)
            col_s[...] = jnp.zeros_like(col_s)

            @pl.loop(0, 4)
            def _(r):
                sl = pl.ds(pl.multiple_of(r * rows, 16), rows)
                s = dot_nt(a_cat[q, sl, :], b_cat[q]) * scale
                e_ref[q, sl, :] = s
                row_m = jnp.max(s, axis=1, keepdims=True)
                row_s = jnp.sum(jnp.exp2(s - row_m), axis=1, keepdims=True)
                a_stat[pl.ds(4 * q + r, 1), :] = row_of(row_m + jnp.log2(row_s), rows)
                blk_m = jnp.max(s, axis=0, keepdims=True)
                blk_s = jnp.sum(jnp.exp2(s - blk_m), axis=0, keepdims=True)
                before = col_m[...]
                top = jnp.maximum(before, blk_m)
                col_s[...] = col_s[...] * jnp.exp2(before - top) + blk_s * jnp.exp2(blk_m - top)
                col_m[...] = top

            lse = col_m[...] + jnp.log2(col_s[...])
            for j in range(4):
                b_stat[pl.ds((q ^ core) * 4 + j, 1), :] = lse[:, j * rows : (j + 1) * rows]

    quadrant(0)
    quadrant(1)


def scores_call(core, a_blocks, b_blocks, scale):
    rows, features = a_blocks[0].shape
    half = 4 * rows
    stat = jax.ShapeDtypeStruct((8, rows), jnp.float32)
    return pl.pallas_call(
        functools.partial(scores_kernel, scale),
        in_specs=[smem_spec()] + [any_spec()] * 16,
        out_specs=[vmem_spec()] * 3 + [smem_spec()],
        out_shape=[
            pltpu.VMEM((2, half, half), jnp.float32),
            stat,
            stat,
            jax.ShapeDtypeStruct((2,), jnp.int32),
        ],
        scratch_shapes=[
            pltpu.VMEM((2, half, features), jnp.bfloat16),
            pltpu.VMEM((2, half, features), jnp.bfloat16),
            pltpu.VMEM((1, half), jnp.float32),
            pltpu.VMEM((1, half), jnp.float32),
            pltpu.SemaphoreType.DMA((16,)),
        ],
        compiler_params=params(),
        cost_estimate=cost(2, half, half, features),
        name="scores",
    )(core, *a_blocks, *b_blocks)


def merge_kernel(place_ref, got_ref, out_ref):
    me = place_ref[0]
    for m in range(8):
        parts = []
        for k in range(8):
            offset = (me ^ k) ^ m
            row = jnp.int32(0)
            for n in range(8):
                row = jnp.where(offset == n, PLACE[n], row)
            parts.append(got_ref[k, pl.ds(row, 1), :])
        top = functools.reduce(jnp.maximum, parts)
        total = functools.reduce(jnp.add, [jnp.exp2(p - top) for p in parts])
        out_ref[PLACE[m] : PLACE[m] + 1, :] = top + jnp.log2(total)


def merge_call(place, got):
    return pl.pallas_call(
        merge_kernel,
        in_specs=[pl.BlockSpec(memory_space=pltpu.SMEM), pl.BlockSpec(memory_space=pltpu.VMEM)],
        out_specs=pl.BlockSpec(memory_space=pltpu.VMEM),
        out_shape=jax.ShapeDtypeStruct(got.shape[1:], jnp.float32),
        compiler_params=pltpu.CompilerParams(vmem_limit_bytes=2 * 1024 * 1024),
        name="merge",
    )(place, got)


def half_copies(refs, h, out, sem):
    rows = refs[0].shape[0]
    return [
        pltpu.make_async_copy(refs[4 * h + j], out.at[pl.ds(j * rows, rows)], sem.at[j]) for j in range(4)
    ]


def start_half(core, refs, shift, out, sem):
    for c in range(2):

        @pl.when(core == c)
        def _():
            for copy in half_copies(refs, c ^ shift, out, sem):
                copy.start()


def wait_half(refs, out, sem):
    for copy in half_copies(refs, 0, out, sem):
        copy.wait()


def half_scratch(block):
    return [pltpu.VMEM((4 * block.shape[0], block.shape[1]), block.dtype), pltpu.SemaphoreType.DMA((4,))]


def weights_kernel(core_ref, flags, e_ref, a_lse, b_lse, *refs):
    a_refs, (w_ref, gb_hi, a_half, a_sem) = refs[:8], refs[8:]
    rows = a_lse.shape[1]
    half = 4 * rows
    core = core_ref[0]
    start_half(core, a_refs, 1, a_half, a_sem)
    for q in range(2):
        a_row = jnp.concatenate([a_lse[4 * q + j : 4 * q + j + 1, :] for j in range(4)], axis=1)
        b_row = jnp.concatenate([b_lse[pl.ds((q ^ core) * 4 + j, 1), :] for j in range(4)], axis=1)

        @pl.when(flags[q] == 0)
        def _():
            a_col = column_of(jnp.exp2(-a_row), half)
            b_exp = jnp.exp2(-b_row)
            for r in range(4):
                sl = slice(r * rows, (r + 1) * rows)
                w_ref[q, sl, :] = (e_ref[q, sl, :] * (a_col[sl, :] + b_exp)).astype(jnp.bfloat16)

        @pl.when(flags[q] != 0)
        def _():
            a_col = column_of(a_row, half)
            for r in range(4):
                sl = slice(r * rows, (r + 1) * rows)
                s = e_ref[q, sl, :]
                w_ref[q, sl, :] = (jnp.exp2(s - a_col[sl, :]) + jnp.exp2(s - b_row)).astype(jnp.bfloat16)

    wait_half(a_refs, a_half, a_sem)
    gb_hi[...] = (0.5 * dot_tn(w_ref[1 - core], a_half[...])).astype(jnp.bfloat16)


def weights_call(core, flags, e, a_lse, b_lse, a_blocks):
    rows, features = a_blocks[0].shape
    half = 4 * rows
    return pl.pallas_call(
        weights_kernel,
        in_specs=[smem_spec()] * 2 + [vmem_spec()] * 3 + [any_spec()] * 8,
        out_specs=[vmem_spec()] * 2,
        out_shape=[
            pltpu.VMEM((2, half, half), jnp.bfloat16),
            jax.ShapeDtypeStruct((half, features), jnp.bfloat16),
        ],
        scratch_shapes=half_scratch(a_blocks[0]),
        compiler_params=params(),
        cost_estimate=cost(1, half, half, features, 12),
        name="weights",
    )(core, flags, e, a_lse, b_lse, *a_blocks)


def middle_kernel(core_ref, w_ref, *refs):
    a_refs, b_refs = refs[:8], refs[8:16]
    ga_hi, gb0, gb_lo, a_half, a_sem, b_half, b_sem = refs[16:]
    rows = gb0.shape[0]
    core = core_ref[0]
    start_half(core, a_refs, 0, a_half, a_sem)
    start_half(core, b_refs, 1, b_half, b_sem)
    wait_half(a_refs, a_half, a_sem)
    g = 0.5 * dot_tn(w_ref[core], a_half[...])
    gb0[...] = g[:rows]
    gb_lo[...] = g[rows:].astype(jnp.bfloat16)
    wait_half(b_refs, b_half, b_sem)
    ga_hi[...] = 0.5 * jnp.dot(w_ref[1], b_half[...], preferred_element_type=jnp.float32)


def middle_call(core, w, a_blocks, b_blocks):
    rows, features = a_blocks[0].shape
    half = 4 * rows
    return pl.pallas_call(
        middle_kernel,
        in_specs=[smem_spec(), vmem_spec()] + [any_spec()] * 16,
        out_specs=[vmem_spec()] * 3,
        out_shape=[
            pltpu.VMEM((half, features), jnp.float32),
            jax.ShapeDtypeStruct((rows, features), jnp.float32),
            jax.ShapeDtypeStruct((half - rows, features), jnp.bfloat16),
        ],
        scratch_shapes=half_scratch(a_blocks[0]) + half_scratch(b_blocks[0]),
        compiler_params=params(),
        cost_estimate=cost(2, half, half, features),
        name="middle",
    )(core, w, *a_blocks, *b_blocks)


def far_kernel(ga_hi, got, *outs):
    rows = outs[0].shape[0]
    for j in range(4):
        sl = slice(j * rows, (j + 1) * rows)
        outs[j][...] = (ga_hi[sl, :] + got[sl, :].astype(jnp.float32)).astype(jnp.bfloat16)


def far_call(ga_hi, got):
    half, features = ga_hi.shape
    rows = half // 4
    return pl.pallas_call(
        far_kernel,
        in_specs=[vmem_spec()] * 2,
        out_specs=[vmem_spec()] * 4,
        out_shape=[jax.ShapeDtypeStruct((rows, features), jnp.bfloat16)] * 4,
        compiler_params=params(),
        cost_estimate=cost(0, half, features, 1, 8),
        name="far",
    )(ga_hi, got)


def last_kernel(core_ref, w_ref, *refs):
    b_refs, (ga_lo, b_half, b_sem) = refs[:8], refs[8:]
    start_half(core_ref[0], b_refs, 0, b_half, b_sem)
    wait_half(b_refs, b_half, b_sem)
    ga_lo[...] = 0.5 * jnp.dot(w_ref[0], b_half[...], preferred_element_type=jnp.float32)


def last_call(core, w, b_blocks):
    rows, features = b_blocks[0].shape
    half = 4 * rows
    return pl.pallas_call(
        last_kernel,
        in_specs=[smem_spec(), vmem_spec()] + [any_spec()] * 8,
        out_specs=vmem_spec(),
        out_shape=pltpu.VMEM((half, features), jnp.float32),
        scratch_shapes=half_scratch(b_blocks[0]),
        compiler_params=params(),
        cost_estimate=cost(1, half, half, features),
        name="last",
    )(core, w, *b_blocks)


def near_kernel(ga_lo, got0, got_lo, r_xy, r_yz, r_xz, p0, p1, p2, p4):
    rows = p0.shape[0]
    wide = lambda ref: ref[...].astype(jnp.float32)
    p0[...] = ga_lo[:rows] + got0[...]
    part = lambda j: ga_lo[j * rows : (j + 1) * rows, :] + got_lo[(j - 1) * rows : j * rows, :].astype(jnp.float32)
    p1[...] = (part(1) + wide(r_xz)).astype(jnp.bfloat16)
    p2[...] = (part(2) + wide(r_xy)).astype(jnp.bfloat16)
    p4[...] = (part(3) + wide(r_yz)).astype(jnp.bfloat16)


def near_call(ga_lo, got0, got_lo, *received):
    rows, features = got0.shape
    narrow = jax.ShapeDtypeStruct((rows, features), jnp.bfloat16)
    return pl.pallas_call(
        near_kernel,
        in_specs=[vmem_spec()] * 6,
        out_specs=[vmem_spec()] * 4,
        out_shape=[pltpu.VMEM((rows, features), jnp.float32)] + [narrow] * 3,
        compiler_params=params(),
        cost_estimate=cost(0, 4 * rows, features, 1, 12),
        name="near",
    )(ga_lo, got0, got_lo, *received)


def body(images, texts):
    rows, features = images.shape
    scale = 4.0 / math.sqrt(features) * LOG2E
    core = lax.axis_index("core")
    first = core == 0
    core_arr = core.astype(jnp.int32).reshape(1)
    place = (
        (lax.axis_index("x") & 1) | ((lax.axis_index("y") & 1) << 1) | ((lax.axis_index("z") & 1) << 2)
    ).astype(jnp.int32).reshape(1)

    theirs = swap(jnp.concatenate([images, texts], axis=0))
    joined = lambda lead, follow: jnp.concatenate([lead, follow], axis=0)
    own = jnp.where(first, joined(images, theirs[:rows]), joined(texts, theirs[rows:]))
    other = jnp.where(first, joined(theirs[rows:], texts), joined(theirs[:rows], images))
    near = {m: to_cube(own, m) for m in (1, 2, 4)}
    far = {7: to_cube(own, 7), 5: to_cube(near[1], 4), 3: to_cube(near[2], 1), 6: to_cube(near[4], 2)}
    blocks = {0: own, **near, **far}
    held = lax.optimization_barrier(tuple(blocks[m] for m in (1, 2, 4, 7)))
    swapped = {0: other}
    for m, a in zip((1, 2, 4, 7), held):
        swapped[m] = swap(a)
    for m in (5, 3, 6):
        swapped[m] = swap(blocks[m])
    a_blocks = [blocks[m] for m in ORDER]
    b_blocks = [swapped[m] for m in ORDER]

    e, a_stat, b_stat, flags = scores_call(core_arr, a_blocks, b_blocks, scale)
    chip_stat = jnp.logaddexp2(a_stat, swap(b_stat))
    got = lax.all_to_all(
        jnp.broadcast_to(chip_stat[None], (8,) + chip_stat.shape), AXES, 0, 0, axis_index_groups=GROUPS
    )
    a_lse = merge_call(place, got)
    b_lse = swap(a_lse)

    w, gb_hi = weights_call(core_arr, flags, e, a_lse, b_lse, a_blocks)
    got_hi = swap(gb_hi)
    ga_hi, gb0, gb_lo = middle_call(core_arr, w, a_blocks, b_blocks)
    got0, got_lo = swap(gb0), swap(gb_lo)
    p = dict(zip(ORDER[4:], far_call(ga_hi, got_hi)))
    from_xy = to_cube(p[3], 1)
    from_yz = to_cube(p[6], 2)
    from_xz = to_cube(p[5], 4)
    from_xyz = to_cube(p[7], 7)
    ga_lo = last_call(core_arr, w, b_blocks)
    p0, p1, p2, p4 = near_call(ga_lo, got0, got_lo, from_xy, from_yz, from_xz)
    wide = lambda a: a.astype(jnp.float32)
    total = p0 + wide(from_xyz) + wide(to_cube(p1, 1)) + wide(to_cube(p2, 2)) + wide(to_cube(p4, 4))
    kept, sent = total[:rows], total[rows:]
    got_sum = swap(sent)
    image_sum = jnp.where(first, kept, got_sum)
    text_sum = jnp.where(first, got_sum, kept)
    return (image_sum - wide(texts), text_sum - wide(images))


def solution(mesh):
    chips = Mesh(mesh.devices.reshape(SIZES), AXES)
    spec = P(AXES, None)
    return jax.shard_map(
        body,
        mesh=chips,
        in_specs=(spec, spec),
        out_specs=(spec, spec),
        check_vma=False,
    )
```

```python
import functools
import math

import jax
import jax.numpy as jnp
from jax import lax
from jax.experimental import pallas as pl
from jax.experimental.pallas import tpu as pltpu
from jax.sharding import Mesh, PartitionSpec as P

AXES = ("y", "core", "x", "z")
SIZES = (4, 2, 4, 4)
ORDER = (0, 1, 2, 4, 3, 5, 6, 7)
PLACE = tuple(ORDER.index(m) for m in range(8))
LOG2E = 1.4426950408889634
VMEM_LIMIT = 12 * 1024 * 1024
RANGE = 60.0


def flat(y, c, x, z):
    return ((y * 2 + c) * 4 + x) * 4 + z


def coords():
    for y in range(4):
        for c in range(2):
            for x in range(4):
                for z in range(4):
                    yield y, c, x, z


def partner(v, c):
    return v ^ 1 if c == 0 else 3 - v


def across(m):
    pairs = []
    for y, c, x, z in coords():
        target = (
            partner(y, c) if m & 2 else y,
            c,
            partner(x, c) if m & 1 else x,
            partner(z, c) if m & 4 else z,
        )
        pairs.append((flat(y, c, x, z), flat(*target)))
    return pairs


SWAP = [(flat(y, c, x, z), flat(y, 1 - c, x, z)) for y, c, x, z in coords()]


def to_cube(a, m):
    return lax.ppermute(a, AXES, across(m))


def swap(a):
    return lax.ppermute(a, AXES, SWAP)


def column_of(row, rows):
    padded = -(-rows // 128) * 128
    wide = jnp.broadcast_to(row, (128, rows))
    if padded != rows:
        wide = jnp.concatenate([wide, jnp.zeros((128, padded - rows), jnp.float32)], axis=1)
    return wide.T[:rows, :1]


def row_of(column, rows):
    padded = -(-rows // 128) * 128
    wide = jnp.broadcast_to(column, (rows, 128))
    if padded != rows:
        wide = jnp.concatenate([wide, jnp.zeros((padded - rows, 128), jnp.float32)], axis=0)
    return wide.T[:1, :rows]


def any_spec():
    return pl.BlockSpec(memory_space=pl.ANY)


def vmem_spec():
    return pl.BlockSpec(memory_space=pltpu.VMEM)


def smem_spec():
    return pl.BlockSpec(memory_space=pltpu.SMEM)


def cost(matmuls, rows, cols, depth, passes=0):
    return pl.CostEstimate(
        flops=2 * matmuls * rows * cols * depth, bytes_accessed=passes * rows * cols, transcendentals=0
    )


def params():
    return pltpu.CompilerParams(vmem_limit_bytes=VMEM_LIMIT)


def dot_nt(a, b):
    return lax.dot_general(a, b, (((1,), (1,)), ((), ())), preferred_element_type=jnp.float32)


def dot_tn(a, b):
    return lax.dot_general(a, b, (((0,), (0,)), ((), ())), preferred_element_type=jnp.float32)


def scores_kernel(scale, core_ref, *refs):
    a_refs, b_refs = refs[:8], refs[8:16]
    e_ref, a_stat, b_stat, flags, a_cat, b_cat, col_m, col_s, sem = refs[16:]
    rows = a_refs[0].shape[0]
    half = 4 * rows
    core = core_ref[0]

    def copies_a(h):
        return [
            pltpu.make_async_copy(a_refs[4 * h + j], a_cat.at[h, pl.ds(j * rows, rows)], sem.at[4 * h + j])
            for j in range(4)
        ]

    def copies_b(h):
        place = h ^ core
        return [
            pltpu.make_async_copy(b_refs[4 * h + j], b_cat.at[place, pl.ds(j * rows, rows)], sem.at[8 + 4 * h + j])
            for j in range(4)
        ]

    for c in copies_b(0) + copies_a(0) + copies_b(1) + copies_a(1):
        c.start()

    def quadrant(q):
        for c in copies_a(q):
            c.wait()
        for h in range(2):

            @pl.when((h ^ core) == q)
            def _():
                for c in copies_b(h):
                    c.wait()

        b_half = b_cat[q]
        sums = []
        col = None
        for r in range(4):
            sl = slice(r * rows, (r + 1) * rows)
            e = jnp.exp2(dot_nt(a_cat[q, sl, :], b_half) * scale)
            e_ref[q, sl, :] = e
            sums.append(jnp.sum(e, axis=1, keepdims=True))
            part = jnp.sum(e, axis=0, keepdims=True)
            col = part if col is None else col + part
        row_lse = jnp.log2(row_of(jnp.concatenate(sums, axis=0), half))
        col_lse = jnp.log2(col)
        for j in range(4):
            sl = slice(j * rows, (j + 1) * rows)
            a_stat[4 * q + j : 4 * q + j + 1, :] = row_lse[:, sl]
            b_stat[pl.ds((q ^ core) * 4 + j, 1), :] = col_lse[:, sl]
        reach = jnp.max(jnp.maximum(jnp.abs(row_lse), jnp.abs(col_lse)))
        bad = jnp.logical_not(reach <= RANGE)
        flags[q] = bad.astype(jnp.int32)

        @pl.when(bad)
        def _():
            col_m[...] = jnp.full_like(col_m, -jnp.inf)
            col_s[...] = jnp.zeros_like(col_s)

            @pl.loop(0, 4)
            def _(r):
                sl = pl.ds(pl.multiple_of(r * rows, 16), rows)
                s = dot_nt(a_cat[q, sl, :], b_cat[q]) * scale
                e_ref[q, sl, :] = s
                row_m = jnp.max(s, axis=1, keepdims=True)
                row_s = jnp.sum(jnp.exp2(s - row_m), axis=1, keepdims=True)
                a_stat[pl.ds(4 * q + r, 1), :] = row_of(row_m + jnp.log2(row_s), rows)
                blk_m = jnp.max(s, axis=0, keepdims=True)
                blk_s = jnp.sum(jnp.exp2(s - blk_m), axis=0, keepdims=True)
                before = col_m[...]
                top = jnp.maximum(before, blk_m)
                col_s[...] = col_s[...] * jnp.exp2(before - top) + blk_s * jnp.exp2(blk_m - top)
                col_m[...] = top

            lse = col_m[...] + jnp.log2(col_s[...])
            for j in range(4):
                b_stat[pl.ds((q ^ core) * 4 + j, 1), :] = lse[:, j * rows : (j + 1) * rows]

    quadrant(0)
    quadrant(1)


def scores_call(core, a_blocks, b_blocks, scale):
    rows, features = a_blocks[0].shape
    half = 4 * rows
    stat = jax.ShapeDtypeStruct((8, rows), jnp.float32)
    return pl.pallas_call(
        functools.partial(scores_kernel, scale),
        in_specs=[smem_spec()] + [any_spec()] * 16,
        out_specs=[vmem_spec()] * 3 + [smem_spec()],
        out_shape=[
            pltpu.VMEM((2, half, half), jnp.float32),
            stat,
            stat,
            jax.ShapeDtypeStruct((2,), jnp.int32),
        ],
        scratch_shapes=[
            pltpu.VMEM((2, half, features), jnp.bfloat16),
            pltpu.VMEM((2, half, features), jnp.bfloat16),
            pltpu.VMEM((1, half), jnp.float32),
            pltpu.VMEM((1, half), jnp.float32),
            pltpu.SemaphoreType.DMA((16,)),
        ],
        compiler_params=params(),
        cost_estimate=cost(2, half, half, features),
        name="scores",
    )(core, *a_blocks, *b_blocks)


def merge_kernel(m, mine_ref, got_ref, out_ref):
    for k in range(8):
        j = PLACE[ORDER[k] ^ m]
        mine, got = mine_ref[k : k + 1, :], got_ref[j : j + 1, :]
        top = jnp.maximum(mine, got)
        out_ref[k : k + 1, :] = top + jnp.log2(jnp.exp2(mine - top) + jnp.exp2(got - top))


def merge_call(mine, got, m):
    return pl.pallas_call(
        functools.partial(merge_kernel, m),
        in_specs=[vmem_spec()] * 2,
        out_specs=vmem_spec(),
        out_shape=jax.ShapeDtypeStruct(mine.shape, jnp.float32),
        compiler_params=pltpu.CompilerParams(vmem_limit_bytes=2 * 1024 * 1024),
        name="merge",
    )(mine, got)


def half_copies(refs, h, out, sem):
    rows = refs[0].shape[0]
    return [
        pltpu.make_async_copy(refs[4 * h + j], out.at[pl.ds(j * rows, rows)], sem.at[j]) for j in range(4)
    ]


def start_half(core, refs, shift, out, sem):
    for c in range(2):

        @pl.when(core == c)
        def _():
            for copy in half_copies(refs, c ^ shift, out, sem):
                copy.start()


def wait_half(refs, out, sem):
    for copy in half_copies(refs, 0, out, sem):
        copy.wait()


def half_scratch(block):
    return [pltpu.VMEM((4 * block.shape[0], block.shape[1]), block.dtype), pltpu.SemaphoreType.DMA((4,))]


def weights_kernel(core_ref, flags, e_ref, a_lse, b_lse, *refs):
    a_refs, (w_ref, gb_hi, a_half, a_sem) = refs[:8], refs[8:]
    rows = a_lse.shape[1]
    half = 4 * rows
    core = core_ref[0]
    start_half(core, a_refs, 1, a_half, a_sem)
    for q in range(2):
        a_row = jnp.concatenate([a_lse[4 * q + j : 4 * q + j + 1, :] for j in range(4)], axis=1)
        b_row = jnp.concatenate([b_lse[pl.ds((q ^ core) * 4 + j, 1), :] for j in range(4)], axis=1)

        @pl.when(flags[q] == 0)
        def _():
            a_col = column_of(jnp.exp2(-a_row), half)
            b_exp = jnp.exp2(-b_row)
            for r in range(4):
                sl = slice(r * rows, (r + 1) * rows)
                w_ref[q, sl, :] = (e_ref[q, sl, :] * (a_col[sl, :] + b_exp)).astype(jnp.bfloat16)

        @pl.when(flags[q] != 0)
        def _():
            a_col = column_of(a_row, half)
            for r in range(4):
                sl = slice(r * rows, (r + 1) * rows)
                s = e_ref[q, sl, :]
                w_ref[q, sl, :] = (jnp.exp2(s - a_col[sl, :]) + jnp.exp2(s - b_row)).astype(jnp.bfloat16)

    wait_half(a_refs, a_half, a_sem)
    gb_hi[...] = (0.5 * dot_tn(w_ref[1 - core], a_half[...])).astype(jnp.bfloat16)


def weights_call(core, flags, e, a_lse, b_lse, a_blocks):
    rows, features = a_blocks[0].shape
    half = 4 * rows
    return pl.pallas_call(
        weights_kernel,
        in_specs=[smem_spec()] * 2 + [vmem_spec()] * 3 + [any_spec()] * 8,
        out_specs=[vmem_spec()] * 2,
        out_shape=[
            pltpu.VMEM((2, half, half), jnp.bfloat16),
            jax.ShapeDtypeStruct((half, features), jnp.bfloat16),
        ],
        scratch_shapes=half_scratch(a_blocks[0]),
        compiler_params=params(),
        cost_estimate=cost(1, half, half, features, 12),
        name="weights",
    )(core, flags, e, a_lse, b_lse, *a_blocks)


def middle_kernel(core_ref, w_ref, *refs):
    a_refs, b_refs = refs[:8], refs[8:16]
    ga_hi, gb0, gb_lo, a_half, a_sem, b_half, b_sem = refs[16:]
    rows = gb0.shape[0]
    core = core_ref[0]
    start_half(core, a_refs, 0, a_half, a_sem)
    start_half(core, b_refs, 1, b_half, b_sem)
    wait_half(a_refs, a_half, a_sem)
    g = 0.5 * dot_tn(w_ref[core], a_half[...])
    gb0[...] = g[:rows]
    gb_lo[...] = g[rows:].astype(jnp.bfloat16)
    wait_half(b_refs, b_half, b_sem)
    ga_hi[...] = 0.5 * jnp.dot(w_ref[1], b_half[...], preferred_element_type=jnp.float32)


def middle_call(core, w, a_blocks, b_blocks):
    rows, features = a_blocks[0].shape
    half = 4 * rows
    return pl.pallas_call(
        middle_kernel,
        in_specs=[smem_spec(), vmem_spec()] + [any_spec()] * 16,
        out_specs=[vmem_spec()] * 3,
        out_shape=[
            pltpu.VMEM((half, features), jnp.float32),
            jax.ShapeDtypeStruct((rows, features), jnp.float32),
            jax.ShapeDtypeStruct((half - rows, features), jnp.bfloat16),
        ],
        scratch_shapes=half_scratch(a_blocks[0]) + half_scratch(b_blocks[0]),
        compiler_params=params(),
        cost_estimate=cost(2, half, half, features),
        name="middle",
    )(core, w, *a_blocks, *b_blocks)


def far_kernel(ga_hi, got, *outs):
    rows = outs[0].shape[0]
    for j in range(4):
        sl = slice(j * rows, (j + 1) * rows)
        outs[j][...] = (ga_hi[sl, :] + got[sl, :].astype(jnp.float32)).astype(jnp.bfloat16)


def far_call(ga_hi, got):
    half, features = ga_hi.shape
    rows = half // 4
    return pl.pallas_call(
        far_kernel,
        in_specs=[vmem_spec()] * 2,
        out_specs=[vmem_spec()] * 4,
        out_shape=[jax.ShapeDtypeStruct((rows, features), jnp.bfloat16)] * 4,
        compiler_params=params(),
        cost_estimate=cost(0, half, features, 1, 8),
        name="far",
    )(ga_hi, got)


def last_kernel(core_ref, w_ref, *refs):
    b_refs, (ga_lo, b_half, b_sem) = refs[:8], refs[8:]
    start_half(core_ref[0], b_refs, 0, b_half, b_sem)
    wait_half(b_refs, b_half, b_sem)
    ga_lo[...] = 0.5 * jnp.dot(w_ref[0], b_half[...], preferred_element_type=jnp.float32)


def last_call(core, w, b_blocks):
    rows, features = b_blocks[0].shape
    half = 4 * rows
    return pl.pallas_call(
        last_kernel,
        in_specs=[smem_spec(), vmem_spec()] + [any_spec()] * 8,
        out_specs=vmem_spec(),
        out_shape=pltpu.VMEM((half, features), jnp.float32),
        scratch_shapes=half_scratch(b_blocks[0]),
        compiler_params=params(),
        cost_estimate=cost(1, half, half, features),
        name="last",
    )(core, w, *b_blocks)


def near_kernel(ga_lo, got0, got_lo, r_xy, r_yz, r_xz, p0, p1, p2, p4):
    rows = p0.shape[0]
    wide = lambda ref: ref[...].astype(jnp.float32)
    p0[...] = ga_lo[:rows] + got0[...]
    part = lambda j: ga_lo[j * rows : (j + 1) * rows, :] + got_lo[(j - 1) * rows : j * rows, :].astype(jnp.float32)
    p1[...] = (part(1) + wide(r_xz)).astype(jnp.bfloat16)
    p2[...] = (part(2) + wide(r_xy)).astype(jnp.bfloat16)
    p4[...] = (part(3) + wide(r_yz)).astype(jnp.bfloat16)


def near_call(ga_lo, got0, got_lo, *received):
    rows, features = got0.shape
    narrow = jax.ShapeDtypeStruct((rows, features), jnp.bfloat16)
    return pl.pallas_call(
        near_kernel,
        in_specs=[vmem_spec()] * 6,
        out_specs=[vmem_spec()] * 4,
        out_shape=[pltpu.VMEM((rows, features), jnp.float32)] + [narrow] * 3,
        compiler_params=params(),
        cost_estimate=cost(0, 4 * rows, features, 1, 12),
        name="near",
    )(ga_lo, got0, got_lo, *received)


def body(images, texts):
    rows, features = images.shape
    scale = 4.0 / math.sqrt(features) * LOG2E
    core = lax.axis_index("core")
    first = core == 0
    core_arr = core.astype(jnp.int32).reshape(1)
    theirs = swap(jnp.concatenate([images, texts], axis=0))
    joined = lambda lead, follow: jnp.concatenate([lead, follow], axis=0)
    own = jnp.where(first, joined(images, theirs[:rows]), joined(texts, theirs[rows:]))
    other = jnp.where(first, joined(theirs[rows:], texts), joined(theirs[:rows], images))
    near = {m: to_cube(own, m) for m in (1, 2, 4)}
    far = {7: to_cube(near[1], 6), 5: to_cube(near[1], 4), 3: to_cube(near[2], 1), 6: to_cube(near[4], 2)}
    blocks = {0: own, **near, **far}
    held = lax.optimization_barrier(tuple(blocks[m] for m in (1, 2, 4, 5)))
    swapped = {0: other}
    for m, a in zip((1, 2, 4, 5), held):
        swapped[m] = swap(a)
    for m in (3, 6, 7):
        swapped[m] = swap(blocks[m])
    a_blocks = [blocks[m] for m in ORDER]
    b_blocks = [swapped[m] for m in ORDER]

    e, a_stat, b_stat, flags = scores_call(core_arr, a_blocks, b_blocks, scale)
    a_lse = merge_call(a_stat, swap(b_stat), 0)
    for m in (1, 2, 4):
        a_lse = merge_call(a_lse, to_cube(a_lse, m), m)
    b_lse = swap(a_lse)

    w, gb_hi = weights_call(core_arr, flags, e, a_lse, b_lse, a_blocks)
    got_hi = swap(gb_hi)
    ga_hi, gb0, gb_lo = middle_call(core_arr, w, a_blocks, b_blocks)
    got0, got_lo = swap(gb0), swap(gb_lo)
    p = dict(zip(ORDER[4:], far_call(ga_hi, got_hi)))
    from_xy = to_cube(p[3], 1)
    from_yz = to_cube(p[6], 2)
    from_xz = to_cube(p[5], 4)
    from_xyz = to_cube(p[7], 7)
    ga_lo = last_call(core_arr, w, b_blocks)
    p0, p1, p2, p4 = near_call(ga_lo, got0, got_lo, from_xy, from_yz, from_xz)
    wide = lambda a: a.astype(jnp.float32)
    total = p0 + wide(from_xyz) + wide(to_cube(p1, 1)) + wide(to_cube(p2, 2)) + wide(to_cube(p4, 4))
    kept, sent = total[:rows], total[rows:]
    got_sum = swap(sent)
    image_sum = jnp.where(first, kept, got_sum)
    text_sum = jnp.where(first, got_sum, kept)
    return (image_sum - wide(texts), text_sum - wide(images))


def solution(mesh):
    chips = Mesh(mesh.devices.reshape(SIZES), AXES)
    spec = P(AXES, None)
    return jax.shard_map(
        body,
        mesh=chips,
        in_specs=(spec, spec),
        out_specs=(spec, spec),
        check_vma=False,
    )
```

```python
import functools
import math

import jax
import jax.numpy as jnp
from jax import lax
from jax.experimental import pallas as pl
from jax.experimental.pallas import tpu as pltpu
from jax.sharding import Mesh, PartitionSpec as P

AXES = ("y", "core", "x", "z")
SIZES = (4, 2, 4, 4)
ORDER = (0, 1, 2, 4, 3, 5, 6, 7)
PLACE = tuple(ORDER.index(m) for m in range(8))
LOG2E = 1.4426950408889634
VMEM_LIMIT = 12 * 1024 * 1024
RANGE = 60.0


def flat(y, c, x, z):
    return ((y * 2 + c) * 4 + x) * 4 + z


def coords():
    for y in range(4):
        for c in range(2):
            for x in range(4):
                for z in range(4):
                    yield y, c, x, z


def partner(v, c):
    return v ^ 1 if c == 0 else 3 - v


def across(m):
    pairs = []
    for y, c, x, z in coords():
        target = (
            partner(y, c) if m & 2 else y,
            c,
            partner(x, c) if m & 1 else x,
            partner(z, c) if m & 4 else z,
        )
        pairs.append((flat(y, c, x, z), flat(*target)))
    return pairs


SWAP = [(flat(y, c, x, z), flat(y, 1 - c, x, z)) for y, c, x, z in coords()]


def to_cube(a, m):
    return lax.ppermute(a, AXES, across(m))


def swap(a):
    return lax.ppermute(a, AXES, SWAP)


def column_of(row, rows):
    padded = -(-rows // 128) * 128
    wide = jnp.broadcast_to(row, (128, rows))
    if padded != rows:
        wide = jnp.concatenate([wide, jnp.zeros((128, padded - rows), jnp.float32)], axis=1)
    return wide.T[:rows, :1]


def row_of(column, rows):
    padded = -(-rows // 128) * 128
    wide = jnp.broadcast_to(column, (rows, 128))
    if padded != rows:
        wide = jnp.concatenate([wide, jnp.zeros((padded - rows, 128), jnp.float32)], axis=0)
    return wide.T[:1, :rows]


def vmem_spec():
    return pl.BlockSpec(memory_space=pltpu.VMEM)


def smem_spec():
    return pl.BlockSpec(memory_space=pltpu.SMEM)


def cost(matmuls, rows, cols, depth, passes=0):
    return pl.CostEstimate(
        flops=2 * matmuls * rows * cols * depth, bytes_accessed=passes * rows * cols, transcendentals=0
    )


def params():
    return pltpu.CompilerParams(vmem_limit_bytes=VMEM_LIMIT)


def dot_nt(a, b):
    return lax.dot_general(a, b, (((1,), (1,)), ((), ())), preferred_element_type=jnp.float32)


def dot_tn(a, b):
    return lax.dot_general(a, b, (((0,), (0,)), ((), ())), preferred_element_type=jnp.float32)


def own_kernel(core_ref, images, texts, got_images, got_texts, own, other):
    rows = images.shape[0]
    core = core_ref[0]

    @pl.when(core == 0)
    def _():
        own[:rows] = images[...]
        own[rows:] = got_images[...]
        other[:rows] = got_texts[...]
        other[rows:] = texts[...]

    @pl.when(core != 0)
    def _():
        own[:rows] = texts[...]
        own[rows:] = got_texts[...]
        other[:rows] = got_images[...]
        other[rows:] = images[...]


def own_call(core, *parts):
    rows, features = parts[0].shape
    block = jax.ShapeDtypeStruct((2 * rows, features), parts[0].dtype)
    return pl.pallas_call(
        own_kernel,
        in_specs=[smem_spec()] + [vmem_spec()] * 4,
        out_specs=[vmem_spec()] * 2,
        out_shape=[block, block],
        compiler_params=params(),
        cost_estimate=cost(0, rows, features, 1, 16),
        name="own",
    )(core, *parts)


def join_kernel(b0, b1, b2, out):
    rows = b0.shape[0]
    for j, b in enumerate((b0, b1, b2)):
        out[j * rows : (j + 1) * rows, :] = b[...]


def join_call(*parts):
    rows, features = parts[0].shape
    return pl.pallas_call(
        join_kernel,
        in_specs=[vmem_spec()] * 3,
        out_specs=vmem_spec(),
        out_shape=jax.ShapeDtypeStruct((3 * rows, features), parts[0].dtype),
        compiler_params=params(),
        cost_estimate=cost(0, 3 * rows, features, 1, 4),
        name="join",
    )(*parts)


def views(refs):
    own, near = refs[:2]
    rows = own.shape[0]
    return [own] + [near.at[pl.ds(j * rows, rows)] for j in range(3)] + list(refs[2:])


def take_half(core, blocks, shift, out):
    rows = blocks[0].shape[0]
    for c in range(2):

        @pl.when(core == c)
        def _():
            for j in range(4):
                out[j * rows : (j + 1) * rows, :] = blocks[4 * (c ^ shift) + j][...]


def scores_kernel(scale, core_ref, *refs):
    a_refs, b_refs = refs[:8], views(refs[8:14])
    e_ref, a_stat, b_stat, flags, a_cat, b_cat, col_m, col_s = refs[14:]
    rows = a_refs[0].shape[0]
    half = 4 * rows
    core = core_ref[0]
    for q in range(2):
        take_half(core, b_refs, q, b_cat.at[q])

    def quadrant(q):
        b_half = b_cat[q]
        sums = []
        col = None
        for r in range(4):
            sl = slice(r * rows, (r + 1) * rows)
            e = jnp.exp2(dot_nt(a_refs[4 * q + r][...], b_half) * scale)
            e_ref[q, sl, :] = e
            sums.append(jnp.sum(e, axis=1, keepdims=True))
            part = jnp.sum(e, axis=0, keepdims=True)
            col = part if col is None else col + part
        row_lse = jnp.log2(row_of(jnp.concatenate(sums, axis=0), half))
        col_lse = jnp.log2(col)
        for j in range(4):
            sl = slice(j * rows, (j + 1) * rows)
            a_stat[4 * q + j : 4 * q + j + 1, :] = row_lse[:, sl]
            b_stat[pl.ds((q ^ core) * 4 + j, 1), :] = col_lse[:, sl]
        reach = jnp.max(jnp.maximum(jnp.abs(row_lse), jnp.abs(col_lse)))
        bad = jnp.logical_not(reach <= RANGE)
        flags[q] = bad.astype(jnp.int32)

        @pl.when(bad)
        def _():
            for r in range(4):
                a_cat[r * rows : (r + 1) * rows, :] = a_refs[4 * q + r][...]
            col_m[...] = jnp.full_like(col_m, -jnp.inf)
            col_s[...] = jnp.zeros_like(col_s)

            @pl.loop(0, 4)
            def _(r):
                sl = pl.ds(pl.multiple_of(r * rows, 16), rows)
                s = dot_nt(a_cat[sl, :], b_cat[q]) * scale
                e_ref[q, sl, :] = s
                row_m = jnp.max(s, axis=1, keepdims=True)
                row_s = jnp.sum(jnp.exp2(s - row_m), axis=1, keepdims=True)
                a_stat[pl.ds(4 * q + r, 1), :] = row_of(row_m + jnp.log2(row_s), rows)
                blk_m = jnp.max(s, axis=0, keepdims=True)
                blk_s = jnp.sum(jnp.exp2(s - blk_m), axis=0, keepdims=True)
                before = col_m[...]
                top = jnp.maximum(before, blk_m)
                col_s[...] = col_s[...] * jnp.exp2(before - top) + blk_s * jnp.exp2(blk_m - top)
                col_m[...] = top

            lse = col_m[...] + jnp.log2(col_s[...])
            for j in range(4):
                b_stat[pl.ds((q ^ core) * 4 + j, 1), :] = lse[:, j * rows : (j + 1) * rows]

    quadrant(0)
    quadrant(1)


def scores_call(core, a_blocks, b_blocks, scale):
    rows, features = a_blocks[0].shape
    half = 4 * rows
    stat = jax.ShapeDtypeStruct((8, rows), jnp.float32)
    return pl.pallas_call(
        functools.partial(scores_kernel, scale),
        in_specs=[smem_spec()] + [vmem_spec()] * 14,
        out_specs=[vmem_spec()] * 3 + [smem_spec()],
        out_shape=[
            pltpu.VMEM((2, half, half), jnp.float32),
            stat,
            stat,
            jax.ShapeDtypeStruct((2,), jnp.int32),
        ],
        scratch_shapes=[
            pltpu.VMEM((half, features), jnp.bfloat16),
            pltpu.VMEM((2, half, features), jnp.bfloat16),
            pltpu.VMEM((1, half), jnp.float32),
            pltpu.VMEM((1, half), jnp.float32),
        ],
        compiler_params=params(),
        cost_estimate=cost(2, half, half, features),
        name="scores",
    )(core, *a_blocks, *b_blocks)


def merge_kernel(m, mine_ref, got_ref, out_ref):
    for k in range(8):
        j = PLACE[ORDER[k] ^ m]
        mine, got = mine_ref[k : k + 1, :], got_ref[j : j + 1, :]
        top = jnp.maximum(mine, got)
        out_ref[k : k + 1, :] = top + jnp.log2(jnp.exp2(mine - top) + jnp.exp2(got - top))


def merge_call(mine, got, m):
    return pl.pallas_call(
        functools.partial(merge_kernel, m),
        in_specs=[vmem_spec()] * 2,
        out_specs=vmem_spec(),
        out_shape=jax.ShapeDtypeStruct(mine.shape, jnp.float32),
        compiler_params=pltpu.CompilerParams(vmem_limit_bytes=2 * 1024 * 1024),
        name="merge",
    )(mine, got)


def weights_kernel(core_ref, flags, e_ref, a_lse, b_lse, *refs):
    a_refs, (w_ref, gb_hi, a_half) = refs[:8], refs[8:]
    rows = a_lse.shape[1]
    half = 4 * rows
    core = core_ref[0]
    take_half(core, a_refs, 1, a_half)
    for q in range(2):
        a_row = jnp.concatenate([a_lse[4 * q + j : 4 * q + j + 1, :] for j in range(4)], axis=1)
        b_row = jnp.concatenate([b_lse[pl.ds((q ^ core) * 4 + j, 1), :] for j in range(4)], axis=1)

        @pl.when(flags[q] == 0)
        def _():
            a_col = column_of(jnp.exp2(-a_row), half)
            b_exp = jnp.exp2(-b_row)
            for r in range(4):
                sl = slice(r * rows, (r + 1) * rows)
                w_ref[q, sl, :] = (e_ref[q, sl, :] * (a_col[sl, :] + b_exp)).astype(jnp.bfloat16)

        @pl.when(flags[q] != 0)
        def _():
            a_col = column_of(a_row, half)
            for r in range(4):
                sl = slice(r * rows, (r + 1) * rows)
                s = e_ref[q, sl, :]
                w_ref[q, sl, :] = (jnp.exp2(s - a_col[sl, :]) + jnp.exp2(s - b_row)).astype(jnp.bfloat16)

    gb_hi[...] = (0.5 * dot_tn(w_ref[1 - core], a_half[...])).astype(jnp.bfloat16)


def weights_call(core, flags, e, a_lse, b_lse, a_blocks):
    rows, features = a_blocks[0].shape
    half = 4 * rows
    return pl.pallas_call(
        weights_kernel,
        in_specs=[smem_spec()] * 2 + [vmem_spec()] * 11,
        out_specs=[vmem_spec()] * 2,
        out_shape=[
            pltpu.VMEM((2, half, half), jnp.bfloat16),
            jax.ShapeDtypeStruct((half, features), jnp.bfloat16),
        ],
        scratch_shapes=[pltpu.VMEM((half, features), jnp.bfloat16)],
        compiler_params=params(),
        cost_estimate=cost(1, half, half, features, 12),
        name="weights",
    )(core, flags, e, a_lse, b_lse, *a_blocks)


def middle_kernel(core_ref, w_ref, *refs):
    a_refs, b_refs = refs[:8], views(refs[8:14])
    ga_hi, gb0, gb_lo, a_half, b_half = refs[14:]
    rows = gb0.shape[0]
    core = core_ref[0]
    take_half(core, a_refs, 0, a_half)
    take_half(core, b_refs, 1, b_half)
    g = 0.5 * dot_tn(w_ref[core], a_half[...])
    gb0[...] = g[:rows]
    gb_lo[...] = g[rows:].astype(jnp.bfloat16)
    ga_hi[...] = 0.5 * jnp.dot(w_ref[1], b_half[...], preferred_element_type=jnp.float32)


def middle_call(core, w, a_blocks, b_blocks):
    rows, features = a_blocks[0].shape
    half = 4 * rows
    return pl.pallas_call(
        middle_kernel,
        in_specs=[smem_spec()] + [vmem_spec()] * 15,
        out_specs=[vmem_spec()] * 3,
        out_shape=[
            pltpu.VMEM((half, features), jnp.float32),
            jax.ShapeDtypeStruct((rows, features), jnp.float32),
            jax.ShapeDtypeStruct((half - rows, features), jnp.bfloat16),
        ],
        scratch_shapes=[pltpu.VMEM((half, features), jnp.bfloat16)] * 2,
        compiler_params=params(),
        cost_estimate=cost(2, half, half, features),
        name="middle",
    )(core, w, *a_blocks, *b_blocks)


def far_kernel(ga_hi, got, *outs):
    rows = outs[0].shape[0]
    for j in range(4):
        sl = slice(j * rows, (j + 1) * rows)
        outs[j][...] = (ga_hi[sl, :] + got[sl, :].astype(jnp.float32)).astype(jnp.bfloat16)


def far_call(ga_hi, got):
    half, features = ga_hi.shape
    rows = half // 4
    return pl.pallas_call(
        far_kernel,
        in_specs=[vmem_spec()] * 2,
        out_specs=[vmem_spec()] * 4,
        out_shape=[jax.ShapeDtypeStruct((rows, features), jnp.bfloat16)] * 4,
        compiler_params=params(),
        cost_estimate=cost(0, half, features, 1, 8),
        name="far",
    )(ga_hi, got)


def last_kernel(core_ref, w_ref, *refs):
    b_refs, (ga_lo, b_half) = views(refs[:6]), refs[6:]
    take_half(core_ref[0], b_refs, 0, b_half)
    ga_lo[...] = 0.5 * jnp.dot(w_ref[0], b_half[...], preferred_element_type=jnp.float32)


def last_call(core, w, b_blocks):
    rows, features = b_blocks[0].shape
    half = 4 * rows
    return pl.pallas_call(
        last_kernel,
        in_specs=[smem_spec()] + [vmem_spec()] * 7,
        out_specs=vmem_spec(),
        out_shape=pltpu.VMEM((half, features), jnp.float32),
        scratch_shapes=[pltpu.VMEM((half, features), jnp.bfloat16)],
        compiler_params=params(),
        cost_estimate=cost(1, half, half, features),
        name="last",
    )(core, w, *b_blocks)


def near_kernel(ga_lo, got0, got_lo, r_xy, r_yz, r_xz, p0, p1, p2, p4):
    rows = p0.shape[0]
    wide = lambda ref: ref[...].astype(jnp.float32)
    p0[...] = ga_lo[:rows] + got0[...]
    part = lambda j: ga_lo[j * rows : (j + 1) * rows, :] + got_lo[(j - 1) * rows : j * rows, :].astype(jnp.float32)
    p1[...] = (part(1) + wide(r_xz)).astype(jnp.bfloat16)
    p2[...] = (part(2) + wide(r_xy)).astype(jnp.bfloat16)
    p4[...] = (part(3) + wide(r_yz)).astype(jnp.bfloat16)


def near_call(ga_lo, got0, got_lo, *received):
    rows, features = got0.shape
    narrow = jax.ShapeDtypeStruct((rows, features), jnp.bfloat16)
    return pl.pallas_call(
        near_kernel,
        in_specs=[vmem_spec()] * 6,
        out_specs=[vmem_spec()] * 4,
        out_shape=[pltpu.VMEM((rows, features), jnp.float32)] + [narrow] * 3,
        compiler_params=params(),
        cost_estimate=cost(0, 4 * rows, features, 1, 12),
        name="near",
    )(ga_lo, got0, got_lo, *received)


def body(images, texts):
    rows, features = images.shape
    scale = 4.0 / math.sqrt(features) * LOG2E
    core = lax.axis_index("core")
    first = core == 0
    core_arr = core.astype(jnp.int32).reshape(1)
    own, other = own_call(core_arr, images, texts, swap(images), swap(texts))
    near = {m: to_cube(own, m) for m in (4, 2, 1)}
    far = {7: to_cube(near[1], 6), 5: to_cube(near[1], 4), 3: to_cube(near[2], 1), 6: to_cube(near[4], 2)}
    blocks = {0: own, **near, **far}
    in_vmem = lambda a: pltpu.with_memory_space_constraint(a, pltpu.VMEM)
    a_blocks = [in_vmem(blocks[m]) for m in ORDER]
    b_blocks = [other, swap(join_call(near[1], near[2], near[4]))] + [swap(far[m]) for m in ORDER[4:]]
    b_blocks = [in_vmem(b) for b in b_blocks]

    e, a_stat, b_stat, flags = scores_call(core_arr, a_blocks, b_blocks, scale)
    a_lse = merge_call(a_stat, swap(b_stat), 0)
    for m in (1, 2, 4):
        a_lse = merge_call(a_lse, to_cube(a_lse, m), m)
    b_lse = swap(a_lse)

    w, gb_hi = weights_call(core_arr, flags, e, a_lse, b_lse, a_blocks)
    got_hi = swap(gb_hi)
    ga_hi, gb0, gb_lo = middle_call(core_arr, w, a_blocks, b_blocks)
    got0, got_lo = swap(gb0), swap(gb_lo)
    p = dict(zip(ORDER[4:], far_call(ga_hi, got_hi)))
    from_xy = to_cube(p[3], 1)
    from_yz = to_cube(p[6], 2)
    from_xz = to_cube(p[5], 4)
    from_xyz = to_cube(p[7], 7)
    ga_lo = last_call(core_arr, w, b_blocks)
    p0, p1, p2, p4 = near_call(ga_lo, got0, got_lo, from_xy, from_yz, from_xz)
    wide = lambda a: a.astype(jnp.float32)
    total = p0 + wide(from_xyz) + wide(to_cube(p1, 1)) + wide(to_cube(p2, 2)) + wide(to_cube(p4, 4))
    kept, sent = total[:rows], total[rows:]
    got_sum = swap(sent)
    image_sum = jnp.where(first, kept, got_sum)
    text_sum = jnp.where(first, got_sum, kept)
    return (image_sum - wide(texts), text_sum - wide(images))


def solution(mesh):
    chips = Mesh(mesh.devices.reshape(SIZES), AXES)
    spec = P(AXES, None)
    return jax.shard_map(
        body,
        mesh=chips,
        in_specs=(spec, spec),
        out_specs=(spec, spec),
        check_vma=False,
    )
```

```python
import functools
import math

import jax
import jax.numpy as jnp
from jax import lax
from jax.experimental import pallas as pl
from jax.experimental.pallas import tpu as pltpu
from jax.sharding import Mesh, PartitionSpec as P

AXES = ("y", "core", "x", "z")
SIZES = (4, 2, 4, 4)
ORDER = (0, 1, 2, 4, 3, 5, 6, 7)
PLACE = tuple(ORDER.index(m) for m in range(8))
LOG2E = 1.4426950408889634
VMEM_LIMIT = 12 * 1024 * 1024
RANGE = 60.0


def flat(y, c, x, z):
    return ((y * 2 + c) * 4 + x) * 4 + z


def coords():
    for y in range(4):
        for c in range(2):
            for x in range(4):
                for z in range(4):
                    yield y, c, x, z


def partner(v, wrapped):
    return 3 - v if wrapped else v ^ 1


def across(m):
    pairs = []
    for y, c, x, z in coords():
        target = (
            partner(y, c == 0) if m & 2 else y,
            c,
            partner(x, c == 1) if m & 1 else x,
            partner(z, c == 1) if m & 4 else z,
        )
        pairs.append((flat(y, c, x, z), flat(*target)))
    return pairs


SWAP = [(flat(y, c, x, z), flat(y, 1 - c, x, z)) for y, c, x, z in coords()]


def to_cube(a, m):
    return lax.ppermute(a, AXES, across(m))


def swap(a):
    return lax.ppermute(a, AXES, SWAP)


def column_of(row, rows):
    padded = -(-rows // 128) * 128
    wide = jnp.broadcast_to(row, (128, rows))
    if padded != rows:
        wide = jnp.concatenate([wide, jnp.zeros((128, padded - rows), jnp.float32)], axis=1)
    return wide.T[:rows, :1]


def row_of(column, rows):
    padded = -(-rows // 128) * 128
    wide = jnp.broadcast_to(column, (rows, 128))
    if padded != rows:
        wide = jnp.concatenate([wide, jnp.zeros((padded - rows, 128), jnp.float32)], axis=0)
    return wide.T[:1, :rows]


def vmem_spec():
    return pl.BlockSpec(memory_space=pltpu.VMEM)


def smem_spec():
    return pl.BlockSpec(memory_space=pltpu.SMEM)


def cost(matmuls, rows, cols, depth, passes=0):
    return pl.CostEstimate(
        flops=2 * matmuls * rows * cols * depth, bytes_accessed=passes * rows * cols, transcendentals=0
    )


def params():
    return pltpu.CompilerParams(vmem_limit_bytes=VMEM_LIMIT)


def dot_nt(a, b):
    return lax.dot_general(a, b, (((1,), (1,)), ((), ())), preferred_element_type=jnp.float32)


def dot_tn(a, b):
    return lax.dot_general(a, b, (((0,), (0,)), ((), ())), preferred_element_type=jnp.float32)


def own_kernel(core_ref, images, texts, got_images, got_texts, own, other, sem):
    rows = images.shape[0]
    core = core_ref[0]
    top, low = pl.ds(0, rows), pl.ds(rows, rows)
    orders = ((images, got_images, got_texts, texts), (texts, got_texts, got_images, images))

    def copies(order):
        places = (own.at[top], own.at[low], other.at[top], other.at[low])
        return [pltpu.make_async_copy(a, p, sem.at[j]) for j, (a, p) in enumerate(zip(order, places))]

    for c in range(2):

        @pl.when(core == c)
        def _():
            for copy in copies(orders[c]):
                copy.start()
            for copy in copies(orders[c]):
                copy.wait()


def own_call(core, *parts):
    rows, features = parts[0].shape
    block = pltpu.VMEM((2 * rows, features), parts[0].dtype)
    return pl.pallas_call(
        own_kernel,
        in_specs=[smem_spec()] + [pl.BlockSpec(memory_space=pl.ANY)] * 4,
        out_specs=[vmem_spec()] * 2,
        out_shape=[block, block],
        scratch_shapes=[pltpu.SemaphoreType.DMA((4,))],
        compiler_params=params(),
        cost_estimate=cost(0, rows, features, 1, 16),
        name="own",
    )(core, *parts)


def join_kernel(b0, b1, b2, out):
    rows = b0.shape[0]
    for j, b in enumerate((b0, b1, b2)):
        out[j * rows : (j + 1) * rows, :] = b[...]


def join_call(*parts):
    rows, features = parts[0].shape
    return pl.pallas_call(
        join_kernel,
        in_specs=[vmem_spec()] * 3,
        out_specs=vmem_spec(),
        out_shape=jax.ShapeDtypeStruct((3 * rows, features), parts[0].dtype),
        compiler_params=params(),
        cost_estimate=cost(0, 3 * rows, features, 1, 4),
        name="join",
    )(*parts)


def views(refs):
    own, near = refs[:2]
    rows = own.shape[0]
    return [own] + [near.at[pl.ds(j * rows, rows)] for j in range(3)] + list(refs[2:])


def take_half(core, blocks, shift, out):
    rows = blocks[0].shape[0]
    for c in range(2):

        @pl.when(core == c)
        def _():
            for j in range(4):
                out[j * rows : (j + 1) * rows, :] = blocks[4 * (c ^ shift) + j][...]


def scores_kernel(scale, core_ref, *refs):
    a_refs, b_refs = refs[:8], views(refs[8:14])
    e_ref, a_stat, b_stat, flags, a_cat, b_cat, col_m, col_s = refs[14:]
    rows = a_refs[0].shape[0]
    half = 4 * rows
    core = core_ref[0]
    for q in range(2):
        take_half(core, b_refs, q, b_cat.at[q])

    def quadrant(q):
        b_half = b_cat[q]
        sums = []
        col = None
        for r in range(4):
            sl = slice(r * rows, (r + 1) * rows)
            e = jnp.exp2(dot_nt(a_refs[4 * q + r][...], b_half) * scale)
            e_ref[q, sl, :] = e
            sums.append(jnp.sum(e, axis=1, keepdims=True))
            part = jnp.sum(e, axis=0, keepdims=True)
            col = part if col is None else col + part
        row_lse = jnp.log2(row_of(jnp.concatenate(sums, axis=0), half))
        col_lse = jnp.log2(col)
        for j in range(4):
            sl = slice(j * rows, (j + 1) * rows)
            a_stat[4 * q + j : 4 * q + j + 1, :] = row_lse[:, sl]
            b_stat[pl.ds((q ^ core) * 4 + j, 1), :] = col_lse[:, sl]
        reach = jnp.max(jnp.maximum(jnp.abs(row_lse), jnp.abs(col_lse)))
        bad = jnp.logical_not(reach <= RANGE)
        flags[q] = bad.astype(jnp.int32)

        @pl.when(bad)
        def _():
            for r in range(4):
                a_cat[r * rows : (r + 1) * rows, :] = a_refs[4 * q + r][...]
            col_m[...] = jnp.full_like(col_m, -jnp.inf)
            col_s[...] = jnp.zeros_like(col_s)

            @pl.loop(0, 4)
            def _(r):
                sl = pl.ds(pl.multiple_of(r * rows, 16), rows)
                s = dot_nt(a_cat[sl, :], b_cat[q]) * scale
                e_ref[q, sl, :] = s
                row_m = jnp.max(s, axis=1, keepdims=True)
                row_s = jnp.sum(jnp.exp2(s - row_m), axis=1, keepdims=True)
                a_stat[pl.ds(4 * q + r, 1), :] = row_of(row_m + jnp.log2(row_s), rows)
                blk_m = jnp.max(s, axis=0, keepdims=True)
                blk_s = jnp.sum(jnp.exp2(s - blk_m), axis=0, keepdims=True)
                before = col_m[...]
                top = jnp.maximum(before, blk_m)
                col_s[...] = col_s[...] * jnp.exp2(before - top) + blk_s * jnp.exp2(blk_m - top)
                col_m[...] = top

            lse = col_m[...] + jnp.log2(col_s[...])
            for j in range(4):
                b_stat[pl.ds((q ^ core) * 4 + j, 1), :] = lse[:, j * rows : (j + 1) * rows]

    quadrant(0)
    quadrant(1)


def scores_call(core, a_blocks, b_blocks, scale):
    rows, features = a_blocks[0].shape
    half = 4 * rows
    stat = jax.ShapeDtypeStruct((8, rows), jnp.float32)
    return pl.pallas_call(
        functools.partial(scores_kernel, scale),
        in_specs=[smem_spec()] + [vmem_spec()] * 14,
        out_specs=[vmem_spec()] * 3 + [smem_spec()],
        out_shape=[
            pltpu.VMEM((2, half, half), jnp.float32),
            stat,
            stat,
            jax.ShapeDtypeStruct((2,), jnp.int32),
        ],
        scratch_shapes=[
            pltpu.VMEM((half, features), jnp.bfloat16),
            pltpu.VMEM((2, half, features), jnp.bfloat16),
            pltpu.VMEM((1, half), jnp.float32),
            pltpu.VMEM((1, half), jnp.float32),
        ],
        compiler_params=params(),
        cost_estimate=cost(2, half, half, features),
        name="scores",
    )(core, *a_blocks, *b_blocks)


def merge_kernel(m, mine_ref, got_ref, out_ref):
    for k in range(8):
        j = PLACE[ORDER[k] ^ m]
        mine, got = mine_ref[k : k + 1, :], got_ref[j : j + 1, :]
        top = jnp.maximum(mine, got)
        out_ref[k : k + 1, :] = top + jnp.log2(jnp.exp2(mine - top) + jnp.exp2(got - top))


def merge_call(mine, got, m):
    return pl.pallas_call(
        functools.partial(merge_kernel, m),
        in_specs=[vmem_spec()] * 2,
        out_specs=vmem_spec(),
        out_shape=jax.ShapeDtypeStruct(mine.shape, jnp.float32),
        compiler_params=pltpu.CompilerParams(vmem_limit_bytes=2 * 1024 * 1024),
        name="merge",
    )(mine, got)


def weights_kernel(core_ref, flags, e_ref, a_lse, b_lse, *refs):
    a_refs, (w_ref, gb_hi, a_half) = refs[:8], refs[8:]
    rows = a_lse.shape[1]
    half = 4 * rows
    core = core_ref[0]
    take_half(core, a_refs, 1, a_half)
    for q in range(2):
        a_row = jnp.concatenate([a_lse[4 * q + j : 4 * q + j + 1, :] for j in range(4)], axis=1)
        b_row = jnp.concatenate([b_lse[pl.ds((q ^ core) * 4 + j, 1), :] for j in range(4)], axis=1)

        @pl.when(flags[q] == 0)
        def _():
            a_col = column_of(jnp.exp2(-a_row), half)
            b_exp = jnp.exp2(-b_row)
            for r in range(4):
                sl = slice(r * rows, (r + 1) * rows)
                w_ref[q, sl, :] = (e_ref[q, sl, :] * (a_col[sl, :] + b_exp)).astype(jnp.bfloat16)

        @pl.when(flags[q] != 0)
        def _():
            a_col = column_of(a_row, half)
            for r in range(4):
                sl = slice(r * rows, (r + 1) * rows)
                s = e_ref[q, sl, :]
                w_ref[q, sl, :] = (jnp.exp2(s - a_col[sl, :]) + jnp.exp2(s - b_row)).astype(jnp.bfloat16)

    half_rows = gb_hi.shape[0]
    gb_hi[...] = (0.5 * dot_tn(w_ref[1 - core, :, :half_rows], a_half[...])).astype(jnp.bfloat16)


def weights_call(core, flags, e, a_lse, b_lse, a_blocks):
    rows, features = a_blocks[0].shape
    half = 4 * rows
    return pl.pallas_call(
        weights_kernel,
        in_specs=[smem_spec()] * 2 + [vmem_spec()] * 11,
        out_specs=[vmem_spec()] * 2,
        out_shape=[
            pltpu.VMEM((2, half, half), jnp.bfloat16),
            jax.ShapeDtypeStruct((2 * rows, features), jnp.bfloat16),
        ],
        scratch_shapes=[pltpu.VMEM((half, features), jnp.bfloat16)],
        compiler_params=params(),
        cost_estimate=cost(1, half, half, features, 12),
        name="weights",
    )(core, flags, e, a_lse, b_lse, *a_blocks)


def second_kernel(core_ref, w_ref, *refs):
    a_refs, (gb, a_half) = refs[:8], refs[8:]
    core = core_ref[0]
    take_half(core, a_refs, 1, a_half)
    gb[...] = (0.5 * dot_tn(w_ref[1 - core, :, gb.shape[0] :], a_half[...])).astype(jnp.bfloat16)


def second_call(core, w, a_blocks):
    rows, features = a_blocks[0].shape
    half = 4 * rows
    return pl.pallas_call(
        second_kernel,
        in_specs=[smem_spec()] + [vmem_spec()] * 9,
        out_specs=vmem_spec(),
        out_shape=jax.ShapeDtypeStruct((2 * rows, features), jnp.bfloat16),
        scratch_shapes=[pltpu.VMEM((half, features), jnp.bfloat16)],
        compiler_params=params(),
        cost_estimate=cost(1, half, 2 * rows, features),
        name="second",
    )(core, w, *a_blocks)


def low_kernel(core_ref, w_ref, *refs):
    a_refs, (gb0, gb_lo, a_half) = refs[:8], refs[8:]
    rows = gb0.shape[0]
    core = core_ref[0]
    take_half(core, a_refs, 0, a_half)
    g = 0.5 * dot_tn(w_ref[core], a_half[...])
    gb0[...] = g[:rows]
    gb_lo[...] = g[rows:].astype(jnp.bfloat16)


def low_call(core, w, a_blocks):
    rows, features = a_blocks[0].shape
    half = 4 * rows
    return pl.pallas_call(
        low_kernel,
        in_specs=[smem_spec()] + [vmem_spec()] * 9,
        out_specs=[vmem_spec()] * 2,
        out_shape=[
            jax.ShapeDtypeStruct((rows, features), jnp.float32),
            jax.ShapeDtypeStruct((half - rows, features), jnp.bfloat16),
        ],
        scratch_shapes=[pltpu.VMEM((half, features), jnp.bfloat16)],
        compiler_params=params(),
        cost_estimate=cost(1, half, half, features),
        name="low",
    )(core, w, *a_blocks)


def far_kernel(ga_hi, got, more, *outs):
    rows = outs[0].shape[0]
    for j in range(4):
        part = (got if j < 2 else more)[(j % 2) * rows : (j % 2 + 1) * rows, :]
        outs[j][...] = (ga_hi[j * rows : (j + 1) * rows, :] + part.astype(jnp.float32)).astype(jnp.bfloat16)


def far_call(ga_hi, got, more):
    half, features = ga_hi.shape
    rows = half // 4
    return pl.pallas_call(
        far_kernel,
        in_specs=[vmem_spec()] * 3,
        out_specs=[vmem_spec()] * 4,
        out_shape=[jax.ShapeDtypeStruct((rows, features), jnp.bfloat16)] * 4,
        compiler_params=params(),
        cost_estimate=cost(0, half, features, 1, 8),
        name="far",
    )(ga_hi, got, more)


def side_kernel(q, core_ref, w_ref, *refs):
    b_refs, (ga, b_half) = views(refs[:6]), refs[6:]
    take_half(core_ref[0], b_refs, q, b_half)
    ga[...] = 0.5 * jnp.dot(w_ref[q], b_half[...], preferred_element_type=jnp.float32)


def side_call(q, core, w, b_blocks):
    rows, features = b_blocks[0].shape
    half = 4 * rows
    return pl.pallas_call(
        functools.partial(side_kernel, q),
        in_specs=[smem_spec()] + [vmem_spec()] * 7,
        out_specs=vmem_spec(),
        out_shape=pltpu.VMEM((half, features), jnp.float32),
        scratch_shapes=[pltpu.VMEM((half, features), jnp.bfloat16)],
        compiler_params=params(),
        cost_estimate=cost(1, half, half if q == 0 else rows // 4, features),
        name="side",
    )(core, w, *b_blocks)


def near_kernel(ga_lo, got0, got_lo, r_xy, r_yz, r_xz, p0, p1, p2, p4):
    rows = p0.shape[0]
    wide = lambda ref: ref[...].astype(jnp.float32)
    p0[...] = ga_lo[:rows] + got0[...]
    part = lambda j: ga_lo[j * rows : (j + 1) * rows, :] + got_lo[(j - 1) * rows : j * rows, :].astype(jnp.float32)
    p1[...] = (part(1) + wide(r_xz)).astype(jnp.bfloat16)
    p2[...] = (part(2) + wide(r_xy)).astype(jnp.bfloat16)
    p4[...] = (part(3) + wide(r_yz)).astype(jnp.bfloat16)


def near_call(ga_lo, got0, got_lo, *received):
    rows, features = got0.shape
    narrow = jax.ShapeDtypeStruct((rows, features), jnp.bfloat16)
    return pl.pallas_call(
        near_kernel,
        in_specs=[vmem_spec()] * 6,
        out_specs=[vmem_spec()] * 4,
        out_shape=[pltpu.VMEM((rows, features), jnp.float32)] + [narrow] * 3,
        compiler_params=params(),
        cost_estimate=cost(0, 4 * rows, features, 1, 12),
        name="near",
    )(ga_lo, got0, got_lo, *received)


def body(images, texts):
    rows, features = images.shape
    scale = 4.0 / math.sqrt(features) * LOG2E
    core = lax.axis_index("core")
    first = core == 0
    core_arr = core.astype(jnp.int32).reshape(1)
    own, other = own_call(core_arr, images, texts, swap(images), swap(texts))
    near = {m: to_cube(own, m) for m in (4, 2, 1)}
    far = {7: to_cube(near[1], 6), 5: to_cube(near[1], 4), 3: to_cube(near[2], 1), 6: to_cube(near[4], 2)}
    blocks = {0: own, **near, **far}
    in_vmem = lambda a: pltpu.with_memory_space_constraint(a, pltpu.VMEM)
    a_blocks = [in_vmem(blocks[m]) for m in ORDER]
    swapped = {m: swap(far[m]) for m in (3, 5, 6)}
    last, swapped[3], swapped[5], swapped[6] = lax.optimization_barrier((far[7], swapped[3], swapped[5], swapped[6]))
    swapped[7] = swap(last)
    b_blocks = [other, swap(join_call(near[1], near[2], near[4]))] + [swapped[m] for m in ORDER[4:]]
    b_blocks = [in_vmem(b) for b in b_blocks]

    e, a_stat, b_stat, flags = scores_call(core_arr, a_blocks, b_blocks, scale)
    a_lse = merge_call(a_stat, swap(b_stat), 0)
    for m in (1, 2, 4):
        a_lse = merge_call(a_lse, to_cube(a_lse, m), m)
    b_lse = swap(a_lse)

    w, gb_hi = weights_call(core_arr, flags, e, a_lse, b_lse, a_blocks)
    got_hi = swap(gb_hi)
    got_more = swap(second_call(core_arr, w, a_blocks))
    ga_hi = side_call(1, core_arr, w, b_blocks)
    p = dict(zip(ORDER[4:], far_call(ga_hi, got_hi, got_more)))
    p[7], w = lax.optimization_barrier((p[7], w))
    from_xy = to_cube(p[3], 1)
    from_yz = to_cube(p[6], 2)
    from_xz = to_cube(p[5], 4)
    from_xyz = to_cube(p[7], 7)
    gb0, gb_lo = low_call(core_arr, w, a_blocks)
    got0, got_lo = swap(gb0), swap(gb_lo)
    ga_lo = side_call(0, core_arr, w, b_blocks)
    p0, p1, p2, p4 = near_call(ga_lo, got0, got_lo, from_xy, from_yz, from_xz)
    wide = lambda a: a.astype(jnp.float32)
    total = p0 + wide(from_xyz) + wide(to_cube(p1, 1)) + wide(to_cube(p2, 2)) + wide(to_cube(p4, 4))
    kept, sent = total[:rows], total[rows:]
    got_sum = swap(sent)
    image_sum = jnp.where(first, kept, got_sum)
    text_sum = jnp.where(first, got_sum, kept)
    return (image_sum - wide(texts), text_sum - wide(images))


def solution(mesh):
    chips = Mesh(mesh.devices.reshape(SIZES), AXES)
    spec = P(AXES, None)
    return jax.shard_map(
        body,
        mesh=chips,
        in_specs=(spec, spec),
        out_specs=(spec, spec),
        check_vma=False,
    )
```

```python
import functools
import math

import jax
import jax.numpy as jnp
from jax import lax
from jax.experimental import pallas as pl
from jax.experimental.pallas import tpu as pltpu
from jax.sharding import Mesh, PartitionSpec as P

AXES = ("y", "core", "x", "z")
SIZES = (4, 2, 4, 4)
ORDER = (0, 1, 2, 4, 3, 5, 6, 7)
PLACE = tuple(ORDER.index(m) for m in range(8))
LOG2E = 1.4426950408889634
VMEM_LIMIT = 12 * 1024 * 1024
RANGE = 80.0


def flat(y, c, x, z):
    return ((y * 2 + c) * 4 + x) * 4 + z


def coords():
    for y in range(4):
        for c in range(2):
            for x in range(4):
                for z in range(4):
                    yield y, c, x, z


def partner(v, wrapped):
    return 3 - v if wrapped else v ^ 1


def across(m):
    pairs = []
    for y, c, x, z in coords():
        target = (
            partner(y, c == 0) if m & 2 else y,
            c,
            partner(x, c == 1) if m & 1 else x,
            partner(z, c == 1) if m & 4 else z,
        )
        pairs.append((flat(y, c, x, z), flat(*target)))
    return pairs


SWAP = [(flat(y, c, x, z), flat(y, 1 - c, x, z)) for y, c, x, z in coords()]


def to_cube(a, m):
    return lax.ppermute(a, AXES, across(m))


def swap(a):
    return lax.ppermute(a, AXES, SWAP)


def column_of(row, rows):
    padded = -(-rows // 128) * 128
    wide = jnp.broadcast_to(row, (128, rows))
    if padded != rows:
        wide = jnp.concatenate([wide, jnp.zeros((128, padded - rows), jnp.float32)], axis=1)
    return wide.T[:rows, :1]


def row_of(column, rows):
    padded = -(-rows // 128) * 128
    wide = jnp.broadcast_to(column, (rows, 128))
    if padded != rows:
        wide = jnp.concatenate([wide, jnp.zeros((padded - rows, 128), jnp.float32)], axis=0)
    return wide.T[:1, :rows]


def vmem_spec():
    return pl.BlockSpec(memory_space=pltpu.VMEM)


def smem_spec():
    return pl.BlockSpec(memory_space=pltpu.SMEM)


def cost(matmuls, rows, cols, depth, passes=0):
    return pl.CostEstimate(
        flops=2 * matmuls * rows * cols * depth, bytes_accessed=passes * rows * cols, transcendentals=0
    )


def params():
    return pltpu.CompilerParams(vmem_limit_bytes=VMEM_LIMIT)


def dot_nt(a, b):
    return lax.dot_general(a, b, (((1,), (1,)), ((), ())), preferred_element_type=jnp.float32)


def dot_tn(a, b):
    return lax.dot_general(a, b, (((0,), (0,)), ((), ())), preferred_element_type=jnp.float32)


def own_kernel(core_ref, images, texts, got_images, got_texts, own, other, sem):
    rows = images.shape[0]
    core = core_ref[0]
    top, low = pl.ds(0, rows), pl.ds(rows, rows)
    orders = ((images, got_images, got_texts, texts), (texts, got_texts, got_images, images))

    def copies(order):
        places = (own.at[top], own.at[low], other.at[top], other.at[low])
        return [pltpu.make_async_copy(a, p, sem.at[j]) for j, (a, p) in enumerate(zip(order, places))]

    for c in range(2):

        @pl.when(core == c)
        def _():
            for copy in copies(orders[c]):
                copy.start()
            for copy in copies(orders[c]):
                copy.wait()


def own_call(core, *parts):
    rows, features = parts[0].shape
    block = pltpu.VMEM((2 * rows, features), parts[0].dtype)
    return pl.pallas_call(
        own_kernel,
        in_specs=[smem_spec()] + [pl.BlockSpec(memory_space=pl.ANY)] * 4,
        out_specs=[vmem_spec()] * 2,
        out_shape=[block, block],
        scratch_shapes=[pltpu.SemaphoreType.DMA((4,))],
        compiler_params=params(),
        cost_estimate=cost(0, rows, features, 1, 16),
        name="own",
    )(core, *parts)


def join_kernel(b0, b1, b2, out):
    rows = b0.shape[0]
    for j, b in enumerate((b0, b1, b2)):
        out[j * rows : (j + 1) * rows, :] = b[...]


def join_call(*parts):
    rows, features = parts[0].shape
    return pl.pallas_call(
        join_kernel,
        in_specs=[vmem_spec()] * 3,
        out_specs=vmem_spec(),
        out_shape=jax.ShapeDtypeStruct((3 * rows, features), parts[0].dtype),
        compiler_params=params(),
        cost_estimate=cost(0, 3 * rows, features, 1, 4),
        name="join",
    )(*parts)


def views(refs):
    own, near = refs[:2]
    rows = own.shape[0]
    return [own] + [near.at[pl.ds(j * rows, rows)] for j in range(3)] + list(refs[2:])


def take_half(core, blocks, shift, out):
    rows = blocks[0].shape[0]
    for c in range(2):

        @pl.when(core == c)
        def _():
            for j in range(4):
                out[j * rows : (j + 1) * rows, :] = blocks[4 * (c ^ shift) + j][...]


def scores_kernel(scale, core_ref, *refs):
    a_refs, b_refs = refs[:8], views(refs[8:14])
    e_ref, a_stat, b_stat, flags, a_cat, b_cat, col_m, col_s = refs[14:]
    rows = a_refs[0].shape[0]
    half = 4 * rows
    core = core_ref[0]
    for q in range(2):
        take_half(core, b_refs, q, b_cat.at[q])

    def quadrant(q):
        b_half = b_cat[q]
        sums = []
        col = None
        for r in range(4):
            sl = slice(r * rows, (r + 1) * rows)
            e = jnp.exp2(dot_nt(a_refs[4 * q + r][...], b_half) * scale)
            e_ref[q, sl, :] = e
            sums.append(jnp.sum(e, axis=1, keepdims=True))
            part = jnp.sum(e, axis=0, keepdims=True)
            col = part if col is None else col + part
        row_lse = jnp.log2(row_of(jnp.concatenate(sums, axis=0), half))
        col_lse = jnp.log2(col)
        for j in range(4):
            sl = slice(j * rows, (j + 1) * rows)
            a_stat[4 * q + j : 4 * q + j + 1, :] = row_lse[:, sl]
            b_stat[pl.ds((q ^ core) * 4 + j, 1), :] = col_lse[:, sl]
        reach = jnp.max(jnp.maximum(jnp.abs(row_lse), jnp.abs(col_lse)))
        bad = jnp.logical_not(reach <= RANGE)
        flags[q] = bad.astype(jnp.int32)

        @pl.when(bad)
        def _():
            for r in range(4):
                a_cat[r * rows : (r + 1) * rows, :] = a_refs[4 * q + r][...]
            col_m[...] = jnp.full_like(col_m, -jnp.inf)
            col_s[...] = jnp.zeros_like(col_s)

            @pl.loop(0, 4)
            def _(r):
                sl = pl.ds(pl.multiple_of(r * rows, 16), rows)
                s = dot_nt(a_cat[sl, :], b_cat[q]) * scale
                e_ref[q, sl, :] = s
                row_m = jnp.max(s, axis=1, keepdims=True)
                row_s = jnp.sum(jnp.exp2(s - row_m), axis=1, keepdims=True)
                a_stat[pl.ds(4 * q + r, 1), :] = row_of(row_m + jnp.log2(row_s), rows)
                blk_m = jnp.max(s, axis=0, keepdims=True)
                blk_s = jnp.sum(jnp.exp2(s - blk_m), axis=0, keepdims=True)
                before = col_m[...]
                top = jnp.maximum(before, blk_m)
                col_s[...] = col_s[...] * jnp.exp2(before - top) + blk_s * jnp.exp2(blk_m - top)
                col_m[...] = top

            lse = col_m[...] + jnp.log2(col_s[...])
            for j in range(4):
                b_stat[pl.ds((q ^ core) * 4 + j, 1), :] = lse[:, j * rows : (j + 1) * rows]

    quadrant(0)
    quadrant(1)


def scores_call(core, a_blocks, b_blocks, scale):
    rows, features = a_blocks[0].shape
    half = 4 * rows
    stat = jax.ShapeDtypeStruct((8, rows), jnp.float32)
    return pl.pallas_call(
        functools.partial(scores_kernel, scale),
        in_specs=[smem_spec()] + [vmem_spec()] * 14,
        out_specs=[vmem_spec()] * 3 + [smem_spec()],
        out_shape=[
            pltpu.VMEM((2, half, half), jnp.float32),
            stat,
            stat,
            jax.ShapeDtypeStruct((2,), jnp.int32),
        ],
        scratch_shapes=[
            pltpu.VMEM((half, features), jnp.bfloat16),
            pltpu.VMEM((2, half, features), jnp.bfloat16),
            pltpu.VMEM((1, half), jnp.float32),
            pltpu.VMEM((1, half), jnp.float32),
        ],
        compiler_params=params(),
        cost_estimate=cost(2, half, half, features),
        name="scores",
    )(core, *a_blocks, *b_blocks)


def merge_kernel(m, mine_ref, got_ref, out_ref):
    for k in range(8):
        j = PLACE[ORDER[k] ^ m]
        mine, got = mine_ref[k : k + 1, :], got_ref[j : j + 1, :]
        top = jnp.maximum(mine, got)
        out_ref[k : k + 1, :] = top + jnp.log2(jnp.exp2(mine - top) + jnp.exp2(got - top))


def merge_call(mine, got, m):
    return pl.pallas_call(
        functools.partial(merge_kernel, m),
        in_specs=[vmem_spec()] * 2,
        out_specs=vmem_spec(),
        out_shape=jax.ShapeDtypeStruct(mine.shape, jnp.float32),
        compiler_params=pltpu.CompilerParams(vmem_limit_bytes=2 * 1024 * 1024),
        name="merge",
    )(mine, got)


def weights_kernel(core_ref, flags, e_ref, a_lse, b_lse, *refs):
    a_refs, (w_ref, gb_hi, a_half) = refs[:8], refs[8:]
    rows = a_lse.shape[1]
    half = 4 * rows
    core = core_ref[0]
    take_half(core, a_refs, 1, a_half)
    for q in range(2):
        a_row = jnp.concatenate([a_lse[4 * q + j : 4 * q + j + 1, :] for j in range(4)], axis=1)
        b_row = jnp.concatenate([b_lse[pl.ds((q ^ core) * 4 + j, 1), :] for j in range(4)], axis=1)

        @pl.when(flags[q] == 0)
        def _():
            a_col = column_of(jnp.exp2(-a_row), half)
            b_exp = jnp.exp2(-b_row)
            for r in range(4):
                sl = slice(r * rows, (r + 1) * rows)
                w_ref[q, sl, :] = (e_ref[q, sl, :] * (a_col[sl, :] + b_exp)).astype(jnp.bfloat16)

        @pl.when(flags[q] != 0)
        def _():
            a_col = column_of(a_row, half)
            for r in range(4):
                sl = slice(r * rows, (r + 1) * rows)
                s = e_ref[q, sl, :]
                w_ref[q, sl, :] = (jnp.exp2(s - a_col[sl, :]) + jnp.exp2(s - b_row)).astype(jnp.bfloat16)

    gb_hi[...] = (0.5 * dot_tn(w_ref[1 - core], a_half[...])).astype(jnp.bfloat16)


def weights_call(core, flags, e, a_lse, b_lse, a_blocks):
    rows, features = a_blocks[0].shape
    half = 4 * rows
    return pl.pallas_call(
        weights_kernel,
        in_specs=[smem_spec()] * 2 + [vmem_spec()] * 11,
        out_specs=[vmem_spec()] * 2,
        out_shape=[
            pltpu.VMEM((2, half, half), jnp.bfloat16),
            jax.ShapeDtypeStruct((half, features), jnp.bfloat16),
        ],
        scratch_shapes=[pltpu.VMEM((half, features), jnp.bfloat16)],
        compiler_params=params(),
        cost_estimate=cost(1, half, half, features, 12),
        name="weights",
    )(core, flags, e, a_lse, b_lse, *a_blocks)


def middle_kernel(core_ref, w_ref, *refs):
    a_refs, b_refs = refs[:8], views(refs[8:14])
    ga_hi, gb0, gb_lo, a_half, b_half = refs[14:]
    rows = gb0.shape[0]
    core = core_ref[0]
    take_half(core, a_refs, 0, a_half)
    take_half(core, b_refs, 1, b_half)
    g = 0.5 * dot_tn(w_ref[core], a_half[...])
    gb0[...] = g[:rows]
    gb_lo[...] = g[rows:].astype(jnp.bfloat16)
    ga_hi[...] = 0.5 * jnp.dot(w_ref[1], b_half[...], preferred_element_type=jnp.float32)


def middle_call(core, w, a_blocks, b_blocks):
    rows, features = a_blocks[0].shape
    half = 4 * rows
    return pl.pallas_call(
        middle_kernel,
        in_specs=[smem_spec()] + [vmem_spec()] * 15,
        out_specs=[vmem_spec()] * 3,
        out_shape=[
            pltpu.VMEM((half, features), jnp.float32),
            jax.ShapeDtypeStruct((rows, features), jnp.float32),
            jax.ShapeDtypeStruct((half - rows, features), jnp.bfloat16),
        ],
        scratch_shapes=[pltpu.VMEM((half, features), jnp.bfloat16)] * 2,
        compiler_params=params(),
        cost_estimate=cost(2, half, half, features),
        name="middle",
    )(core, w, *a_blocks, *b_blocks)


def far_kernel(ga_hi, got, *outs):
    rows = outs[0].shape[0]
    for j in range(4):
        sl = slice(j * rows, (j + 1) * rows)
        outs[j][...] = (ga_hi[sl, :] + got[sl, :].astype(jnp.float32)).astype(jnp.bfloat16)


def far_call(ga_hi, got):
    half, features = ga_hi.shape
    rows = half // 4
    return pl.pallas_call(
        far_kernel,
        in_specs=[vmem_spec()] * 2,
        out_specs=[vmem_spec()] * 4,
        out_shape=[jax.ShapeDtypeStruct((rows, features), jnp.bfloat16)] * 4,
        compiler_params=params(),
        cost_estimate=cost(0, half, features, 1, 8),
        name="far",
    )(ga_hi, got)


def last_kernel(core_ref, w_ref, *refs):
    b_refs, (ga_lo, b_half) = views(refs[:6]), refs[6:]
    take_half(core_ref[0], b_refs, 0, b_half)
    ga_lo[...] = 0.5 * jnp.dot(w_ref[0], b_half[...], preferred_element_type=jnp.float32)


def last_call(core, w, b_blocks):
    rows, features = b_blocks[0].shape
    half = 4 * rows
    return pl.pallas_call(
        last_kernel,
        in_specs=[smem_spec()] + [vmem_spec()] * 7,
        out_specs=vmem_spec(),
        out_shape=pltpu.VMEM((half, features), jnp.float32),
        scratch_shapes=[pltpu.VMEM((half, features), jnp.bfloat16)],
        compiler_params=params(),
        cost_estimate=cost(1, half, half, features),
        name="last",
    )(core, w, *b_blocks)


def near_kernel(ga_lo, got0, got_lo, r_xy, r_yz, r_xz, r_xyz, p0, p1, p2, p4):
    rows = p0.shape[0]
    wide = lambda ref: ref[...].astype(jnp.float32)
    p0[...] = ga_lo[:rows] + got0[...] + wide(r_xyz)
    part = lambda j: ga_lo[j * rows : (j + 1) * rows, :] + got_lo[(j - 1) * rows : j * rows, :].astype(jnp.float32)
    p1[...] = (part(1) + wide(r_xz)).astype(jnp.bfloat16)
    p2[...] = (part(2) + wide(r_xy)).astype(jnp.bfloat16)
    p4[...] = (part(3) + wide(r_yz)).astype(jnp.bfloat16)


def near_call(ga_lo, got0, got_lo, *received):
    rows, features = got0.shape
    narrow = jax.ShapeDtypeStruct((rows, features), jnp.bfloat16)
    return pl.pallas_call(
        near_kernel,
        in_specs=[vmem_spec()] * 7,
        out_specs=[vmem_spec()] * 4,
        out_shape=[pltpu.VMEM((rows, features), jnp.float32)] + [narrow] * 3,
        compiler_params=params(),
        cost_estimate=cost(0, 4 * rows, features, 1, 12),
        name="near",
    )(ga_lo, got0, got_lo, *received)


def body(images, texts):
    rows, features = images.shape
    scale = 4.0 / math.sqrt(features) * LOG2E
    core = lax.axis_index("core")
    first = core == 0
    core_arr = core.astype(jnp.int32).reshape(1)
    in_hbm = lambda a: pltpu.with_memory_space_constraint(a, pltpu.HBM)
    own, other = own_call(core_arr, in_hbm(images), in_hbm(texts), swap(images), swap(texts))
    near = {m: to_cube(own, m) for m in (4, 2, 1)}
    far = {7: to_cube(near[1], 6), 5: to_cube(near[1], 4), 3: to_cube(near[2], 1), 6: to_cube(near[4], 2)}
    blocks = {0: own, **near, **far}
    in_vmem = lambda a: pltpu.with_memory_space_constraint(a, pltpu.VMEM)
    a_blocks = [in_vmem(blocks[m]) for m in ORDER]
    swapped = {m: swap(far[m]) for m in (3, 5, 6)}
    last, swapped[3], swapped[5], swapped[6] = lax.optimization_barrier((far[7], swapped[3], swapped[5], swapped[6]))
    swapped[7] = swap(last)
    b_blocks = [other, swap(join_call(near[1], near[2], near[4]))] + [swapped[m] for m in ORDER[4:]]
    b_blocks = [in_vmem(b) for b in b_blocks]

    e, a_stat, b_stat, flags = scores_call(core_arr, a_blocks, b_blocks, scale)
    a_lse = merge_call(a_stat, swap(b_stat), 0)
    for m in (1, 2, 4):
        a_lse = merge_call(a_lse, to_cube(a_lse, m), m)
    b_lse = swap(a_lse)

    w, gb_hi = weights_call(core_arr, flags, e, a_lse, b_lse, a_blocks)
    got_hi = swap(gb_hi)
    ga_hi, gb0, gb_lo = middle_call(core_arr, w, a_blocks, b_blocks)
    got0, got_lo = swap(gb0), swap(gb_lo)
    p = dict(zip(ORDER[4:], far_call(ga_hi, got_hi)))
    from_xy = to_cube(p[3], 1)
    from_yz = to_cube(p[6], 2)
    from_xz = to_cube(p[5], 4)
    from_xyz = to_cube(p[7], 7)
    ga_lo = last_call(core_arr, w, b_blocks)
    p0, p1, p2, p4 = near_call(ga_lo, got0, got_lo, from_xy, from_yz, from_xz, from_xyz)
    wide = lambda a: a.astype(jnp.float32)
    total = p0 + wide(to_cube(p1, 1)) + wide(to_cube(p2, 2)) + wide(to_cube(p4, 4))
    kept, sent = total[:rows], total[rows:]
    got_sum = swap(sent)
    image_sum = jnp.where(first, kept, got_sum)
    text_sum = jnp.where(first, got_sum, kept)
    return (image_sum - wide(texts), text_sum - wide(images))


def solution(mesh):
    chips = Mesh(mesh.devices.reshape(SIZES), AXES)
    spec = P(AXES, None)
    return jax.shard_map(
        body,
        mesh=chips,
        in_specs=(spec, spec),
        out_specs=(spec, spec),
        check_vma=False,
    )
```

```python
import functools
import math

import jax
import jax.numpy as jnp
from jax import lax
from jax.experimental import pallas as pl
from jax.experimental.pallas import tpu as pltpu
from jax.sharding import Mesh, PartitionSpec as P

AXES = ("y", "core", "x", "z")
SIZES = (4, 2, 4, 4)
ORDER = (0, 1, 2, 4, 3, 5, 6, 7)
PLACE = tuple(ORDER.index(m) for m in range(8))
LOG2E = 1.4426950408889634
VMEM_LIMIT = 12 * 1024 * 1024
RANGE = 80.0


def flat(y, c, x, z):
    return ((y * 2 + c) * 4 + x) * 4 + z


def coords():
    for y in range(4):
        for c in range(2):
            for x in range(4):
                for z in range(4):
                    yield y, c, x, z


def partner(v, wrapped):
    return 3 - v if wrapped else v ^ 1


def across(m):
    pairs = []
    for y, c, x, z in coords():
        target = (
            partner(y, c == 0) if m & 2 else y,
            c,
            partner(x, c == 1) if m & 1 else x,
            partner(z, c == 1) if m & 4 else z,
        )
        pairs.append((flat(y, c, x, z), flat(*target)))
    return pairs


SWAP = [(flat(y, c, x, z), flat(y, 1 - c, x, z)) for y, c, x, z in coords()]


def to_cube(a, m):
    return lax.ppermute(a, AXES, across(m))


def swap(a):
    return lax.ppermute(a, AXES, SWAP)


def column_of(row, rows):
    padded = -(-rows // 128) * 128
    wide = jnp.broadcast_to(row, (128, rows))
    if padded != rows:
        wide = jnp.concatenate([wide, jnp.zeros((128, padded - rows), jnp.float32)], axis=1)
    return wide.T[:rows, :1]


def row_of(column, rows):
    padded = -(-rows // 128) * 128
    wide = jnp.broadcast_to(column, (rows, 128))
    if padded != rows:
        wide = jnp.concatenate([wide, jnp.zeros((padded - rows, 128), jnp.float32)], axis=0)
    return wide.T[:1, :rows]


def vmem_spec():
    return pl.BlockSpec(memory_space=pltpu.VMEM)


def smem_spec():
    return pl.BlockSpec(memory_space=pltpu.SMEM)


def cost(matmuls, rows, cols, depth, passes=0):
    return pl.CostEstimate(
        flops=2 * matmuls * rows * cols * depth, bytes_accessed=passes * rows * cols, transcendentals=0
    )


def params():
    return pltpu.CompilerParams(vmem_limit_bytes=VMEM_LIMIT)


def dot_nt(a, b):
    return lax.dot_general(a, b, (((1,), (1,)), ((), ())), preferred_element_type=jnp.float32)


def dot_tn(a, b):
    return lax.dot_general(a, b, (((0,), (0,)), ((), ())), preferred_element_type=jnp.float32)


def own_kernel(core_ref, images, texts, got_images, got_texts, own, other, sem):
    rows = images.shape[0]
    core = core_ref[0]
    top, low = pl.ds(0, rows), pl.ds(rows, rows)
    orders = ((images, got_images, got_texts, texts), (texts, got_texts, got_images, images))

    def copies(order):
        places = (own.at[top], own.at[low], other.at[top], other.at[low])
        return [pltpu.make_async_copy(a, p, sem.at[j]) for j, (a, p) in enumerate(zip(order, places))]

    for c in range(2):

        @pl.when(core == c)
        def _():
            for copy in copies(orders[c]):
                copy.start()
            for copy in copies(orders[c]):
                copy.wait()


def own_call(core, *parts):
    rows, features = parts[0].shape
    block = pltpu.VMEM((2 * rows, features), parts[0].dtype)
    return pl.pallas_call(
        own_kernel,
        in_specs=[smem_spec()] + [pl.BlockSpec(memory_space=pl.ANY)] * 4,
        out_specs=[vmem_spec()] * 2,
        out_shape=[block, block],
        scratch_shapes=[pltpu.SemaphoreType.DMA((4,))],
        compiler_params=params(),
        cost_estimate=cost(0, rows, features, 1, 16),
        name="own",
    )(core, *parts)


def join_kernel(b0, b1, b2, out):
    rows = b0.shape[0]
    for j, b in enumerate((b0, b1, b2)):
        out[j * rows : (j + 1) * rows, :] = b[...]


def join_call(*parts):
    rows, features = parts[0].shape
    return pl.pallas_call(
        join_kernel,
        in_specs=[vmem_spec()] * 3,
        out_specs=vmem_spec(),
        out_shape=jax.ShapeDtypeStruct((3 * rows, features), parts[0].dtype),
        compiler_params=params(),
        cost_estimate=cost(0, 3 * rows, features, 1, 4),
        name="join",
    )(*parts)


def views(refs):
    own, near = refs[:2]
    rows = own.shape[0]
    return [own] + [near.at[pl.ds(j * rows, rows)] for j in range(3)] + list(refs[2:])


def take_half(core, blocks, shift, out):
    rows = blocks[0].shape[0]
    for c in range(2):

        @pl.when(core == c)
        def _():
            for j in range(4):
                out[j * rows : (j + 1) * rows, :] = blocks[4 * (c ^ shift) + j][...]


def scores_kernel(scale, core_ref, *refs):
    a_refs, b_refs = refs[:8], views(refs[8:14])
    e_ref, a_stat, b_stat, flags, a_cat, b_cat, col_m, col_s = refs[14:]
    rows = a_refs[0].shape[0]
    half = 4 * rows
    core = core_ref[0]
    for q in range(2):
        take_half(core, b_refs, q, b_cat.at[q])

    def quadrant(q):
        b_half = b_cat[q]
        sums = []
        col = None
        for r in range(4):
            sl = slice(r * rows, (r + 1) * rows)
            e = jnp.exp2(dot_nt(a_refs[4 * q + r][...], b_half) * scale)
            e_ref[q, sl, :] = e
            sums.append(jnp.sum(e, axis=1, keepdims=True))
            part = jnp.sum(e, axis=0, keepdims=True)
            col = part if col is None else col + part
        row_lse = jnp.log2(row_of(jnp.concatenate(sums, axis=0), half))
        col_lse = jnp.log2(col)
        for j in range(4):
            sl = slice(j * rows, (j + 1) * rows)
            a_stat[4 * q + j : 4 * q + j + 1, :] = row_lse[:, sl]
            b_stat[pl.ds((q ^ core) * 4 + j, 1), :] = col_lse[:, sl]
        reach = jnp.max(jnp.maximum(jnp.abs(row_lse), jnp.abs(col_lse)))
        bad = jnp.logical_not(reach <= RANGE)
        flags[q] = bad.astype(jnp.int32)

        @pl.when(bad)
        def _():
            for r in range(4):
                a_cat[r * rows : (r + 1) * rows, :] = a_refs[4 * q + r][...]
            col_m[...] = jnp.full_like(col_m, -jnp.inf)
            col_s[...] = jnp.zeros_like(col_s)

            @pl.loop(0, 4)
            def _(r):
                sl = pl.ds(pl.multiple_of(r * rows, 16), rows)
                s = dot_nt(a_cat[sl, :], b_cat[q]) * scale
                e_ref[q, sl, :] = s
                row_m = jnp.max(s, axis=1, keepdims=True)
                row_s = jnp.sum(jnp.exp2(s - row_m), axis=1, keepdims=True)
                a_stat[pl.ds(4 * q + r, 1), :] = row_of(row_m + jnp.log2(row_s), rows)
                blk_m = jnp.max(s, axis=0, keepdims=True)
                blk_s = jnp.sum(jnp.exp2(s - blk_m), axis=0, keepdims=True)
                before = col_m[...]
                top = jnp.maximum(before, blk_m)
                col_s[...] = col_s[...] * jnp.exp2(before - top) + blk_s * jnp.exp2(blk_m - top)
                col_m[...] = top

            lse = col_m[...] + jnp.log2(col_s[...])
            for j in range(4):
                b_stat[pl.ds((q ^ core) * 4 + j, 1), :] = lse[:, j * rows : (j + 1) * rows]

    quadrant(0)
    quadrant(1)


def scores_call(core, a_blocks, b_blocks, scale):
    rows, features = a_blocks[0].shape
    half = 4 * rows
    stat = jax.ShapeDtypeStruct((8, rows), jnp.float32)
    return pl.pallas_call(
        functools.partial(scores_kernel, scale),
        in_specs=[smem_spec()] + [vmem_spec()] * 14,
        out_specs=[vmem_spec()] * 3 + [smem_spec()],
        out_shape=[
            pltpu.VMEM((2, half, half), jnp.float32),
            stat,
            stat,
            jax.ShapeDtypeStruct((2,), jnp.int32),
        ],
        scratch_shapes=[
            pltpu.VMEM((half, features), jnp.bfloat16),
            pltpu.VMEM((2, half, features), jnp.bfloat16),
            pltpu.VMEM((1, half), jnp.float32),
            pltpu.VMEM((1, half), jnp.float32),
        ],
        compiler_params=params(),
        cost_estimate=cost(2, half, half, features),
        name="scores",
    )(core, *a_blocks, *b_blocks)


def merge_kernel(m, mine_ref, got_ref, out_ref):
    for k in range(8):
        j = PLACE[ORDER[k] ^ m]
        mine, got = mine_ref[k : k + 1, :], got_ref[j : j + 1, :]
        top = jnp.maximum(mine, got)
        out_ref[k : k + 1, :] = top + jnp.log2(jnp.exp2(mine - top) + jnp.exp2(got - top))


def merge_call(mine, got, m):
    return pl.pallas_call(
        functools.partial(merge_kernel, m),
        in_specs=[vmem_spec()] * 2,
        out_specs=vmem_spec(),
        out_shape=jax.ShapeDtypeStruct(mine.shape, jnp.float32),
        compiler_params=pltpu.CompilerParams(vmem_limit_bytes=2 * 1024 * 1024),
        name="merge",
    )(mine, got)


def weights_kernel(core_ref, flags, e_ref, a_lse, b_lse, *refs):
    a_refs, (w_ref, gb_hi, a_half) = refs[:8], refs[8:]
    rows = a_lse.shape[1]
    half = 4 * rows
    core = core_ref[0]
    take_half(core, a_refs, 1, a_half)
    for q in range(2):
        a_row = jnp.concatenate([a_lse[4 * q + j : 4 * q + j + 1, :] for j in range(4)], axis=1)
        b_row = jnp.concatenate([b_lse[pl.ds((q ^ core) * 4 + j, 1), :] for j in range(4)], axis=1)

        @pl.when(flags[q] == 0)
        def _():
            a_col = column_of(jnp.exp2(-a_row), half)
            b_exp = jnp.exp2(-b_row)
            for r in range(4):
                sl = slice(r * rows, (r + 1) * rows)
                w_ref[q, sl, :] = (e_ref[q, sl, :] * (a_col[sl, :] + b_exp)).astype(jnp.bfloat16)

        @pl.when(flags[q] != 0)
        def _():
            a_col = column_of(a_row, half)
            for r in range(4):
                sl = slice(r * rows, (r + 1) * rows)
                s = e_ref[q, sl, :]
                w_ref[q, sl, :] = (jnp.exp2(s - a_col[sl, :]) + jnp.exp2(s - b_row)).astype(jnp.bfloat16)

    gb_hi[...] = (0.5 * dot_tn(w_ref[1 - core], a_half[...])).astype(jnp.bfloat16)


def weights_call(core, flags, e, a_lse, b_lse, a_blocks):
    rows, features = a_blocks[0].shape
    half = 4 * rows
    return pl.pallas_call(
        weights_kernel,
        in_specs=[smem_spec()] * 2 + [vmem_spec()] * 11,
        out_specs=[vmem_spec()] * 2,
        out_shape=[
            pltpu.VMEM((2, half, half), jnp.bfloat16),
            jax.ShapeDtypeStruct((half, features), jnp.bfloat16),
        ],
        scratch_shapes=[pltpu.VMEM((half, features), jnp.bfloat16)],
        compiler_params=params(),
        cost_estimate=cost(1, half, half, features, 12),
        name="weights",
    )(core, flags, e, a_lse, b_lse, *a_blocks)


def middle_kernel(core_ref, w_ref, *refs):
    a_refs, b_refs = refs[:8], views(refs[8:14])
    ga_hi, gb0, gb_lo, a_half, b_half = refs[14:]
    rows = gb0.shape[0]
    core = core_ref[0]
    take_half(core, a_refs, 0, a_half)
    take_half(core, b_refs, 1, b_half)
    g = 0.5 * dot_tn(w_ref[core], a_half[...])
    gb0[...] = g[:rows]
    gb_lo[...] = g[rows:].astype(jnp.bfloat16)
    ga_hi[...] = 0.5 * jnp.dot(w_ref[1], b_half[...], preferred_element_type=jnp.float32)


def middle_call(core, w, a_blocks, b_blocks):
    rows, features = a_blocks[0].shape
    half = 4 * rows
    return pl.pallas_call(
        middle_kernel,
        in_specs=[smem_spec()] + [vmem_spec()] * 15,
        out_specs=[vmem_spec()] * 3,
        out_shape=[
            pltpu.VMEM((half, features), jnp.float32),
            jax.ShapeDtypeStruct((rows, features), jnp.float32),
            jax.ShapeDtypeStruct((half - rows, features), jnp.bfloat16),
        ],
        scratch_shapes=[pltpu.VMEM((half, features), jnp.bfloat16)] * 2,
        compiler_params=params(),
        cost_estimate=cost(2, half, half, features),
        name="middle",
    )(core, w, *a_blocks, *b_blocks)


def far_kernel(ga_hi, got, *outs):
    rows = outs[0].shape[0]
    for j in range(4):
        sl = slice(j * rows, (j + 1) * rows)
        outs[j][...] = (ga_hi[sl, :] + got[sl, :].astype(jnp.float32)).astype(jnp.bfloat16)


def far_call(ga_hi, got):
    half, features = ga_hi.shape
    rows = half // 4
    return pl.pallas_call(
        far_kernel,
        in_specs=[vmem_spec()] * 2,
        out_specs=[vmem_spec()] * 4,
        out_shape=[jax.ShapeDtypeStruct((rows, features), jnp.bfloat16)] * 4,
        compiler_params=params(),
        cost_estimate=cost(0, half, features, 1, 8),
        name="far",
    )(ga_hi, got)


def last_kernel(core_ref, w_ref, *refs):
    b_refs, (ga_lo, b_half) = views(refs[:6]), refs[6:]
    take_half(core_ref[0], b_refs, 0, b_half)
    ga_lo[...] = 0.5 * jnp.dot(w_ref[0], b_half[...], preferred_element_type=jnp.float32)


def last_call(core, w, b_blocks):
    rows, features = b_blocks[0].shape
    half = 4 * rows
    return pl.pallas_call(
        last_kernel,
        in_specs=[smem_spec()] + [vmem_spec()] * 7,
        out_specs=vmem_spec(),
        out_shape=pltpu.VMEM((half, features), jnp.float32),
        scratch_shapes=[pltpu.VMEM((half, features), jnp.bfloat16)],
        compiler_params=params(),
        cost_estimate=cost(1, half, half, features),
        name="last",
    )(core, w, *b_blocks)


def near_kernel(ga_lo, got0, got_lo, r_xy, r_yz, r_xz, p0, p1, p2, p4):
    rows = p0.shape[0]
    wide = lambda ref: ref[...].astype(jnp.float32)
    p0[...] = ga_lo[:rows] + got0[...]
    part = lambda j: ga_lo[j * rows : (j + 1) * rows, :] + got_lo[(j - 1) * rows : j * rows, :].astype(jnp.float32)
    p1[...] = (part(1) + wide(r_xz)).astype(jnp.bfloat16)
    p2[...] = (part(2) + wide(r_xy)).astype(jnp.bfloat16)
    p4[...] = (part(3) + wide(r_yz)).astype(jnp.bfloat16)


def near_call(ga_lo, got0, got_lo, *received):
    rows, features = got0.shape
    narrow = jax.ShapeDtypeStruct((rows, features), jnp.bfloat16)
    return pl.pallas_call(
        near_kernel,
        in_specs=[vmem_spec()] * 6,
        out_specs=[vmem_spec()] * 4,
        out_shape=[pltpu.VMEM((rows, features), jnp.float32)] + [narrow] * 3,
        compiler_params=params(),
        cost_estimate=cost(0, 4 * rows, features, 1, 12),
        name="near",
    )(ga_lo, got0, got_lo, *received)


def body(images, texts):
    rows, features = images.shape
    scale = 4.0 / math.sqrt(features) * LOG2E
    core = lax.axis_index("core")
    first = core == 0
    core_arr = core.astype(jnp.int32).reshape(1)
    in_hbm = lambda a: pltpu.with_memory_space_constraint(a, pltpu.HBM)
    own, other = own_call(core_arr, in_hbm(images), in_hbm(texts), swap(images), swap(texts))
    near = {m: to_cube(own, m) for m in (4, 2, 1)}
    far = {7: to_cube(own, 7), 5: to_cube(near[1], 4), 3: to_cube(near[2], 1), 6: to_cube(near[4], 2)}
    blocks = {0: own, **near, **far}
    in_vmem = lambda a: pltpu.with_memory_space_constraint(a, pltpu.VMEM)
    a_blocks = [in_vmem(blocks[m]) for m in ORDER]
    swapped = {m: swap(far[m]) for m in (7, 5, 3)}
    last, *held = lax.optimization_barrier((far[6], swapped[7], swapped[5], swapped[3]))
    swapped.update(zip((7, 5, 3), held))
    swapped[6] = swap(last)
    b_blocks = [other, swap(join_call(near[1], near[2], near[4]))] + [swapped[m] for m in ORDER[4:]]
    b_blocks = [in_vmem(b) for b in b_blocks]

    e, a_stat, b_stat, flags = scores_call(core_arr, a_blocks, b_blocks, scale)
    a_lse = merge_call(a_stat, swap(b_stat), 0)
    for m in (1, 2, 4):
        a_lse = merge_call(a_lse, to_cube(a_lse, m), m)
    b_lse = swap(a_lse)

    w, gb_hi = weights_call(core_arr, flags, e, a_lse, b_lse, a_blocks)
    got_hi = swap(gb_hi)
    ga_hi, gb0, gb_lo = middle_call(core_arr, w, a_blocks, b_blocks)
    got0, got_lo = swap(gb0), swap(gb_lo)
    p = dict(zip(ORDER[4:], far_call(ga_hi, got_hi)))
    from_xy = to_cube(p[3], 1)
    from_yz = to_cube(p[6], 2)
    from_xz = to_cube(p[5], 4)
    from_xyz = to_cube(p[7], 7)
    ga_lo = last_call(core_arr, w, b_blocks)
    p0, p1, p2, p4 = near_call(ga_lo, got0, got_lo, from_xy, from_yz, from_xz)
    wide = lambda a: a.astype(jnp.float32)
    total = p0 + wide(from_xyz) + wide(to_cube(p1, 1)) + wide(to_cube(p2, 2)) + wide(to_cube(p4, 4))
    kept, sent = total[:rows], total[rows:]
    got_sum = swap(sent)
    image_sum = jnp.where(first, kept, got_sum)
    text_sum = jnp.where(first, got_sum, kept)
    return (image_sum - wide(texts), text_sum - wide(images))


def solution(mesh):
    chips = Mesh(mesh.devices.reshape(SIZES), AXES)
    spec = P(AXES, None)
    return jax.shard_map(
        body,
        mesh=chips,
        in_specs=(spec, spec),
        out_specs=(spec, spec),
        check_vma=False,
    )
```

```python
import functools
import math

import jax
import jax.numpy as jnp
from jax import lax
from jax.experimental import pallas as pl
from jax.experimental.pallas import tpu as pltpu
from jax.sharding import Mesh, PartitionSpec as P

AXES = ("y", "core", "x", "z")
SIZES = (4, 2, 4, 4)
ORDER = (0, 1, 2, 4, 3, 5, 6, 7)
PLACE = tuple(ORDER.index(m) for m in range(8))
LOG2E = 1.4426950408889634
VMEM_LIMIT = 12 * 1024 * 1024
RANGE = 80.0


def flat(y, c, x, z):
    return ((y * 2 + c) * 4 + x) * 4 + z


def coords():
    for y in range(4):
        for c in range(2):
            for x in range(4):
                for z in range(4):
                    yield y, c, x, z


def partner(v, wrapped):
    return 3 - v if wrapped else v ^ 1


def across(m):
    pairs = []
    for y, c, x, z in coords():
        target = (
            partner(y, c == 0) if m & 2 else y,
            c,
            partner(x, c == 1) if m & 1 else x,
            partner(z, c == 1) if m & 4 else z,
        )
        pairs.append((flat(y, c, x, z), flat(*target)))
    return pairs


SWAP = [(flat(y, c, x, z), flat(y, 1 - c, x, z)) for y, c, x, z in coords()]


def to_cube(a, m):
    return lax.ppermute(a, AXES, across(m))


def swap(a):
    return lax.ppermute(a, AXES, SWAP)


def column_of(row, rows):
    padded = -(-rows // 128) * 128
    wide = jnp.broadcast_to(row, (128, rows))
    if padded != rows:
        wide = jnp.concatenate([wide, jnp.zeros((128, padded - rows), jnp.float32)], axis=1)
    return wide.T[:rows, :1]


def row_of(column, rows):
    padded = -(-rows // 128) * 128
    wide = jnp.broadcast_to(column, (rows, 128))
    if padded != rows:
        wide = jnp.concatenate([wide, jnp.zeros((padded - rows, 128), jnp.float32)], axis=0)
    return wide.T[:1, :rows]


def vmem_spec():
    return pl.BlockSpec(memory_space=pltpu.VMEM)


def smem_spec():
    return pl.BlockSpec(memory_space=pltpu.SMEM)


def cost(matmuls, rows, cols, depth, passes=0):
    return pl.CostEstimate(
        flops=2 * matmuls * rows * cols * depth, bytes_accessed=passes * rows * cols, transcendentals=0
    )


def params():
    return pltpu.CompilerParams(vmem_limit_bytes=VMEM_LIMIT)


def dot_nt(a, b):
    return lax.dot_general(a, b, (((1,), (1,)), ((), ())), preferred_element_type=jnp.float32)


def dot_tn(a, b):
    return lax.dot_general(a, b, (((0,), (0,)), ((), ())), preferred_element_type=jnp.float32)


def own_kernel(core_ref, images, texts, got_images, got_texts, own, other, sem):
    rows = images.shape[0]
    core = core_ref[0]
    top, low = pl.ds(0, rows), pl.ds(rows, rows)
    orders = ((images, got_images, got_texts, texts), (texts, got_texts, got_images, images))

    def copies(order):
        places = (own.at[top], own.at[low], other.at[top], other.at[low])
        return [pltpu.make_async_copy(a, p, sem.at[j]) for j, (a, p) in enumerate(zip(order, places))]

    for c in range(2):

        @pl.when(core == c)
        def _():
            for copy in copies(orders[c]):
                copy.start()
            for copy in copies(orders[c]):
                copy.wait()


def own_call(core, *parts):
    rows, features = parts[0].shape
    block = pltpu.VMEM((2 * rows, features), parts[0].dtype)
    return pl.pallas_call(
        own_kernel,
        in_specs=[smem_spec()] + [pl.BlockSpec(memory_space=pl.ANY)] * 4,
        out_specs=[vmem_spec()] * 2,
        out_shape=[block, block],
        scratch_shapes=[pltpu.SemaphoreType.DMA((4,))],
        compiler_params=params(),
        cost_estimate=cost(0, rows, features, 1, 16),
        name="own",
    )(core, *parts)


def join_kernel(b0, b1, b2, out0, out1):
    rows = b0.shape[0]
    cut = rows // 2
    out0[:rows] = b0[...]
    out0[rows:] = b1[:cut]
    out1[:cut] = b1[cut:]
    out1[cut:] = b2[...]


def join_call(*parts):
    rows, features = parts[0].shape
    out = jax.ShapeDtypeStruct((3 * rows // 2, features), parts[0].dtype)
    return pl.pallas_call(
        join_kernel,
        in_specs=[vmem_spec()] * 3,
        out_specs=[vmem_spec()] * 2,
        out_shape=[out, out],
        compiler_params=params(),
        cost_estimate=cost(0, 3 * rows, features, 1, 4),
        name="join",
    )(*parts)


def take_half(core, blocks, shift, out):
    rows = blocks[0].shape[0]
    for c in range(2):

        @pl.when(core == c)
        def _():
            for j in range(4):
                out[j * rows : (j + 1) * rows, :] = blocks[4 * (c ^ shift) + j][...]


def scores_kernel(t, scale, core_ref, *refs):
    a_refs, refs = refs[:8], refs[8:]
    rows = a_refs[0].shape[0]
    if t == 0:
        b_refs, refs = refs[:3], refs[3:]
    else:
        b_refs, a_before, b_before = refs[:4], refs[4], refs[5]
        refs = refs[6:]
    e_ref, a_cat, b_cat, a_stat, b_stat, flag, col_m, col_s = refs
    half = 4 * rows
    core = core_ref[0]
    a_first = 0 if t == 0 else 4 * (1 - core)
    b_first = 4 * t
    if t == 1:
        for j in range(4):
            a_stat[pl.ds(4 * core + j, 1), :] = a_before[j : j + 1, :]
        b_stat[:4, :] = b_before[...]
    take_half(core, a_refs, t, a_cat)
    at = 0
    for b in b_refs:
        b_cat[at : at + b.shape[0], :] = b[...]
        at += b.shape[0]
    b_half = b_cat[...]
    sums = []
    col = None
    for r in range(4):
        sl = slice(r * rows, (r + 1) * rows)
        e = jnp.exp2(dot_nt(a_cat[sl, :], b_half) * scale)
        e_ref[sl, :] = e
        sums.append(jnp.sum(e, axis=1, keepdims=True))
        part = jnp.sum(e, axis=0, keepdims=True)
        col = part if col is None else col + part
    row_lse = jnp.log2(row_of(jnp.concatenate(sums, axis=0), half))
    col_lse = jnp.log2(col)
    for j in range(4):
        sl = slice(j * rows, (j + 1) * rows)
        a_stat[pl.ds(a_first + j, 1), :] = row_lse[:, sl]
        b_stat[b_first + j : b_first + j + 1, :] = col_lse[:, sl]
    reach = jnp.max(jnp.maximum(jnp.abs(row_lse), jnp.abs(col_lse)))
    bad = jnp.logical_not(reach <= RANGE)
    flag[0] = bad.astype(jnp.int32)

    @pl.when(bad)
    def _():
        col_m[...] = jnp.full_like(col_m, -jnp.inf)
        col_s[...] = jnp.zeros_like(col_s)

        @pl.loop(0, 4)
        def _(r):
            sl = pl.ds(pl.multiple_of(r * rows, 16), rows)
            s = dot_nt(a_cat[sl, :], b_cat[...]) * scale
            e_ref[sl, :] = s
            row_m = jnp.max(s, axis=1, keepdims=True)
            row_s = jnp.sum(jnp.exp2(s - row_m), axis=1, keepdims=True)
            a_stat[pl.ds(a_first + r, 1), :] = row_of(row_m + jnp.log2(row_s), rows)
            blk_m = jnp.max(s, axis=0, keepdims=True)
            blk_s = jnp.sum(jnp.exp2(s - blk_m), axis=0, keepdims=True)
            before = col_m[...]
            top = jnp.maximum(before, blk_m)
            col_s[...] = col_s[...] * jnp.exp2(before - top) + blk_s * jnp.exp2(blk_m - top)
            col_m[...] = top

        lse = col_m[...] + jnp.log2(col_s[...])
        for j in range(4):
            b_stat[b_first + j : b_first + j + 1, :] = lse[:, j * rows : (j + 1) * rows]


def scores_call(t, core, a_blocks, b_parts, scale):
    rows, features = a_blocks[0].shape
    half = 4 * rows
    stat = jax.ShapeDtypeStruct((4 * (t + 1), rows), jnp.float32)
    joined = pltpu.VMEM((half, features), jnp.bfloat16)
    return pl.pallas_call(
        functools.partial(scores_kernel, t, scale),
        in_specs=[smem_spec()] + [vmem_spec()] * (8 + len(b_parts)),
        out_specs=[vmem_spec()] * 5 + [smem_spec()],
        out_shape=[
            pltpu.VMEM((half, half), jnp.float32),
            joined,
            joined,
            stat,
            stat,
            jax.ShapeDtypeStruct((1,), jnp.int32),
        ],
        scratch_shapes=[pltpu.VMEM((1, half), jnp.float32), pltpu.VMEM((1, half), jnp.float32)],
        compiler_params=params(),
        cost_estimate=cost(1, half, half, features),
        name="scores",
    )(core, *a_blocks, *b_parts)


def merge_kernel(m, mine_ref, got_ref, out_ref):
    for k in range(8):
        j = PLACE[ORDER[k] ^ m]
        mine, got = mine_ref[k : k + 1, :], got_ref[j : j + 1, :]
        top = jnp.maximum(mine, got)
        out_ref[k : k + 1, :] = top + jnp.log2(jnp.exp2(mine - top) + jnp.exp2(got - top))


def merge_call(mine, got, m):
    return pl.pallas_call(
        functools.partial(merge_kernel, m),
        in_specs=[vmem_spec()] * 2,
        out_specs=vmem_spec(),
        out_shape=jax.ShapeDtypeStruct(mine.shape, jnp.float32),
        compiler_params=pltpu.CompilerParams(vmem_limit_bytes=2 * 1024 * 1024),
        name="merge",
    )(mine, got)


def weights_kernel(core_ref, flag0, flag1, e0, e1, a_lse, b_lse, a_cat1, w0, w1, gb_hi):
    rows = a_lse.shape[1]
    half = 4 * rows
    core = core_ref[0]
    flags, es, ws = (flag0, flag1), (e0, e1), (w0, w1)

    def lse_rows(t):
        a_row = jnp.concatenate([a_lse[pl.ds((core ^ t) * 4 + j, 1), :] for j in range(4)], axis=1)
        b_row = jnp.concatenate([b_lse[4 * t + j : 4 * t + j + 1, :] for j in range(4)], axis=1)
        return a_row, b_row

    def from_exp(t):
        a_row, b_row = lse_rows(t)
        a_col = column_of(jnp.exp2(-a_row), half)
        b_exp = jnp.exp2(-b_row)
        for r in range(4):
            sl = slice(r * rows, (r + 1) * rows)
            ws[t][sl, :] = (es[t][sl, :] * (a_col[sl, :] + b_exp)).astype(jnp.bfloat16)

    def from_scores(t):
        a_row, b_row = lse_rows(t)
        a_col = column_of(a_row, half)
        for r in range(4):
            sl = slice(r * rows, (r + 1) * rows)
            s = es[t][sl, :]
            ws[t][sl, :] = (jnp.exp2(s - a_col[sl, :]) + jnp.exp2(s - b_row)).astype(jnp.bfloat16)

    def product():
        gb_hi[...] = (0.5 * dot_tn(w1[...], a_cat1[...])).astype(jnp.bfloat16)

    calm = flag0[0] + flag1[0] == 0

    @pl.when(calm)
    def _():
        from_exp(1)
        product()
        from_exp(0)

    @pl.when(jnp.logical_not(calm))
    def _():
        for t in range(2):
            pl.when(flags[t][0] == 0)(functools.partial(from_exp, t))
            pl.when(flags[t][0] != 0)(functools.partial(from_scores, t))
        product()


def weights_call(core, flag0, flag1, e0, e1, a_lse, b_lse, a_cat1):
    half, features = a_cat1.shape
    w = pltpu.VMEM((half, half), jnp.bfloat16)
    return pl.pallas_call(
        weights_kernel,
        in_specs=[smem_spec()] * 3 + [vmem_spec()] * 5,
        out_specs=[vmem_spec()] * 3,
        out_shape=[w, w, jax.ShapeDtypeStruct((half, features), jnp.bfloat16)],
        compiler_params=params(),
        cost_estimate=cost(1, half, half, features, 12),
        name="weights",
    )(core, flag0, flag1, e0, e1, a_lse, b_lse, a_cat1)


def half_product(core, w0, w1, b_cat0, b_cat1, shift, out):
    for c in range(2):

        @pl.when(core == c)
        def _():
            w, b = (w0, b_cat0) if c == shift else (w1, b_cat1)
            out[...] = 0.5 * jnp.dot(w[...], b[...], preferred_element_type=jnp.float32)


def middle_kernel(core_ref, w0, w1, a_cat0, b_cat0, b_cat1, ga_hi, gb0, gb_lo):
    rows = gb0.shape[0]
    g = 0.5 * dot_tn(w0[...], a_cat0[...])
    gb0[...] = g[:rows]
    gb_lo[...] = g[rows:].astype(jnp.bfloat16)
    half_product(core_ref[0], w0, w1, b_cat0, b_cat1, 1, ga_hi)


def middle_call(core, w0, w1, a_cat0, b_cat0, b_cat1):
    half, features = a_cat0.shape
    rows = half // 4
    return pl.pallas_call(
        middle_kernel,
        in_specs=[smem_spec()] + [vmem_spec()] * 5,
        out_specs=[vmem_spec()] * 3,
        out_shape=[
            pltpu.VMEM((half, features), jnp.float32),
            jax.ShapeDtypeStruct((rows, features), jnp.float32),
            jax.ShapeDtypeStruct((half - rows, features), jnp.bfloat16),
        ],
        compiler_params=params(),
        cost_estimate=cost(2, half, half, features),
        name="middle",
    )(core, w0, w1, a_cat0, b_cat0, b_cat1)


def far_kernel(ga_hi, got, *outs):
    rows = outs[0].shape[0]
    for j in range(4):
        sl = slice(j * rows, (j + 1) * rows)
        outs[j][...] = (ga_hi[sl, :] + got[sl, :].astype(jnp.float32)).astype(jnp.bfloat16)


def far_call(ga_hi, got):
    half, features = ga_hi.shape
    rows = half // 4
    return pl.pallas_call(
        far_kernel,
        in_specs=[vmem_spec()] * 2,
        out_specs=[vmem_spec()] * 4,
        out_shape=[jax.ShapeDtypeStruct((rows, features), jnp.bfloat16)] * 4,
        compiler_params=params(),
        cost_estimate=cost(0, half, features, 1, 8),
        name="far",
    )(ga_hi, got)


def last_kernel(core_ref, w0, w1, b_cat0, b_cat1, ga_lo):
    half_product(core_ref[0], w0, w1, b_cat0, b_cat1, 0, ga_lo)


def last_call(core, w0, w1, b_cat0, b_cat1):
    half, features = b_cat0.shape
    return pl.pallas_call(
        last_kernel,
        in_specs=[smem_spec()] + [vmem_spec()] * 4,
        out_specs=vmem_spec(),
        out_shape=pltpu.VMEM((half, features), jnp.float32),
        compiler_params=params(),
        cost_estimate=cost(1, half, half, features),
        name="last",
    )(core, w0, w1, b_cat0, b_cat1)


def near_kernel(ga_lo, got0, got_lo, r_xy, r_yz, r_xz, p0, p1, p2, p4):
    rows = p0.shape[0]
    wide = lambda ref: ref[...].astype(jnp.float32)
    p0[...] = ga_lo[:rows] + got0[...]
    part = lambda j: ga_lo[j * rows : (j + 1) * rows, :] + got_lo[(j - 1) * rows : j * rows, :].astype(jnp.float32)
    p1[...] = (part(1) + wide(r_xz)).astype(jnp.bfloat16)
    p2[...] = (part(2) + wide(r_xy)).astype(jnp.bfloat16)
    p4[...] = (part(3) + wide(r_yz)).astype(jnp.bfloat16)


def near_call(ga_lo, got0, got_lo, *received):
    rows, features = got0.shape
    narrow = jax.ShapeDtypeStruct((rows, features), jnp.bfloat16)
    return pl.pallas_call(
        near_kernel,
        in_specs=[vmem_spec()] * 6,
        out_specs=[vmem_spec()] * 4,
        out_shape=[pltpu.VMEM((rows, features), jnp.float32)] + [narrow] * 3,
        compiler_params=params(),
        cost_estimate=cost(0, 4 * rows, features, 1, 12),
        name="near",
    )(ga_lo, got0, got_lo, *received)


def body(images, texts):
    rows, features = images.shape
    scale = 4.0 / math.sqrt(features) * LOG2E
    core = lax.axis_index("core")
    first = core == 0
    core_arr = core.astype(jnp.int32).reshape(1)
    in_hbm = lambda a: pltpu.with_memory_space_constraint(a, pltpu.HBM)
    own, other = own_call(core_arr, in_hbm(images), in_hbm(texts), swap(images), swap(texts))
    near = {m: to_cube(own, m) for m in (4, 2, 1)}
    far = {7: to_cube(own, 7), 5: to_cube(near[1], 4), 3: to_cube(near[2], 1), 6: to_cube(near[4], 2)}
    blocks = {0: own, **near, **far}
    in_vmem = lambda a: pltpu.with_memory_space_constraint(a, pltpu.VMEM)
    a_blocks = [in_vmem(blocks[m]) for m in ORDER]
    swapped = {m: swap(far[m]) for m in (7, 5, 3)}
    last, *held = lax.optimization_barrier((far[6], swapped[7], swapped[5], swapped[3]))
    swapped.update(zip((7, 5, 3), held))
    swapped[6] = swap(last)
    b_lo = [in_vmem(other)] + [in_vmem(swap(a)) for a in join_call(near[1], near[2], near[4])]
    b_hi = [in_vmem(swapped[m]) for m in ORDER[4:]]

    e0, a_cat0, b_cat0, a_part, b_part, flag0 = scores_call(0, core_arr, a_blocks, b_lo, scale)
    e1, a_cat1, b_cat1, a_stat, b_stat, flag1 = scores_call(1, core_arr, a_blocks, b_hi + [a_part, b_part], scale)
    a_lse = merge_call(a_stat, swap(b_stat), 0)
    for m in (1, 2, 4):
        a_lse = merge_call(a_lse, to_cube(a_lse, m), m)
    b_lse = swap(a_lse)

    w0, w1, gb_hi = weights_call(core_arr, flag0, flag1, e0, e1, a_lse, b_lse, a_cat1)
    got_hi = swap(gb_hi)
    ga_hi, gb0, gb_lo = middle_call(core_arr, w0, w1, a_cat0, b_cat0, b_cat1)
    got0, got_lo = swap(gb0), swap(gb_lo)
    p = dict(zip(ORDER[4:], far_call(ga_hi, got_hi)))
    from_xy = to_cube(p[3], 1)
    from_yz = to_cube(p[6], 2)
    from_xz = to_cube(p[5], 4)
    from_xyz = to_cube(p[7], 7)
    ga_lo = last_call(core_arr, w0, w1, b_cat0, b_cat1)
    p0, p1, p2, p4 = near_call(ga_lo, got0, got_lo, from_xy, from_yz, from_xz)
    wide = lambda a: a.astype(jnp.float32)
    total = p0 + wide(from_xyz) + wide(to_cube(p1, 1)) + wide(to_cube(p2, 2)) + wide(to_cube(p4, 4))
    kept, sent = total[:rows], total[rows:]
    got_sum = swap(sent)
    image_sum = jnp.where(first, kept, got_sum)
    text_sum = jnp.where(first, got_sum, kept)
    return (image_sum - wide(texts), text_sum - wide(images))


def solution(mesh):
    chips = Mesh(mesh.devices.reshape(SIZES), AXES)
    spec = P(AXES, None)
    return jax.shard_map(
        body,
        mesh=chips,
        in_specs=(spec, spec),
        out_specs=(spec, spec),
        check_vma=False,
    )
```

```python
import functools
import math

import jax
import jax.numpy as jnp
from jax import lax
from jax.experimental import pallas as pl
from jax.experimental.pallas import tpu as pltpu
from jax.sharding import Mesh, PartitionSpec as P

AXES = ("y", "core", "x", "z")
SIZES = (4, 2, 4, 4)
ORDER = (0, 1, 2, 4, 3, 5, 6, 7)
PLACE = tuple(ORDER.index(m) for m in range(8))
LOG2E = 1.4426950408889634
VMEM_LIMIT = 12 * 1024 * 1024
RANGE = 80.0


def flat(y, c, x, z):
    return ((y * 2 + c) * 4 + x) * 4 + z


def coords():
    for y in range(4):
        for c in range(2):
            for x in range(4):
                for z in range(4):
                    yield y, c, x, z


def partner(v, wrapped):
    return 3 - v if wrapped else v ^ 1


def across(m):
    pairs = []
    for y, c, x, z in coords():
        target = (
            partner(y, c == 0) if m & 2 else y,
            c,
            partner(x, c == 1) if m & 1 else x,
            partner(z, c == 1) if m & 4 else z,
        )
        pairs.append((flat(y, c, x, z), flat(*target)))
    return pairs


SWAP = [(flat(y, c, x, z), flat(y, 1 - c, x, z)) for y, c, x, z in coords()]


def to_cube(a, m):
    return lax.ppermute(a, AXES, across(m))


def swap(a):
    return lax.ppermute(a, AXES, SWAP)


def column_of(row, rows):
    padded = -(-rows // 128) * 128
    wide = jnp.broadcast_to(row, (128, rows))
    if padded != rows:
        wide = jnp.concatenate([wide, jnp.zeros((128, padded - rows), jnp.float32)], axis=1)
    return wide.T[:rows, :1]


def row_of(column, rows):
    padded = -(-rows // 128) * 128
    wide = jnp.broadcast_to(column, (rows, 128))
    if padded != rows:
        wide = jnp.concatenate([wide, jnp.zeros((padded - rows, 128), jnp.float32)], axis=0)
    return wide.T[:1, :rows]


def vmem_spec():
    return pl.BlockSpec(memory_space=pltpu.VMEM)


def smem_spec():
    return pl.BlockSpec(memory_space=pltpu.SMEM)


def cost(matmuls, rows, cols, depth, passes=0):
    return pl.CostEstimate(
        flops=2 * matmuls * rows * cols * depth, bytes_accessed=passes * rows * cols, transcendentals=0
    )


def params():
    return pltpu.CompilerParams(vmem_limit_bytes=VMEM_LIMIT)


def dot_nt(a, b):
    return lax.dot_general(a, b, (((1,), (1,)), ((), ())), preferred_element_type=jnp.float32)


def dot_tn(a, b):
    return lax.dot_general(a, b, (((0,), (0,)), ((), ())), preferred_element_type=jnp.float32)


def own_kernel(core_ref, images, texts, got_images, got_texts, own, other, sem):
    rows = images.shape[0]
    core = core_ref[0]
    top, low = pl.ds(0, rows), pl.ds(rows, rows)
    orders = ((images, got_images, got_texts, texts), (texts, got_texts, got_images, images))

    def copies(order):
        places = (own.at[top], own.at[low], other.at[top], other.at[low])
        return [pltpu.make_async_copy(a, p, sem.at[j]) for j, (a, p) in enumerate(zip(order, places))]

    for c in range(2):

        @pl.when(core == c)
        def _():
            for copy in copies(orders[c]):
                copy.start()
            for copy in copies(orders[c]):
                copy.wait()


def own_call(core, *parts):
    rows, features = parts[0].shape
    block = pltpu.VMEM((2 * rows, features), parts[0].dtype)
    return pl.pallas_call(
        own_kernel,
        in_specs=[smem_spec()] + [pl.BlockSpec(memory_space=pl.ANY)] * 4,
        out_specs=[vmem_spec()] * 2,
        out_shape=[block, block],
        scratch_shapes=[pltpu.SemaphoreType.DMA((4,))],
        compiler_params=params(),
        cost_estimate=cost(0, rows, features, 1, 16),
        name="own",
    )(core, *parts)


def join_kernel(b0, b1, b2, out0, out1):
    rows = b0.shape[0]
    cut = rows // 2
    out0[:rows] = b0[...]
    out0[rows:] = b1[:cut]
    out1[:cut] = b1[cut:]
    out1[cut:] = b2[...]


def join_call(*parts):
    rows, features = parts[0].shape
    out = jax.ShapeDtypeStruct((3 * rows // 2, features), parts[0].dtype)
    return pl.pallas_call(
        join_kernel,
        in_specs=[vmem_spec()] * 3,
        out_specs=[vmem_spec()] * 2,
        out_shape=[out, out],
        compiler_params=params(),
        cost_estimate=cost(0, 3 * rows, features, 1, 4),
        name="join",
    )(*parts)


def take_half(core, blocks, shift, out):
    rows = blocks[0].shape[0]
    for c in range(2):

        @pl.when(core == c)
        def _():
            for j in range(4):
                out[j * rows : (j + 1) * rows, :] = blocks[4 * (c ^ shift) + j][...]


def scores_kernel(t, scale, core_ref, *refs):
    a_refs, refs = refs[:8], refs[8:]
    rows = a_refs[0].shape[0]
    if t == 0:
        b_refs, refs = refs[:3], refs[3:]
    else:
        b_refs, a_before, b_before = refs[:4], refs[4], refs[5]
        refs = refs[6:]
    e_ref, a_cat, b_cat, a_stat, b_stat, flag, col_m, col_s = refs
    half = 4 * rows
    core = core_ref[0]
    a_first = 0 if t == 0 else 4 * (1 - core)
    b_first = 4 * t
    if t == 1:
        for j in range(4):
            a_stat[pl.ds(4 * core + j, 1), :] = a_before[j : j + 1, :]
        b_stat[:4, :] = b_before[...]
    take_half(core, a_refs, t, a_cat)
    at = 0
    for b in b_refs:
        b_cat[at : at + b.shape[0], :] = b[...]
        at += b.shape[0]
    b_half = b_cat[...]
    sums = []
    col = None
    for r in range(4):
        sl = slice(r * rows, (r + 1) * rows)
        e = jnp.exp2(dot_nt(a_cat[sl, :], b_half) * scale)
        e_ref[sl, :] = e
        sums.append(jnp.sum(e, axis=1, keepdims=True))
        part = jnp.sum(e, axis=0, keepdims=True)
        col = part if col is None else col + part
    row_lse = jnp.log2(row_of(jnp.concatenate(sums, axis=0), half))
    col_lse = jnp.log2(col)
    for j in range(4):
        sl = slice(j * rows, (j + 1) * rows)
        a_stat[pl.ds(a_first + j, 1), :] = row_lse[:, sl]
        b_stat[b_first + j : b_first + j + 1, :] = col_lse[:, sl]
    reach = jnp.max(jnp.maximum(jnp.abs(row_lse), jnp.abs(col_lse)))
    bad = jnp.logical_not(reach <= RANGE)
    flag[0] = bad.astype(jnp.int32)

    @pl.when(bad)
    def _():
        col_m[...] = jnp.full_like(col_m, -jnp.inf)
        col_s[...] = jnp.zeros_like(col_s)

        @pl.loop(0, 4)
        def _(r):
            sl = pl.ds(pl.multiple_of(r * rows, 16), rows)
            s = dot_nt(a_cat[sl, :], b_cat[...]) * scale
            e_ref[sl, :] = s
            row_m = jnp.max(s, axis=1, keepdims=True)
            row_s = jnp.sum(jnp.exp2(s - row_m), axis=1, keepdims=True)
            a_stat[pl.ds(a_first + r, 1), :] = row_of(row_m + jnp.log2(row_s), rows)
            blk_m = jnp.max(s, axis=0, keepdims=True)
            blk_s = jnp.sum(jnp.exp2(s - blk_m), axis=0, keepdims=True)
            before = col_m[...]
            top = jnp.maximum(before, blk_m)
            col_s[...] = col_s[...] * jnp.exp2(before - top) + blk_s * jnp.exp2(blk_m - top)
            col_m[...] = top

        lse = col_m[...] + jnp.log2(col_s[...])
        for j in range(4):
            b_stat[b_first + j : b_first + j + 1, :] = lse[:, j * rows : (j + 1) * rows]


def scores_call(t, core, a_blocks, b_parts, scale):
    rows, features = a_blocks[0].shape
    half = 4 * rows
    stat = jax.ShapeDtypeStruct((4 * (t + 1), rows), jnp.float32)
    joined = pltpu.VMEM((half, features), jnp.bfloat16)
    return pl.pallas_call(
        functools.partial(scores_kernel, t, scale),
        in_specs=[smem_spec()] + [vmem_spec()] * (8 + len(b_parts)),
        out_specs=[vmem_spec()] * 5 + [smem_spec()],
        out_shape=[
            pltpu.VMEM((half, half), jnp.float32),
            joined,
            joined,
            stat,
            stat,
            jax.ShapeDtypeStruct((1,), jnp.int32),
        ],
        scratch_shapes=[pltpu.VMEM((1, half), jnp.float32), pltpu.VMEM((1, half), jnp.float32)],
        compiler_params=params(),
        cost_estimate=cost(1, half, half, features),
        name="scores",
    )(core, *a_blocks, *b_parts)


def merge_kernel(m, mine_ref, got_ref, out_ref):
    for k in range(8):
        j = PLACE[ORDER[k] ^ m]
        mine, got = mine_ref[k : k + 1, :], got_ref[j : j + 1, :]
        top = jnp.maximum(mine, got)
        out_ref[k : k + 1, :] = top + jnp.log2(jnp.exp2(mine - top) + jnp.exp2(got - top))


def merge_call(mine, got, m):
    return pl.pallas_call(
        functools.partial(merge_kernel, m),
        in_specs=[vmem_spec()] * 2,
        out_specs=vmem_spec(),
        out_shape=jax.ShapeDtypeStruct(mine.shape, jnp.float32),
        compiler_params=pltpu.CompilerParams(vmem_limit_bytes=2 * 1024 * 1024),
        name="merge",
    )(mine, got)


def weights_kernel(core_ref, flag0, flag1, e0, e1, a_lse, b_lse, a_cat1, w_ref, gb_hi):
    rows = a_lse.shape[1]
    half = 4 * rows
    core = core_ref[0]
    flags, es = (flag0, flag1), (e0, e1)

    def lse_rows(t):
        a_row = jnp.concatenate([a_lse[pl.ds((core ^ t) * 4 + j, 1), :] for j in range(4)], axis=1)
        b_row = jnp.concatenate([b_lse[4 * t + j : 4 * t + j + 1, :] for j in range(4)], axis=1)
        return a_row, b_row

    def from_exp(t):
        a_row, b_row = lse_rows(t)
        a_col = column_of(jnp.exp2(-a_row), half)
        b_exp = jnp.exp2(-b_row)
        for r in range(4):
            sl = slice(r * rows, (r + 1) * rows)
            w_ref[t, sl, :] = (es[t][sl, :] * (a_col[sl, :] + b_exp)).astype(jnp.bfloat16)

    def from_scores(t):
        a_row, b_row = lse_rows(t)
        a_col = column_of(a_row, half)
        for r in range(4):
            sl = slice(r * rows, (r + 1) * rows)
            s = es[t][sl, :]
            w_ref[t, sl, :] = (jnp.exp2(s - a_col[sl, :]) + jnp.exp2(s - b_row)).astype(jnp.bfloat16)

    for t in range(2):
        pl.when(flags[t][0] == 0)(functools.partial(from_exp, t))
        pl.when(flags[t][0] != 0)(functools.partial(from_scores, t))
    gb_hi[...] = (0.5 * dot_tn(w_ref[1], a_cat1[...])).astype(jnp.bfloat16)


def weights_call(core, flag0, flag1, e0, e1, a_lse, b_lse, a_cat1):
    half, features = a_cat1.shape
    return pl.pallas_call(
        weights_kernel,
        in_specs=[smem_spec()] * 3 + [vmem_spec()] * 5,
        out_specs=[vmem_spec()] * 2,
        out_shape=[pltpu.VMEM((2, half, half), jnp.bfloat16), jax.ShapeDtypeStruct((half, features), jnp.bfloat16)],
        compiler_params=params(),
        cost_estimate=cost(1, half, half, features, 12),
        name="weights",
    )(core, flag0, flag1, e0, e1, a_lse, b_lse, a_cat1)


def half_product(core, w_ref, b_cat0, b_cat1, shift, b_half):
    pl.when(core == shift)(lambda: b_half.__setitem__(Ellipsis, b_cat0[...]))
    pl.when(core != shift)(lambda: b_half.__setitem__(Ellipsis, b_cat1[...]))
    return 0.5 * jnp.dot(w_ref[core ^ shift], b_half[...], preferred_element_type=jnp.float32)


def middle_kernel(core_ref, w_ref, a_cat0, b_cat0, b_cat1, ga_hi, gb0, gb_lo, b_half):
    rows = gb0.shape[0]
    g = 0.5 * dot_tn(w_ref[0], a_cat0[...])
    gb0[...] = g[:rows]
    gb_lo[...] = g[rows:].astype(jnp.bfloat16)
    ga_hi[...] = half_product(core_ref[0], w_ref, b_cat0, b_cat1, 1, b_half)


def middle_call(core, w, a_cat0, b_cat0, b_cat1):
    half, features = a_cat0.shape
    rows = half // 4
    return pl.pallas_call(
        middle_kernel,
        in_specs=[smem_spec()] + [vmem_spec()] * 4,
        out_specs=[vmem_spec()] * 3,
        out_shape=[
            pltpu.VMEM((half, features), jnp.float32),
            jax.ShapeDtypeStruct((rows, features), jnp.float32),
            jax.ShapeDtypeStruct((half - rows, features), jnp.bfloat16),
        ],
        scratch_shapes=[pltpu.VMEM((half, features), jnp.bfloat16)],
        compiler_params=params(),
        cost_estimate=cost(2, half, half, features),
        name="middle",
    )(core, w, a_cat0, b_cat0, b_cat1)


def far_kernel(ga_hi, got, *outs):
    rows = outs[0].shape[0]
    for j in range(4):
        sl = slice(j * rows, (j + 1) * rows)
        outs[j][...] = (ga_hi[sl, :] + got[sl, :].astype(jnp.float32)).astype(jnp.bfloat16)


def far_call(ga_hi, got):
    half, features = ga_hi.shape
    rows = half // 4
    return pl.pallas_call(
        far_kernel,
        in_specs=[vmem_spec()] * 2,
        out_specs=[vmem_spec()] * 4,
        out_shape=[jax.ShapeDtypeStruct((rows, features), jnp.bfloat16)] * 4,
        compiler_params=params(),
        cost_estimate=cost(0, half, features, 1, 8),
        name="far",
    )(ga_hi, got)


def last_kernel(core_ref, w_ref, b_cat0, b_cat1, ga_lo, b_half):
    ga_lo[...] = half_product(core_ref[0], w_ref, b_cat0, b_cat1, 0, b_half)


def last_call(core, w, b_cat0, b_cat1):
    half, features = b_cat0.shape
    return pl.pallas_call(
        last_kernel,
        in_specs=[smem_spec()] + [vmem_spec()] * 3,
        out_specs=vmem_spec(),
        out_shape=pltpu.VMEM((half, features), jnp.float32),
        scratch_shapes=[pltpu.VMEM((half, features), jnp.bfloat16)],
        compiler_params=params(),
        cost_estimate=cost(1, half, half, features),
        name="last",
    )(core, w, b_cat0, b_cat1)


def near_kernel(ga_lo, got0, got_lo, r_xy, r_yz, r_xz, p0, p1, p2, p4):
    rows = p0.shape[0]
    wide = lambda ref: ref[...].astype(jnp.float32)
    p0[...] = ga_lo[:rows] + got0[...]
    part = lambda j: ga_lo[j * rows : (j + 1) * rows, :] + got_lo[(j - 1) * rows : j * rows, :].astype(jnp.float32)
    p1[...] = (part(1) + wide(r_xz)).astype(jnp.bfloat16)
    p2[...] = (part(2) + wide(r_xy)).astype(jnp.bfloat16)
    p4[...] = (part(3) + wide(r_yz)).astype(jnp.bfloat16)


def near_call(ga_lo, got0, got_lo, *received):
    rows, features = got0.shape
    narrow = jax.ShapeDtypeStruct((rows, features), jnp.bfloat16)
    return pl.pallas_call(
        near_kernel,
        in_specs=[vmem_spec()] * 6,
        out_specs=[vmem_spec()] * 4,
        out_shape=[pltpu.VMEM((rows, features), jnp.float32)] + [narrow] * 3,
        compiler_params=params(),
        cost_estimate=cost(0, 4 * rows, features, 1, 12),
        name="near",
    )(ga_lo, got0, got_lo, *received)


def body(images, texts):
    rows, features = images.shape
    scale = 4.0 / math.sqrt(features) * LOG2E
    core = lax.axis_index("core")
    first = core == 0
    core_arr = core.astype(jnp.int32).reshape(1)
    in_hbm = lambda a: pltpu.with_memory_space_constraint(a, pltpu.HBM)
    own, other = own_call(core_arr, in_hbm(images), in_hbm(texts), swap(images), swap(texts))
    near = {m: to_cube(own, m) for m in (4, 2, 1)}
    far = {7: to_cube(own, 7), 5: to_cube(near[1], 4), 3: to_cube(near[2], 1), 6: to_cube(near[4], 2)}
    blocks = {0: own, **near, **far}
    in_vmem = lambda a: pltpu.with_memory_space_constraint(a, pltpu.VMEM)
    a_blocks = [in_vmem(blocks[m]) for m in ORDER]
    swapped = {m: swap(far[m]) for m in (7, 5, 3)}
    joined = [swap(a) for a in join_call(near[1], near[2], near[4])]
    last, *held = lax.optimization_barrier((far[6], swapped[7], swapped[5], swapped[3], *joined))
    swapped.update(zip((7, 5, 3), held))
    swapped[6] = swap(last)
    b_lo = [in_vmem(b) for b in [other] + held[3:]]
    b_hi = [in_vmem(swapped[m]) for m in ORDER[4:]]

    e0, a_cat0, b_cat0, a_part, b_part, flag0 = scores_call(0, core_arr, a_blocks, b_lo, scale)
    e1, a_cat1, b_cat1, a_stat, b_stat, flag1 = scores_call(1, core_arr, a_blocks, b_hi + [a_part, b_part], scale)
    a_lse = merge_call(a_stat, swap(b_stat), 0)
    for m in (1, 2, 4):
        a_lse = merge_call(a_lse, to_cube(a_lse, m), m)
    b_lse = swap(a_lse)

    w, gb_hi = weights_call(core_arr, flag0, flag1, e0, e1, a_lse, b_lse, a_cat1)
    got_hi = swap(gb_hi)
    ga_hi, gb0, gb_lo = middle_call(core_arr, w, a_cat0, b_cat0, b_cat1)
    got0, got_lo = swap(gb0), swap(gb_lo)
    p = dict(zip(ORDER[4:], far_call(ga_hi, got_hi)))
    from_xy = to_cube(p[3], 1)
    from_yz = to_cube(p[6], 2)
    from_xz = to_cube(p[5], 4)
    from_xyz = to_cube(p[7], 7)
    ga_lo = last_call(core_arr, w, b_cat0, b_cat1)
    p0, p1, p2, p4 = near_call(ga_lo, got0, got_lo, from_xy, from_yz, from_xz)
    wide = lambda a: a.astype(jnp.float32)
    total = p0 + wide(from_xyz) + wide(to_cube(p1, 1)) + wide(to_cube(p2, 2)) + wide(to_cube(p4, 4))
    kept, sent = total[:rows], total[rows:]
    got_sum = swap(sent)
    image_sum = jnp.where(first, kept, got_sum)
    text_sum = jnp.where(first, got_sum, kept)
    return (image_sum - wide(texts), text_sum - wide(images))


def solution(mesh):
    chips = Mesh(mesh.devices.reshape(SIZES), AXES)
    spec = P(AXES, None)
    return jax.shard_map(
        body,
        mesh=chips,
        in_specs=(spec, spec),
        out_specs=(spec, spec),
        check_vma=False,
    )
```

```python
import functools
import math

import jax
import jax.numpy as jnp
from jax import lax
from jax.experimental import pallas as pl
from jax.experimental.pallas import tpu as pltpu
from jax.sharding import Mesh, PartitionSpec as P

AXES = ("y", "core", "x", "z")
SIZES = (4, 2, 4, 4)
ORDER = (0, 1, 2, 4, 3, 5, 6, 7)
PLACE = tuple(ORDER.index(m) for m in range(8))
LOG2E = 1.4426950408889634
VMEM_LIMIT = 12 * 1024 * 1024
RANGE = 80.0


def flat(y, c, x, z):
    return ((y * 2 + c) * 4 + x) * 4 + z


def coords():
    for y in range(4):
        for c in range(2):
            for x in range(4):
                for z in range(4):
                    yield y, c, x, z


def partner(v, wrapped):
    return 3 - v if wrapped else v ^ 1


def across(m):
    pairs = []
    for y, c, x, z in coords():
        target = (
            partner(y, c == 0) if m & 2 else y,
            c,
            partner(x, c == 1) if m & 1 else x,
            partner(z, c == 1) if m & 4 else z,
        )
        pairs.append((flat(y, c, x, z), flat(*target)))
    return pairs


SWAP = [(flat(y, c, x, z), flat(y, 1 - c, x, z)) for y, c, x, z in coords()]


def to_cube(a, m):
    return lax.ppermute(a, AXES, across(m))


def swap(a):
    return lax.ppermute(a, AXES, SWAP)


def column_of(row, rows):
    padded = -(-rows // 128) * 128
    wide = jnp.broadcast_to(row, (128, rows))
    if padded != rows:
        wide = jnp.concatenate([wide, jnp.zeros((128, padded - rows), jnp.float32)], axis=1)
    return wide.T[:rows, :1]


def row_of(column, rows):
    padded = -(-rows // 128) * 128
    wide = jnp.broadcast_to(column, (rows, 128))
    if padded != rows:
        wide = jnp.concatenate([wide, jnp.zeros((padded - rows, 128), jnp.float32)], axis=0)
    return wide.T[:1, :rows]


def vmem_spec():
    return pl.BlockSpec(memory_space=pltpu.VMEM)


def smem_spec():
    return pl.BlockSpec(memory_space=pltpu.SMEM)


def cost(matmuls, rows, cols, depth, passes=0):
    return pl.CostEstimate(
        flops=2 * matmuls * rows * cols * depth, bytes_accessed=passes * rows * cols, transcendentals=0
    )


def params():
    return pltpu.CompilerParams(vmem_limit_bytes=VMEM_LIMIT)


def dot_nt(a, b):
    return lax.dot_general(a, b, (((1,), (1,)), ((), ())), preferred_element_type=jnp.float32)


def dot_tn(a, b):
    return lax.dot_general(a, b, (((0,), (0,)), ((), ())), preferred_element_type=jnp.float32)


def load_kernel(core_ref, images, texts, mine, yours, sem):
    core = core_ref[0]
    for c, order in enumerate(((mine, yours), (yours, mine))):

        @pl.when(core == c)
        def _():
            copies = [pltpu.make_async_copy(a, o, sem.at[j]) for j, (a, o) in enumerate(zip((images, texts), order))]
            for copy in copies:
                copy.start()
            for copy in copies:
                copy.wait()


def load_call(core, images, texts):
    block = pltpu.VMEM(images.shape, images.dtype)
    return pl.pallas_call(
        load_kernel,
        in_specs=[smem_spec()] + [pl.BlockSpec(memory_space=pl.ANY)] * 2,
        out_specs=[vmem_spec()] * 2,
        out_shape=[block, block],
        scratch_shapes=[pltpu.SemaphoreType.DMA((2,))],
        compiler_params=params(),
        cost_estimate=cost(0, images.shape[0], images.shape[1], 1, 32),
        name="load",
    )(core, images, texts)


def own_kernel(core_ref, mine, yours, got_images, got_texts, own, other):
    rows = mine.shape[0]
    own[:rows] = mine[...]
    other[rows:] = yours[...]
    for c, (low, top) in enumerate(((got_images, got_texts), (got_texts, got_images))):

        @pl.when(core_ref[0] == c)
        def _():
            own[rows:] = low[...]
            other[:rows] = top[...]


def own_call(core, *parts):
    rows, features = parts[0].shape
    block = pltpu.VMEM((2 * rows, features), parts[0].dtype)
    return pl.pallas_call(
        own_kernel,
        in_specs=[smem_spec()] + [vmem_spec()] * 4,
        out_specs=[vmem_spec()] * 2,
        out_shape=[block, block],
        compiler_params=params(),
        cost_estimate=cost(0, rows, features, 1, 16),
        name="own",
    )(core, *parts)


def join_kernel(b0, b1, b2, out0, out1):
    rows = b0.shape[0]
    cut = rows // 2
    out0[:rows] = b0[...]
    out0[rows:] = b1[:cut]
    out1[:cut] = b1[cut:]
    out1[cut:] = b2[...]


def join_call(*parts):
    rows, features = parts[0].shape
    out = jax.ShapeDtypeStruct((3 * rows // 2, features), parts[0].dtype)
    return pl.pallas_call(
        join_kernel,
        in_specs=[vmem_spec()] * 3,
        out_specs=[vmem_spec()] * 2,
        out_shape=[out, out],
        compiler_params=params(),
        cost_estimate=cost(0, 3 * rows, features, 1, 4),
        name="join",
    )(*parts)


def take_half(core, halves, shift, out):
    for c in range(2):

        @pl.when(core == c)
        def _():
            at = 0
            for part in halves[c ^ shift]:
                out[at : at + part.shape[0], :] = part[...]
                at += part.shape[0]


def a_halves(refs):
    return refs[:4], refs[4:8]


def b_halves(refs):
    return refs[:3], refs[3:7]


def scores_kernel(scale, core_ref, *refs):
    a_refs, b_refs = refs[:8], b_halves(refs[8:15])
    e_ref, a_stat, b_stat, flags, a_cat, b_cat, col_m, col_s = refs[15:]
    rows = a_refs[0].shape[0]
    half = 4 * rows
    core = core_ref[0]
    for q in range(2):
        take_half(core, b_refs, q, b_cat.at[q])

    def quadrant(q):
        b_half = b_cat[q]
        sums = []
        col = None
        for r in range(4):
            sl = slice(r * rows, (r + 1) * rows)
            e = jnp.exp2(dot_nt(a_refs[4 * q + r][...], b_half) * scale)
            e_ref[q, sl, :] = e
            sums.append(jnp.sum(e, axis=1, keepdims=True))
            part = jnp.sum(e, axis=0, keepdims=True)
            col = part if col is None else col + part
        row_lse = jnp.log2(row_of(jnp.concatenate(sums, axis=0), half))
        col_lse = jnp.log2(col)
        for j in range(4):
            sl = slice(j * rows, (j + 1) * rows)
            a_stat[4 * q + j : 4 * q + j + 1, :] = row_lse[:, sl]
            b_stat[pl.ds((q ^ core) * 4 + j, 1), :] = col_lse[:, sl]
        return jnp.maximum(jnp.abs(row_lse), jnp.abs(col_lse))

    def by_maxima(q):
        for r in range(4):
            a_cat[r * rows : (r + 1) * rows, :] = a_refs[4 * q + r][...]
        col_m[...] = jnp.full_like(col_m, -jnp.inf)
        col_s[...] = jnp.zeros_like(col_s)

        @pl.loop(0, 4)
        def _(r):
            sl = pl.ds(pl.multiple_of(r * rows, 16), rows)
            s = dot_nt(a_cat[sl, :], b_cat[q]) * scale
            e_ref[q, sl, :] = s
            row_m = jnp.max(s, axis=1, keepdims=True)
            row_s = jnp.sum(jnp.exp2(s - row_m), axis=1, keepdims=True)
            a_stat[pl.ds(4 * q + r, 1), :] = row_of(row_m + jnp.log2(row_s), rows)
            blk_m = jnp.max(s, axis=0, keepdims=True)
            blk_s = jnp.sum(jnp.exp2(s - blk_m), axis=0, keepdims=True)
            before = col_m[...]
            top = jnp.maximum(before, blk_m)
            col_s[...] = col_s[...] * jnp.exp2(before - top) + blk_s * jnp.exp2(blk_m - top)
            col_m[...] = top

        lse = col_m[...] + jnp.log2(col_s[...])
        for j in range(4):
            b_stat[pl.ds((q ^ core) * 4 + j, 1), :] = lse[:, j * rows : (j + 1) * rows]

    bad = jnp.logical_not(jnp.max(jnp.maximum(quadrant(0), quadrant(1))) <= RANGE)
    flags[0] = bad.astype(jnp.int32)

    @pl.when(bad)
    def _():
        by_maxima(0)
        by_maxima(1)


def scores_call(core, a_blocks, b_blocks, scale):
    rows, features = a_blocks[0].shape
    half = 4 * rows
    stat = jax.ShapeDtypeStruct((8, rows), jnp.float32)
    return pl.pallas_call(
        functools.partial(scores_kernel, scale),
        in_specs=[smem_spec()] + [vmem_spec()] * 15,
        out_specs=[vmem_spec()] * 3 + [smem_spec()],
        out_shape=[
            pltpu.VMEM((2, half, half), jnp.float32),
            stat,
            stat,
            jax.ShapeDtypeStruct((1,), jnp.int32),
        ],
        scratch_shapes=[
            pltpu.VMEM((half, features), jnp.bfloat16),
            pltpu.VMEM((2, half, features), jnp.bfloat16),
            pltpu.VMEM((1, half), jnp.float32),
            pltpu.VMEM((1, half), jnp.float32),
        ],
        compiler_params=params(),
        cost_estimate=cost(2, half, half, features),
        name="scores",
    )(core, *a_blocks, *b_blocks)


def merge_kernel(m, mine_ref, got_ref, out_ref):
    for k in range(8):
        j = PLACE[ORDER[k] ^ m]
        mine, got = mine_ref[k : k + 1, :], got_ref[j : j + 1, :]
        top = jnp.maximum(mine, got)
        out_ref[k : k + 1, :] = top + jnp.log2(jnp.exp2(mine - top) + jnp.exp2(got - top))


def merge_call(mine, got, m):
    return pl.pallas_call(
        functools.partial(merge_kernel, m),
        in_specs=[vmem_spec()] * 2,
        out_specs=vmem_spec(),
        out_shape=jax.ShapeDtypeStruct(mine.shape, jnp.float32),
        compiler_params=pltpu.CompilerParams(vmem_limit_bytes=2 * 1024 * 1024),
        name="merge",
    )(mine, got)


def weights_kernel(core_ref, flags, e_ref, a_lse, b_lse, *refs):
    a_refs, (w_ref, gb_hi, a_half) = refs[:8], refs[8:]
    rows = a_lse.shape[1]
    half = 4 * rows
    core = core_ref[0]
    take_half(core, a_halves(a_refs), 1, a_half)
    for q in range(2):
        a_row = jnp.concatenate([a_lse[4 * q + j : 4 * q + j + 1, :] for j in range(4)], axis=1)
        b_row = jnp.concatenate([b_lse[pl.ds((q ^ core) * 4 + j, 1), :] for j in range(4)], axis=1)

        @pl.when(flags[0] == 0)
        def _():
            a_col = column_of(jnp.exp2(-a_row), half)
            b_exp = jnp.exp2(-b_row)
            for r in range(4):
                sl = slice(r * rows, (r + 1) * rows)
                w_ref[q, sl, :] = (e_ref[q, sl, :] * (a_col[sl, :] + b_exp)).astype(jnp.bfloat16)

        @pl.when(flags[0] != 0)
        def _():
            a_col = column_of(a_row, half)
            for r in range(4):
                sl = slice(r * rows, (r + 1) * rows)
                s = e_ref[q, sl, :]
                w_ref[q, sl, :] = (jnp.exp2(s - a_col[sl, :]) + jnp.exp2(s - b_row)).astype(jnp.bfloat16)

    gb_hi[...] = (0.5 * dot_tn(w_ref[1 - core], a_half[...])).astype(jnp.bfloat16)


def weights_call(core, flags, e, a_lse, b_lse, a_blocks):
    rows, features = a_blocks[0].shape
    half = 4 * rows
    return pl.pallas_call(
        weights_kernel,
        in_specs=[smem_spec()] * 2 + [vmem_spec()] * 11,
        out_specs=[vmem_spec()] * 2,
        out_shape=[
            pltpu.VMEM((2, half, half), jnp.bfloat16),
            jax.ShapeDtypeStruct((half, features), jnp.bfloat16),
        ],
        scratch_shapes=[pltpu.VMEM((half, features), jnp.bfloat16)],
        compiler_params=params(),
        cost_estimate=cost(1, half, half, features, 12),
        name="weights",
    )(core, flags, e, a_lse, b_lse, *a_blocks)


def middle_kernel(core_ref, w_ref, *refs):
    a_refs, b_refs = refs[:8], b_halves(refs[8:15])
    ga_hi, gb_lo, a_half, b_half = refs[15:]
    rows = a_refs[0].shape[0]
    core = core_ref[0]
    take_half(core, a_halves(a_refs), 0, a_half)
    take_half(core, b_refs, 1, b_half)
    g = 0.5 * dot_tn(w_ref[core], a_half[...])
    high = g[:rows].astype(jnp.bfloat16)
    gb_lo[:rows] = high
    gb_lo[rows : 2 * rows] = (g[:rows] - high.astype(jnp.float32)).astype(jnp.bfloat16)
    gb_lo[2 * rows :] = g[rows:].astype(jnp.bfloat16)
    ga_hi[...] = 0.5 * jnp.dot(w_ref[1], b_half[...], preferred_element_type=jnp.float32)


def middle_call(core, w, a_blocks, b_blocks):
    rows, features = a_blocks[0].shape
    half = 4 * rows
    return pl.pallas_call(
        middle_kernel,
        in_specs=[smem_spec()] + [vmem_spec()] * 16,
        out_specs=[vmem_spec()] * 2,
        out_shape=[
            pltpu.VMEM((half, features), jnp.float32),
            jax.ShapeDtypeStruct((half + rows, features), jnp.bfloat16),
        ],
        scratch_shapes=[pltpu.VMEM((half, features), jnp.bfloat16)] * 2,
        compiler_params=params(),
        cost_estimate=cost(2, half, half, features),
        name="middle",
    )(core, w, *a_blocks, *b_blocks)


def far_kernel(ga_hi, got, *outs):
    rows = outs[0].shape[0]
    for j in range(4):
        sl = slice(j * rows, (j + 1) * rows)
        outs[j][...] = (ga_hi[sl, :] + got[sl, :].astype(jnp.float32)).astype(jnp.bfloat16)


def far_call(ga_hi, got):
    half, features = ga_hi.shape
    rows = half // 4
    return pl.pallas_call(
        far_kernel,
        in_specs=[vmem_spec()] * 2,
        out_specs=[vmem_spec()] * 4,
        out_shape=[jax.ShapeDtypeStruct((rows, features), jnp.bfloat16)] * 4,
        compiler_params=params(),
        cost_estimate=cost(0, half, features, 1, 8),
        name="far",
    )(ga_hi, got)


def last_kernel(core_ref, w_ref, *refs):
    b_refs, (ga_lo, b_half) = b_halves(refs[:7]), refs[7:]
    take_half(core_ref[0], b_refs, 0, b_half)
    ga_lo[...] = 0.5 * jnp.dot(w_ref[0], b_half[...], preferred_element_type=jnp.float32)


def last_call(core, w, b_blocks):
    rows, features = b_blocks[0].shape
    half = 4 * rows
    return pl.pallas_call(
        last_kernel,
        in_specs=[smem_spec()] + [vmem_spec()] * 8,
        out_specs=vmem_spec(),
        out_shape=pltpu.VMEM((half, features), jnp.float32),
        scratch_shapes=[pltpu.VMEM((half, features), jnp.bfloat16)],
        compiler_params=params(),
        cost_estimate=cost(1, half, half, features),
        name="last",
    )(core, w, *b_blocks)


def near_kernel(ga_lo, got_lo, r_xy, r_yz, r_xz, p0, p1, p2, p4):
    rows = p0.shape[0]
    wide = lambda a: a.astype(jnp.float32)
    p0[...] = ga_lo[:rows] + (wide(got_lo[:rows]) + wide(got_lo[rows : 2 * rows]))
    part = lambda j: ga_lo[j * rows : (j + 1) * rows, :] + wide(got_lo[(j + 1) * rows : (j + 2) * rows, :])
    p1[...] = (part(1) + wide(r_xz[...])).astype(jnp.bfloat16)
    p2[...] = (part(2) + wide(r_xy[...])).astype(jnp.bfloat16)
    p4[...] = (part(3) + wide(r_yz[...])).astype(jnp.bfloat16)


def near_call(ga_lo, got_lo, *received):
    rows, features = received[0].shape
    narrow = jax.ShapeDtypeStruct((rows, features), jnp.bfloat16)
    return pl.pallas_call(
        near_kernel,
        in_specs=[vmem_spec()] * 5,
        out_specs=[vmem_spec()] * 4,
        out_shape=[pltpu.VMEM((rows, features), jnp.float32)] + [narrow] * 3,
        compiler_params=params(),
        cost_estimate=cost(0, 4 * rows, features, 1, 12),
        name="near",
    )(ga_lo, got_lo, *received)


def body(images, texts):
    rows, features = images.shape
    scale = 4.0 / math.sqrt(features) * LOG2E
    core = lax.axis_index("core")
    first = core == 0
    core_arr = core.astype(jnp.int32).reshape(1)
    in_hbm = lambda a: pltpu.with_memory_space_constraint(a, pltpu.HBM)
    got = swap(images), swap(texts)
    own, other = own_call(core_arr, *load_call(core_arr, in_hbm(images), in_hbm(texts)), *got)
    near = {m: to_cube(own, m) for m in (4, 2, 1)}
    far = {7: to_cube(own, 7), 5: to_cube(near[1], 4), 3: to_cube(near[2], 1), 6: to_cube(near[4], 2)}
    blocks = {0: own, **near, **far}
    in_vmem = lambda a: pltpu.with_memory_space_constraint(a, pltpu.VMEM)
    a_blocks = [in_vmem(blocks[m]) for m in ORDER]
    swapped = {m: swap(far[m]) for m in (7, 5, 3)}
    joined = [swap(a) for a in join_call(near[1], near[2], near[4])]
    last, *held = lax.optimization_barrier((far[6], swapped[7], swapped[5], swapped[3], *joined))
    swapped.update(zip((7, 5, 3), held))
    swapped[6] = swap(last)
    b_blocks = [other] + held[3:] + [swapped[m] for m in ORDER[4:]]
    b_blocks = [in_vmem(b) for b in b_blocks]

    e, a_stat, b_stat, flags = scores_call(core_arr, a_blocks, b_blocks, scale)
    a_lse = merge_call(a_stat, swap(b_stat), 0)
    for m in (1, 2, 4):
        a_lse = merge_call(a_lse, to_cube(a_lse, m), m)
    b_lse = swap(a_lse)

    w, gb_hi = weights_call(core_arr, flags, e, a_lse, b_lse, a_blocks)
    got_hi = swap(gb_hi)
    ga_hi, gb_lo = middle_call(core_arr, w, a_blocks, b_blocks)
    got_lo = swap(gb_lo)
    p = dict(zip(ORDER[4:], far_call(ga_hi, got_hi)))
    from_xy = to_cube(p[3], 1)
    from_yz = to_cube(p[6], 2)
    from_xz = to_cube(p[5], 4)
    from_xyz = to_cube(p[7], 7)
    ga_lo = last_call(core_arr, w, b_blocks)
    p0, p1, p2, p4 = near_call(ga_lo, got_lo, from_xy, from_yz, from_xz)
    wide = lambda a: a.astype(jnp.float32)
    total = p0 + wide(from_xyz) + wide(to_cube(p1, 1)) + wide(to_cube(p2, 2)) + wide(to_cube(p4, 4))
    kept, sent = total[:rows], total[rows:]
    got_sum = swap(sent)
    image_sum = jnp.where(first, kept, got_sum)
    text_sum = jnp.where(first, got_sum, kept)
    return (image_sum - wide(texts), text_sum - wide(images))


def solution(mesh):
    chips = Mesh(mesh.devices.reshape(SIZES), AXES)
    spec = P(AXES, None)
    return jax.shard_map(
        body,
        mesh=chips,
        in_specs=(spec, spec),
        out_specs=(spec, spec),
        check_vma=False,
    )
```

```python
import functools
import math

import jax
import jax.numpy as jnp
from jax import lax
from jax.experimental import pallas as pl
from jax.experimental.pallas import tpu as pltpu
from jax.sharding import Mesh, PartitionSpec as P

AXES = ("y", "core", "x", "z")
SIZES = (4, 2, 4, 4)
ORDER = (0, 1, 2, 4, 3, 5, 6, 7)
PLACE = tuple(ORDER.index(m) for m in range(8))
LOG2E = 1.4426950408889634
VMEM_LIMIT = 12 * 1024 * 1024
RANGE = 80.0


def flat(y, c, x, z):
    return ((y * 2 + c) * 4 + x) * 4 + z


def coords():
    for y in range(4):
        for c in range(2):
            for x in range(4):
                for z in range(4):
                    yield y, c, x, z


def partner(v, wrapped):
    return 3 - v if wrapped else v ^ 1


def across(m):
    pairs = []
    for y, c, x, z in coords():
        target = (
            partner(y, c == 0) if m & 2 else y,
            c,
            partner(x, c == 1) if m & 1 else x,
            partner(z, c == 1) if m & 4 else z,
        )
        pairs.append((flat(y, c, x, z), flat(*target)))
    return pairs


SWAP = [(flat(y, c, x, z), flat(y, 1 - c, x, z)) for y, c, x, z in coords()]


def to_cube(a, m):
    return lax.ppermute(a, AXES, across(m))


def swap(a):
    return lax.ppermute(a, AXES, SWAP)


def column_of(row, rows):
    padded = -(-rows // 128) * 128
    wide = jnp.broadcast_to(row, (128, rows))
    if padded != rows:
        wide = jnp.concatenate([wide, jnp.zeros((128, padded - rows), jnp.float32)], axis=1)
    return wide.T[:rows, :1]


def row_of(column, rows):
    padded = -(-rows // 128) * 128
    wide = jnp.broadcast_to(column, (rows, 128))
    if padded != rows:
        wide = jnp.concatenate([wide, jnp.zeros((padded - rows, 128), jnp.float32)], axis=0)
    return wide.T[:1, :rows]


def vmem_spec():
    return pl.BlockSpec(memory_space=pltpu.VMEM)


def smem_spec():
    return pl.BlockSpec(memory_space=pltpu.SMEM)


def cost(matmuls, rows, cols, depth, passes=0):
    return pl.CostEstimate(
        flops=2 * matmuls * rows * cols * depth, bytes_accessed=passes * rows * cols, transcendentals=0
    )


def params():
    return pltpu.CompilerParams(vmem_limit_bytes=VMEM_LIMIT)


def dot_nt(a, b):
    return lax.dot_general(a, b, (((1,), (1,)), ((), ())), preferred_element_type=jnp.float32)


def dot_tn(a, b):
    return lax.dot_general(a, b, (((0,), (0,)), ((), ())), preferred_element_type=jnp.float32)


def load_kernel(core_ref, images, texts, mine, yours, sem):
    core = core_ref[0]
    for c, order in enumerate(((mine, yours), (yours, mine))):

        @pl.when(core == c)
        def _():
            copies = [pltpu.make_async_copy(a, o, sem.at[j]) for j, (a, o) in enumerate(zip((images, texts), order))]
            for copy in copies:
                copy.start()
            for copy in copies:
                copy.wait()


def load_call(core, images, texts):
    block = pltpu.VMEM(images.shape, images.dtype)
    return pl.pallas_call(
        load_kernel,
        in_specs=[smem_spec()] + [pl.BlockSpec(memory_space=pl.ANY)] * 2,
        out_specs=[vmem_spec()] * 2,
        out_shape=[block, block],
        scratch_shapes=[pltpu.SemaphoreType.DMA((2,))],
        compiler_params=params(),
        cost_estimate=cost(0, images.shape[0], images.shape[1], 1, 32),
        name="load",
    )(core, images, texts)


def own_kernel(core_ref, mine, yours, got_images, got_texts, own, other):
    rows = mine.shape[0]
    own[:rows] = mine[...]
    other[rows:] = yours[...]
    for c, (low, top) in enumerate(((got_images, got_texts), (got_texts, got_images))):

        @pl.when(core_ref[0] == c)
        def _():
            own[rows:] = low[...]
            other[:rows] = top[...]


def own_call(core, *parts):
    rows, features = parts[0].shape
    block = pltpu.VMEM((2 * rows, features), parts[0].dtype)
    return pl.pallas_call(
        own_kernel,
        in_specs=[smem_spec()] + [vmem_spec()] * 4,
        out_specs=[vmem_spec()] * 2,
        out_shape=[block, block],
        compiler_params=params(),
        cost_estimate=cost(0, rows, features, 1, 16),
        name="own",
    )(core, *parts)


def join_kernel(b0, b1, b2, out0, out1):
    rows = b0.shape[0]
    cut = rows // 2
    out0[:rows] = b0[...]
    out0[rows:] = b1[:cut]
    out1[:cut] = b1[cut:]
    out1[cut:] = b2[...]


def join_call(*parts):
    rows, features = parts[0].shape
    out = jax.ShapeDtypeStruct((3 * rows // 2, features), parts[0].dtype)
    return pl.pallas_call(
        join_kernel,
        in_specs=[vmem_spec()] * 3,
        out_specs=[vmem_spec()] * 2,
        out_shape=[out, out],
        compiler_params=params(),
        cost_estimate=cost(0, 3 * rows, features, 1, 4),
        name="join",
    )(*parts)


def take_half(core, halves, shift, out):
    for c in range(2):

        @pl.when(core == c)
        def _():
            at = 0
            for part in halves[c ^ shift]:
                out[at : at + part.shape[0], :] = part[...]
                at += part.shape[0]


def a_halves(refs):
    return refs[:4], refs[4:8]


def b_halves(refs):
    return refs[:3], refs[3:7]


def scores_kernel(scale, core_ref, *refs):
    a_refs, b_refs = refs[:8], b_halves(refs[8:15])
    e_ref, a_stat, b_stat, flags, a_cat, b_cat, col_m, col_s = refs[15:]
    rows = a_refs[0].shape[0]
    half = 4 * rows
    core = core_ref[0]
    for q in range(2):
        take_half(core, b_refs, q, b_cat.at[q])

    def quadrant(q):
        b_half = b_cat[q]
        sums = []
        col = None
        for r in range(4):
            sl = slice(r * rows, (r + 1) * rows)
            e = jnp.exp2(dot_nt(a_refs[4 * q + r][...], b_half) * scale)
            e_ref[q, sl, :] = e
            sums.append(jnp.sum(e, axis=1, keepdims=True))
            part = jnp.sum(e, axis=0, keepdims=True)
            col = part if col is None else col + part
        row_lse = jnp.log2(row_of(jnp.concatenate(sums, axis=0), half))
        col_lse = jnp.log2(col)
        for j in range(4):
            sl = slice(j * rows, (j + 1) * rows)
            a_stat[4 * q + j : 4 * q + j + 1, :] = row_lse[:, sl]
            b_stat[pl.ds((q ^ core) * 4 + j, 1), :] = col_lse[:, sl]
        return jnp.maximum(jnp.abs(row_lse), jnp.abs(col_lse))

    def by_maxima(q):
        for r in range(4):
            a_cat[r * rows : (r + 1) * rows, :] = a_refs[4 * q + r][...]
        col_m[...] = jnp.full_like(col_m, -jnp.inf)
        col_s[...] = jnp.zeros_like(col_s)

        @pl.loop(0, 4)
        def _(r):
            sl = pl.ds(pl.multiple_of(r * rows, 16), rows)
            s = dot_nt(a_cat[sl, :], b_cat[q]) * scale
            e_ref[q, sl, :] = s
            row_m = jnp.max(s, axis=1, keepdims=True)
            row_s = jnp.sum(jnp.exp2(s - row_m), axis=1, keepdims=True)
            a_stat[pl.ds(4 * q + r, 1), :] = row_of(row_m + jnp.log2(row_s), rows)
            blk_m = jnp.max(s, axis=0, keepdims=True)
            blk_s = jnp.sum(jnp.exp2(s - blk_m), axis=0, keepdims=True)
            before = col_m[...]
            top = jnp.maximum(before, blk_m)
            col_s[...] = col_s[...] * jnp.exp2(before - top) + blk_s * jnp.exp2(blk_m - top)
            col_m[...] = top

        lse = col_m[...] + jnp.log2(col_s[...])
        for j in range(4):
            b_stat[pl.ds((q ^ core) * 4 + j, 1), :] = lse[:, j * rows : (j + 1) * rows]

    bad = jnp.logical_not(jnp.max(jnp.maximum(quadrant(0), quadrant(1))) <= RANGE)
    flags[0] = bad.astype(jnp.int32)

    @pl.when(bad)
    def _():
        by_maxima(0)
        by_maxima(1)


def scores_call(core, a_blocks, b_blocks, scale):
    rows, features = a_blocks[0].shape
    half = 4 * rows
    stat = jax.ShapeDtypeStruct((8, rows), jnp.float32)
    return pl.pallas_call(
        functools.partial(scores_kernel, scale),
        in_specs=[smem_spec()] + [vmem_spec()] * 15,
        out_specs=[vmem_spec()] * 3 + [smem_spec()],
        out_shape=[
            pltpu.VMEM((2, half, half), jnp.float32),
            stat,
            stat,
            jax.ShapeDtypeStruct((1,), jnp.int32),
        ],
        scratch_shapes=[
            pltpu.VMEM((half, features), jnp.bfloat16),
            pltpu.VMEM((2, half, features), jnp.bfloat16),
            pltpu.VMEM((1, half), jnp.float32),
            pltpu.VMEM((1, half), jnp.float32),
        ],
        compiler_params=params(),
        cost_estimate=cost(2, half, half, features),
        name="scores",
    )(core, *a_blocks, *b_blocks)


def merge_kernel(m, mine_ref, got_ref, out_ref):
    for k in range(8):
        j = PLACE[ORDER[k] ^ m]
        mine, got = mine_ref[k : k + 1, :], got_ref[j : j + 1, :]
        top = jnp.maximum(mine, got)
        out_ref[k : k + 1, :] = top + jnp.log2(jnp.exp2(mine - top) + jnp.exp2(got - top))


def merge_call(mine, got, m):
    return pl.pallas_call(
        functools.partial(merge_kernel, m),
        in_specs=[vmem_spec()] * 2,
        out_specs=vmem_spec(),
        out_shape=jax.ShapeDtypeStruct(mine.shape, jnp.float32),
        compiler_params=pltpu.CompilerParams(vmem_limit_bytes=2 * 1024 * 1024),
        name="merge",
    )(mine, got)


def weights_kernel(core_ref, flags, e_ref, a_lse, b_lse, *refs):
    a_refs, (w_ref, gb_hi, a_half) = refs[:8], refs[8:]
    rows = a_lse.shape[1]
    half = 4 * rows
    core = core_ref[0]
    take_half(core, a_halves(a_refs), 1, a_half)
    for q in range(2):
        a_row = jnp.concatenate([a_lse[4 * q + j : 4 * q + j + 1, :] for j in range(4)], axis=1)
        b_row = jnp.concatenate([b_lse[pl.ds((q ^ core) * 4 + j, 1), :] for j in range(4)], axis=1)

        @pl.when(flags[0] == 0)
        def _():
            a_col = column_of(jnp.exp2(-a_row), half)
            b_exp = jnp.exp2(-b_row)
            for r in range(4):
                sl = slice(r * rows, (r + 1) * rows)
                w_ref[q, sl, :] = (e_ref[q, sl, :] * (a_col[sl, :] + b_exp)).astype(jnp.bfloat16)

        @pl.when(flags[0] != 0)
        def _():
            a_col = column_of(a_row, half)
            for r in range(4):
                sl = slice(r * rows, (r + 1) * rows)
                s = e_ref[q, sl, :]
                w_ref[q, sl, :] = (jnp.exp2(s - a_col[sl, :]) + jnp.exp2(s - b_row)).astype(jnp.bfloat16)

    gb_hi[...] = (0.5 * dot_tn(w_ref[1 - core], a_half[...])).astype(jnp.bfloat16)


def weights_call(core, flags, e, a_lse, b_lse, a_blocks):
    rows, features = a_blocks[0].shape
    half = 4 * rows
    return pl.pallas_call(
        weights_kernel,
        in_specs=[smem_spec()] * 2 + [vmem_spec()] * 11,
        out_specs=[vmem_spec()] * 2,
        out_shape=[
            pltpu.VMEM((2, half, half), jnp.bfloat16),
            jax.ShapeDtypeStruct((half, features), jnp.bfloat16),
        ],
        scratch_shapes=[pltpu.VMEM((half, features), jnp.bfloat16)],
        compiler_params=params(),
        cost_estimate=cost(1, half, half, features, 12),
        name="weights",
    )(core, flags, e, a_lse, b_lse, *a_blocks)


def middle_kernel(core_ref, w_ref, *refs):
    a_refs, b_refs = refs[:8], b_halves(refs[8:15])
    ga_hi, gb_lo, a_half, b_half = refs[15:]
    rows = a_refs[0].shape[0]
    core = core_ref[0]
    take_half(core, a_halves(a_refs), 0, a_half)
    take_half(core, b_refs, 1, b_half)
    g = 0.5 * dot_tn(w_ref[core], a_half[...])
    high = g[:rows].astype(jnp.bfloat16)
    gb_lo[:rows] = high
    gb_lo[rows : 2 * rows] = (g[:rows] - high.astype(jnp.float32)).astype(jnp.bfloat16)
    gb_lo[2 * rows :] = g[rows:].astype(jnp.bfloat16)
    ga_hi[...] = 0.5 * jnp.dot(w_ref[1], b_half[...], preferred_element_type=jnp.float32)


def middle_call(core, w, a_blocks, b_blocks):
    rows, features = a_blocks[0].shape
    half = 4 * rows
    return pl.pallas_call(
        middle_kernel,
        in_specs=[smem_spec()] + [vmem_spec()] * 16,
        out_specs=[vmem_spec()] * 2,
        out_shape=[
            pltpu.VMEM((half, features), jnp.float32),
            jax.ShapeDtypeStruct((half + rows, features), jnp.bfloat16),
        ],
        scratch_shapes=[pltpu.VMEM((half, features), jnp.bfloat16)] * 2,
        compiler_params=params(),
        cost_estimate=cost(2, half, half, features),
        name="middle",
    )(core, w, *a_blocks, *b_blocks)


def far_kernel(ga_hi, got, *outs):
    rows = outs[0].shape[0]
    for j in range(4):
        sl = slice(j * rows, (j + 1) * rows)
        outs[j][...] = (ga_hi[sl, :] + got[sl, :].astype(jnp.float32)).astype(jnp.bfloat16)


def far_call(ga_hi, got):
    half, features = ga_hi.shape
    rows = half // 4
    return pl.pallas_call(
        far_kernel,
        in_specs=[vmem_spec()] * 2,
        out_specs=[vmem_spec()] * 4,
        out_shape=[jax.ShapeDtypeStruct((rows, features), jnp.bfloat16)] * 4,
        compiler_params=params(),
        cost_estimate=cost(0, half, features, 1, 8),
        name="far",
    )(ga_hi, got)


def last_kernel(core_ref, w_ref, *refs):
    b_refs, (ga_lo, b_half) = b_halves(refs[:7]), refs[7:]
    take_half(core_ref[0], b_refs, 0, b_half)
    ga_lo[...] = 0.5 * jnp.dot(w_ref[0], b_half[...], preferred_element_type=jnp.float32)


def last_call(core, w, b_blocks):
    rows, features = b_blocks[0].shape
    half = 4 * rows
    return pl.pallas_call(
        last_kernel,
        in_specs=[smem_spec()] + [vmem_spec()] * 8,
        out_specs=vmem_spec(),
        out_shape=pltpu.VMEM((half, features), jnp.float32),
        scratch_shapes=[pltpu.VMEM((half, features), jnp.bfloat16)],
        compiler_params=params(),
        cost_estimate=cost(1, half, half, features),
        name="last",
    )(core, w, *b_blocks)


def near_kernel(ga_lo, got_lo, r_xy, r_yz, r_xz, p0, p1, p2, p4):
    rows = p0.shape[0]
    wide = lambda a: a.astype(jnp.float32)
    p0[...] = ga_lo[:rows] + (wide(got_lo[:rows]) + wide(got_lo[rows : 2 * rows]))
    part = lambda j: ga_lo[j * rows : (j + 1) * rows, :] + wide(got_lo[(j + 1) * rows : (j + 2) * rows, :])
    p1[...] = (part(1) + wide(r_xz[...])).astype(jnp.bfloat16)
    p2[...] = (part(2) + wide(r_xy[...])).astype(jnp.bfloat16)
    p4[...] = (part(3) + wide(r_yz[...])).astype(jnp.bfloat16)


def near_call(ga_lo, got_lo, *received):
    rows, features = received[0].shape
    narrow = jax.ShapeDtypeStruct((rows, features), jnp.bfloat16)
    return pl.pallas_call(
        near_kernel,
        in_specs=[vmem_spec()] * 5,
        out_specs=[vmem_spec()] * 4,
        out_shape=[pltpu.VMEM((rows, features), jnp.float32)] + [narrow] * 3,
        compiler_params=params(),
        cost_estimate=cost(0, 4 * rows, features, 1, 12),
        name="near",
    )(ga_lo, got_lo, *received)


def body(images, texts):
    rows, features = images.shape
    scale = 4.0 / math.sqrt(features) * LOG2E
    core = lax.axis_index("core")
    first = core == 0
    core_arr = core.astype(jnp.int32).reshape(1)
    in_hbm = lambda a: pltpu.with_memory_space_constraint(a, pltpu.HBM)
    got = swap(images), swap(texts)
    own, other = own_call(core_arr, *load_call(core_arr, in_hbm(images), in_hbm(texts)), *got)
    near = {m: to_cube(own, m) for m in (4, 2, 1)}
    late = lax.optimization_barrier((own, near[1]))[0]
    far = {7: to_cube(late, 7), 5: to_cube(near[1], 4), 3: to_cube(near[2], 1), 6: to_cube(near[4], 2)}
    blocks = {0: own, **near, **far}
    in_vmem = lambda a: pltpu.with_memory_space_constraint(a, pltpu.VMEM)
    a_blocks = [in_vmem(blocks[m]) for m in ORDER]
    swapped = {m: swap(far[m]) for m in (7, 5, 3)}
    joined = [swap(a) for a in join_call(near[1], near[2], near[4])]
    last, *held = lax.optimization_barrier((far[6], swapped[7], swapped[5], swapped[3], *joined))
    swapped.update(zip((7, 5, 3), held))
    swapped[6] = swap(last)
    b_blocks = [other] + held[3:] + [swapped[m] for m in ORDER[4:]]
    b_blocks = [in_vmem(b) for b in b_blocks]

    e, a_stat, b_stat, flags = scores_call(core_arr, a_blocks, b_blocks, scale)
    a_lse = merge_call(a_stat, swap(b_stat), 0)
    for m in (1, 2, 4):
        a_lse = merge_call(a_lse, to_cube(a_lse, m), m)
    b_lse = swap(a_lse)

    w, gb_hi = weights_call(core_arr, flags, e, a_lse, b_lse, a_blocks)
    got_hi = swap(gb_hi)
    ga_hi, gb_lo = middle_call(core_arr, w, a_blocks, b_blocks)
    got_lo = swap(gb_lo)
    p = dict(zip(ORDER[4:], far_call(ga_hi, got_hi)))
    from_xy = to_cube(p[3], 1)
    from_yz = to_cube(p[6], 2)
    from_xz = to_cube(p[5], 4)
    from_xyz = to_cube(p[7], 7)
    ga_lo = last_call(core_arr, w, b_blocks)
    p0, p1, p2, p4 = near_call(ga_lo, got_lo, from_xy, from_yz, from_xz)
    wide = lambda a: a.astype(jnp.float32)
    total = p0 + wide(from_xyz) + wide(to_cube(p1, 1)) + wide(to_cube(p2, 2)) + wide(to_cube(p4, 4))
    kept, sent = total[:rows], total[rows:]
    got_sum = swap(sent)
    image_sum = jnp.where(first, kept, got_sum)
    text_sum = jnp.where(first, got_sum, kept)
    return (image_sum - wide(texts), text_sum - wide(images))


def solution(mesh):
    chips = Mesh(mesh.devices.reshape(SIZES), AXES)
    spec = P(AXES, None)
    return jax.shard_map(
        body,
        mesh=chips,
        in_specs=(spec, spec),
        out_specs=(spec, spec),
        check_vma=False,
    )
```

```python
import functools
import math

import jax
import jax.numpy as jnp
from jax import lax
from jax.experimental import pallas as pl
from jax.experimental.pallas import tpu as pltpu
from jax.sharding import Mesh, PartitionSpec as P

AXES = ("y", "core", "x", "z")
SIZES = (4, 2, 4, 4)
ORDER = (0, 1, 2, 4, 3, 5, 6, 7)
PLACE = tuple(ORDER.index(m) for m in range(8))
LOG2E = 1.4426950408889634
VMEM_LIMIT = 12 * 1024 * 1024
RANGE = 80.0


def flat(y, c, x, z):
    return ((y * 2 + c) * 4 + x) * 4 + z


def coords():
    for y in range(4):
        for c in range(2):
            for x in range(4):
                for z in range(4):
                    yield y, c, x, z


def partner(v, wrapped):
    return 3 - v if wrapped else v ^ 1


def across(m):
    pairs = []
    for y, c, x, z in coords():
        target = (
            partner(y, c == 0) if m & 2 else y,
            c,
            partner(x, c == 1) if m & 1 else x,
            partner(z, c == 1) if m & 4 else z,
        )
        pairs.append((flat(y, c, x, z), flat(*target)))
    return pairs


SWAP = [(flat(y, c, x, z), flat(y, 1 - c, x, z)) for y, c, x, z in coords()]


def to_cube(a, m):
    return lax.ppermute(a, AXES, across(m))


def swap(a):
    return lax.ppermute(a, AXES, SWAP)


def column_of(row, rows):
    padded = -(-rows // 128) * 128
    wide = jnp.broadcast_to(row, (128, rows))
    if padded != rows:
        wide = jnp.concatenate([wide, jnp.zeros((128, padded - rows), jnp.float32)], axis=1)
    return wide.T[:rows, :1]


def row_of(column, rows):
    padded = -(-rows // 128) * 128
    wide = jnp.broadcast_to(column, (rows, 128))
    if padded != rows:
        wide = jnp.concatenate([wide, jnp.zeros((padded - rows, 128), jnp.float32)], axis=0)
    return wide.T[:1, :rows]


def vmem_spec():
    return pl.BlockSpec(memory_space=pltpu.VMEM)


def smem_spec():
    return pl.BlockSpec(memory_space=pltpu.SMEM)


def cost(matmuls, rows, cols, depth, passes=0):
    return pl.CostEstimate(
        flops=2 * matmuls * rows * cols * depth, bytes_accessed=passes * rows * cols, transcendentals=0
    )


def params():
    return pltpu.CompilerParams(vmem_limit_bytes=VMEM_LIMIT)


def dot_nt(a, b):
    return lax.dot_general(a, b, (((1,), (1,)), ((), ())), preferred_element_type=jnp.float32)


def dot_tn(a, b):
    return lax.dot_general(a, b, (((0,), (0,)), ((), ())), preferred_element_type=jnp.float32)


def load_kernel(images, texts, mine, yours, sem):
    core = lax.axis_index("core")
    for c, order in enumerate(((mine, yours), (yours, mine))):

        @pl.when(core == c)
        def _():
            copies = [pltpu.make_async_copy(a, o, sem.at[j]) for j, (a, o) in enumerate(zip((images, texts), order))]
            for copy in copies:
                copy.start()
            for copy in copies:
                copy.wait()


def load_call(images, texts):
    block = pltpu.VMEM(images.shape, images.dtype)
    return pl.pallas_call(
        load_kernel,
        in_specs=[pl.BlockSpec(memory_space=pl.ANY)] * 2,
        out_specs=[vmem_spec()] * 2,
        out_shape=[block, block],
        scratch_shapes=[pltpu.SemaphoreType.DMA((2,))],
        compiler_params=params(),
        cost_estimate=cost(0, images.shape[0], images.shape[1], 1, 32),
        name="load",
    )(images, texts)


def own_kernel(mine, yours, got_images, got_texts, own, other):
    rows = mine.shape[0]
    own[:rows] = mine[...]
    other[rows:] = yours[...]
    for c, (low, top) in enumerate(((got_images, got_texts), (got_texts, got_images))):

        @pl.when(lax.axis_index("core") == c)
        def _():
            own[rows:] = low[...]
            other[:rows] = top[...]


def own_call(*parts):
    rows, features = parts[0].shape
    block = pltpu.VMEM((2 * rows, features), parts[0].dtype)
    return pl.pallas_call(
        own_kernel,
        in_specs=[vmem_spec()] * 4,
        out_specs=[vmem_spec()] * 2,
        out_shape=[block, block],
        compiler_params=params(),
        cost_estimate=cost(0, rows, features, 1, 16),
        name="own",
    )(*parts)


def join_kernel(b0, b1, b2, out0, out1):
    rows = b0.shape[0]
    cut = rows // 2
    out0[:rows] = b0[...]
    out0[rows:] = b1[:cut]
    out1[:cut] = b1[cut:]
    out1[cut:] = b2[...]


def join_call(*parts):
    rows, features = parts[0].shape
    out = jax.ShapeDtypeStruct((3 * rows // 2, features), parts[0].dtype)
    return pl.pallas_call(
        join_kernel,
        in_specs=[vmem_spec()] * 3,
        out_specs=[vmem_spec()] * 2,
        out_shape=[out, out],
        compiler_params=params(),
        cost_estimate=cost(0, 3 * rows, features, 1, 4),
        name="join",
    )(*parts)


def take_half(core, halves, shift, out):
    for c in range(2):

        @pl.when(core == c)
        def _():
            at = 0
            for part in halves[c ^ shift]:
                out[at : at + part.shape[0], :] = part[...]
                at += part.shape[0]


def a_halves(refs):
    return refs[:4], refs[4:8]


def b_halves(refs):
    return refs[:3], refs[3:7]


def scores_kernel(scale, *refs):
    a_refs, b_refs = refs[:8], b_halves(refs[8:15])
    e_ref, a_stat, b_stat, flags, a_cat, b_cat, col_m, col_s = refs[15:]
    rows = a_refs[0].shape[0]
    half = 4 * rows
    core = lax.axis_index("core")
    for q in range(2):
        take_half(core, b_refs, q, b_cat.at[q])

    def quadrant(q):
        b_half = b_cat[q]
        sums = []
        col = None
        for r in range(4):
            sl = slice(r * rows, (r + 1) * rows)
            e = jnp.exp2(dot_nt(a_refs[4 * q + r][...], b_half) * scale)
            e_ref[q, sl, :] = e
            sums.append(jnp.sum(e, axis=1, keepdims=True))
            part = jnp.sum(e, axis=0, keepdims=True)
            col = part if col is None else col + part
        row_lse = jnp.log2(row_of(jnp.concatenate(sums, axis=0), half))
        col_lse = jnp.log2(col)
        for j in range(4):
            sl = slice(j * rows, (j + 1) * rows)
            a_stat[4 * q + j : 4 * q + j + 1, :] = row_lse[:, sl]
            b_stat[pl.ds((q ^ core) * 4 + j, 1), :] = col_lse[:, sl]
        return jnp.maximum(jnp.abs(row_lse), jnp.abs(col_lse))

    def by_maxima(q):
        for r in range(4):
            a_cat[r * rows : (r + 1) * rows, :] = a_refs[4 * q + r][...]
        col_m[...] = jnp.full_like(col_m, -jnp.inf)
        col_s[...] = jnp.zeros_like(col_s)

        @pl.loop(0, 4)
        def _(r):
            sl = pl.ds(pl.multiple_of(r * rows, 16), rows)
            s = dot_nt(a_cat[sl, :], b_cat[q]) * scale
            e_ref[q, sl, :] = s
            row_m = jnp.max(s, axis=1, keepdims=True)
            row_s = jnp.sum(jnp.exp2(s - row_m), axis=1, keepdims=True)
            a_stat[pl.ds(4 * q + r, 1), :] = row_of(row_m + jnp.log2(row_s), rows)
            blk_m = jnp.max(s, axis=0, keepdims=True)
            blk_s = jnp.sum(jnp.exp2(s - blk_m), axis=0, keepdims=True)
            before = col_m[...]
            top = jnp.maximum(before, blk_m)
            col_s[...] = col_s[...] * jnp.exp2(before - top) + blk_s * jnp.exp2(blk_m - top)
            col_m[...] = top

        lse = col_m[...] + jnp.log2(col_s[...])
        for j in range(4):
            b_stat[pl.ds((q ^ core) * 4 + j, 1), :] = lse[:, j * rows : (j + 1) * rows]

    bad = jnp.logical_not(jnp.max(jnp.maximum(quadrant(0), quadrant(1))) <= RANGE)
    flags[0] = bad.astype(jnp.int32)
    flags[1] = bad.astype(jnp.int32)

    @pl.when(bad)
    def _():
        by_maxima(0)
        by_maxima(1)


def scores_call(a_blocks, b_blocks, scale):
    rows, features = a_blocks[0].shape
    half = 4 * rows
    stat = jax.ShapeDtypeStruct((8, rows), jnp.float32)
    return pl.pallas_call(
        functools.partial(scores_kernel, scale),
        in_specs=[vmem_spec()] * 15,
        out_specs=[vmem_spec()] * 3 + [smem_spec()],
        out_shape=[
            pltpu.VMEM((2, half, half), jnp.float32),
            stat,
            stat,
            jax.ShapeDtypeStruct((2,), jnp.int32),
        ],
        scratch_shapes=[
            pltpu.VMEM((half, features), jnp.bfloat16),
            pltpu.VMEM((2, half, features), jnp.bfloat16),
            pltpu.VMEM((1, half), jnp.float32),
            pltpu.VMEM((1, half), jnp.float32),
        ],
        compiler_params=params(),
        cost_estimate=cost(2, half, half, features),
        name="scores",
    )(*a_blocks, *b_blocks)


def merge_kernel(m, mine_ref, got_ref, out_ref):
    for k in range(8):
        j = PLACE[ORDER[k] ^ m]
        mine, got = mine_ref[k : k + 1, :], got_ref[j : j + 1, :]
        top = jnp.maximum(mine, got)
        out_ref[k : k + 1, :] = top + jnp.log2(jnp.exp2(mine - top) + jnp.exp2(got - top))


def merge_call(mine, got, m):
    return pl.pallas_call(
        functools.partial(merge_kernel, m),
        in_specs=[vmem_spec()] * 2,
        out_specs=vmem_spec(),
        out_shape=jax.ShapeDtypeStruct(mine.shape, jnp.float32),
        compiler_params=pltpu.CompilerParams(vmem_limit_bytes=2 * 1024 * 1024),
        name="merge",
    )(mine, got)


def weights_kernel(flags, e_ref, a_lse, b_lse, *refs):
    a_refs, (w_ref, gb_hi, a_half) = refs[:8], refs[8:]
    rows = a_lse.shape[1]
    half = 4 * rows
    core = lax.axis_index("core")
    take_half(core, a_halves(a_refs), 1, a_half)
    for q in range(2):
        a_row = jnp.concatenate([a_lse[4 * q + j : 4 * q + j + 1, :] for j in range(4)], axis=1)
        b_row = jnp.concatenate([b_lse[pl.ds((q ^ core) * 4 + j, 1), :] for j in range(4)], axis=1)

        @pl.when(flags[q] == 0)
        def _():
            a_col = column_of(jnp.exp2(-a_row), half)
            b_exp = jnp.exp2(-b_row)
            for r in range(4):
                sl = slice(r * rows, (r + 1) * rows)
                w_ref[q, sl, :] = (e_ref[q, sl, :] * (a_col[sl, :] + b_exp)).astype(jnp.bfloat16)

        @pl.when(flags[q] != 0)
        def _():
            a_col = column_of(a_row, half)
            for r in range(4):
                sl = slice(r * rows, (r + 1) * rows)
                s = e_ref[q, sl, :]
                w_ref[q, sl, :] = (jnp.exp2(s - a_col[sl, :]) + jnp.exp2(s - b_row)).astype(jnp.bfloat16)

    gb_hi[...] = (0.5 * dot_tn(w_ref[1 - core], a_half[...])).astype(jnp.bfloat16)


def weights_call(flags, e, a_lse, b_lse, a_blocks):
    rows, features = a_blocks[0].shape
    half = 4 * rows
    return pl.pallas_call(
        weights_kernel,
        in_specs=[smem_spec()] + [vmem_spec()] * 11,
        out_specs=[vmem_spec()] * 2,
        out_shape=[
            pltpu.VMEM((2, half, half), jnp.bfloat16),
            jax.ShapeDtypeStruct((half, features), jnp.bfloat16),
        ],
        scratch_shapes=[pltpu.VMEM((half, features), jnp.bfloat16)],
        compiler_params=params(),
        cost_estimate=cost(1, half, half, features, 12),
        name="weights",
    )(flags, e, a_lse, b_lse, *a_blocks)


def middle_kernel(w_ref, *refs):
    a_refs, b_refs = refs[:8], b_halves(refs[8:15])
    ga_hi, gb_lo, a_half, b_half = refs[15:]
    rows = a_refs[0].shape[0]
    core = lax.axis_index("core")
    take_half(core, a_halves(a_refs), 0, a_half)
    take_half(core, b_refs, 1, b_half)
    g = 0.5 * dot_tn(w_ref[core], a_half[...])
    high = g[:rows].astype(jnp.bfloat16)
    gb_lo[:rows] = high
    gb_lo[rows : 2 * rows] = (g[:rows] - high.astype(jnp.float32)).astype(jnp.bfloat16)
    gb_lo[2 * rows :] = g[rows:].astype(jnp.bfloat16)
    ga_hi[...] = 0.5 * jnp.dot(w_ref[1], b_half[...], preferred_element_type=jnp.float32)


def middle_call(w, a_blocks, b_blocks):
    rows, features = a_blocks[0].shape
    half = 4 * rows
    return pl.pallas_call(
        middle_kernel,
        in_specs=[vmem_spec()] * 16,
        out_specs=[vmem_spec()] * 2,
        out_shape=[
            pltpu.VMEM((half, features), jnp.float32),
            jax.ShapeDtypeStruct((half + rows, features), jnp.bfloat16),
        ],
        scratch_shapes=[pltpu.VMEM((half, features), jnp.bfloat16)] * 2,
        compiler_params=params(),
        cost_estimate=cost(2, half, half, features),
        name="middle",
    )(w, *a_blocks, *b_blocks)


def far_kernel(ga_hi, got, *outs):
    rows = outs[0].shape[0]
    for j in range(4):
        sl = slice(j * rows, (j + 1) * rows)
        outs[j][...] = (ga_hi[sl, :] + got[sl, :].astype(jnp.float32)).astype(jnp.bfloat16)


def far_call(ga_hi, got):
    half, features = ga_hi.shape
    rows = half // 4
    return pl.pallas_call(
        far_kernel,
        in_specs=[vmem_spec()] * 2,
        out_specs=[vmem_spec()] * 4,
        out_shape=[jax.ShapeDtypeStruct((rows, features), jnp.bfloat16)] * 4,
        compiler_params=params(),
        cost_estimate=cost(0, half, features, 1, 8),
        name="far",
    )(ga_hi, got)


def last_kernel(w_ref, *refs):
    b_refs, (ga_lo, b_half) = b_halves(refs[:7]), refs[7:]
    take_half(lax.axis_index("core"), b_refs, 0, b_half)
    ga_lo[...] = 0.5 * jnp.dot(w_ref[0], b_half[...], preferred_element_type=jnp.float32)


def last_call(w, b_blocks):
    rows, features = b_blocks[0].shape
    half = 4 * rows
    return pl.pallas_call(
        last_kernel,
        in_specs=[vmem_spec()] * 8,
        out_specs=vmem_spec(),
        out_shape=pltpu.VMEM((half, features), jnp.float32),
        scratch_shapes=[pltpu.VMEM((half, features), jnp.bfloat16)],
        compiler_params=params(),
        cost_estimate=cost(1, half, half, features),
        name="last",
    )(w, *b_blocks)


def near_kernel(ga_lo, got_lo, r_xy, r_yz, r_xz, p0, p1, p2, p4):
    rows = p0.shape[0]
    wide = lambda a: a.astype(jnp.float32)
    p0[...] = ga_lo[:rows] + (wide(got_lo[:rows]) + wide(got_lo[rows : 2 * rows]))
    part = lambda j: ga_lo[j * rows : (j + 1) * rows, :] + wide(got_lo[(j + 1) * rows : (j + 2) * rows, :])
    p1[...] = (part(1) + wide(r_xz[...])).astype(jnp.bfloat16)
    p2[...] = (part(2) + wide(r_xy[...])).astype(jnp.bfloat16)
    p4[...] = (part(3) + wide(r_yz[...])).astype(jnp.bfloat16)


def near_call(ga_lo, got_lo, *received):
    rows, features = received[0].shape
    narrow = jax.ShapeDtypeStruct((rows, features), jnp.bfloat16)
    return pl.pallas_call(
        near_kernel,
        in_specs=[vmem_spec()] * 5,
        out_specs=[vmem_spec()] * 4,
        out_shape=[pltpu.VMEM((rows, features), jnp.float32)] + [narrow] * 3,
        compiler_params=params(),
        cost_estimate=cost(0, 4 * rows, features, 1, 12),
        name="near",
    )(ga_lo, got_lo, *received)


def body(images, texts):
    rows, features = images.shape
    scale = 4.0 / math.sqrt(features) * LOG2E
    core = lax.axis_index("core")
    first = core == 0
    in_hbm = lambda a: pltpu.with_memory_space_constraint(a, pltpu.HBM)
    got = swap(images), swap(texts)
    own, other = own_call(*load_call(in_hbm(images), in_hbm(texts)), *got)
    near = {m: to_cube(own, m) for m in (4, 2, 1)}
    late = lax.optimization_barrier((own, near[1]))[0]
    far = {7: to_cube(late, 7), 5: to_cube(near[1], 4), 3: to_cube(near[2], 1), 6: to_cube(near[4], 2)}
    blocks = {0: own, **near, **far}
    in_vmem = lambda a: pltpu.with_memory_space_constraint(a, pltpu.VMEM)
    a_blocks = [in_vmem(blocks[m]) for m in ORDER]
    swapped = {m: swap(far[m]) for m in (7, 5, 3)}
    joined = [swap(a) for a in join_call(near[1], near[2], near[4])]
    last, *held = lax.optimization_barrier((far[6], swapped[7], swapped[5], swapped[3], *joined))
    swapped.update(zip((7, 5, 3), held))
    swapped[6] = swap(last)
    b_blocks = [other] + held[3:] + [swapped[m] for m in ORDER[4:]]
    b_blocks = [in_vmem(b) for b in b_blocks]

    e, a_stat, b_stat, flags = scores_call(a_blocks, b_blocks, scale)
    a_lse = merge_call(a_stat, swap(b_stat), 0)
    for m in (1, 2, 4):
        a_lse = merge_call(a_lse, to_cube(a_lse, m), m)
    b_lse = swap(a_lse)

    w, gb_hi = weights_call(flags, e, a_lse, b_lse, a_blocks)
    got_hi = swap(gb_hi)
    ga_hi, gb_lo = middle_call(w, a_blocks, b_blocks)
    got_lo = swap(gb_lo)
    p = dict(zip(ORDER[4:], far_call(ga_hi, got_hi)))
    from_xy = to_cube(p[3], 1)
    from_yz = to_cube(p[6], 2)
    from_xz = to_cube(p[5], 4)
    from_xyz = to_cube(p[7], 7)
    ga_lo = last_call(w, b_blocks)
    p0, p1, p2, p4 = near_call(ga_lo, got_lo, from_xy, from_yz, from_xz)
    wide = lambda a: a.astype(jnp.float32)
    total = p0 + wide(from_xyz) + wide(to_cube(p1, 1)) + wide(to_cube(p2, 2)) + wide(to_cube(p4, 4))
    kept, sent = total[:rows], total[rows:]
    got_sum = swap(sent)
    image_sum = jnp.where(first, kept, got_sum)
    text_sum = jnp.where(first, got_sum, kept)
    return (image_sum - wide(texts), text_sum - wide(images))


def solution(mesh):
    chips = Mesh(mesh.devices.reshape(SIZES), AXES)
    spec = P(AXES, None)
    return jax.shard_map(
        body,
        mesh=chips,
        in_specs=(spec, spec),
        out_specs=(spec, spec),
        check_vma=False,
    )
```

```python
import functools
import math

import jax
import jax.numpy as jnp
from jax import lax
from jax.experimental import pallas as pl
from jax.experimental.pallas import tpu as pltpu
from jax.sharding import Mesh, PartitionSpec as P

AXES = ("y", "core", "x", "z")
SIZES = (4, 2, 4, 4)
ORDER = (0, 1, 2, 4, 3, 5, 6, 7)
PLACE = tuple(ORDER.index(m) for m in range(8))
LOG2E = 1.4426950408889634
VMEM_LIMIT = 12 * 1024 * 1024
RANGE = 80.0


def flat(y, c, x, z):
    return ((y * 2 + c) * 4 + x) * 4 + z


def coords():
    for y in range(4):
        for c in range(2):
            for x in range(4):
                for z in range(4):
                    yield y, c, x, z


def partner(v, wrapped):
    return 3 - v if wrapped else v ^ 1


def across(m):
    pairs = []
    for y, c, x, z in coords():
        target = (
            partner(y, c == 1) if m & 2 else y,
            c,
            partner(x, c == 0) if m & 1 else x,
            partner(z, c == 1) if m & 4 else z,
        )
        pairs.append((flat(y, c, x, z), flat(*target)))
    return pairs


SWAP = [(flat(y, c, x, z), flat(y, 1 - c, x, z)) for y, c, x, z in coords()]


def to_cube(a, m):
    return lax.ppermute(a, AXES, across(m))


def swap(a):
    return lax.ppermute(a, AXES, SWAP)


def column_of(row, rows):
    padded = -(-rows // 128) * 128
    wide = jnp.broadcast_to(row, (128, rows))
    if padded != rows:
        wide = jnp.concatenate([wide, jnp.zeros((128, padded - rows), jnp.float32)], axis=1)
    return wide.T[:rows, :1]


def row_of(column, rows):
    padded = -(-rows // 128) * 128
    wide = jnp.broadcast_to(column, (rows, 128))
    if padded != rows:
        wide = jnp.concatenate([wide, jnp.zeros((padded - rows, 128), jnp.float32)], axis=0)
    return wide.T[:1, :rows]


def vmem_spec():
    return pl.BlockSpec(memory_space=pltpu.VMEM)


def smem_spec():
    return pl.BlockSpec(memory_space=pltpu.SMEM)


def cost(matmuls, rows, cols, depth, passes=0):
    return pl.CostEstimate(
        flops=2 * matmuls * rows * cols * depth, bytes_accessed=passes * rows * cols, transcendentals=0
    )


def params():
    return pltpu.CompilerParams(vmem_limit_bytes=VMEM_LIMIT)


def dot_nt(a, b):
    return lax.dot_general(a, b, (((1,), (1,)), ((), ())), preferred_element_type=jnp.float32)


def dot_tn(a, b):
    return lax.dot_general(a, b, (((0,), (0,)), ((), ())), preferred_element_type=jnp.float32)


def load_kernel(images, texts, mine, yours, sem):
    core = lax.axis_index("core")
    for c, order in enumerate(((mine, yours), (yours, mine))):

        @pl.when(core == c)
        def _():
            copies = [pltpu.make_async_copy(a, o, sem.at[j]) for j, (a, o) in enumerate(zip((images, texts), order))]
            for copy in copies:
                copy.start()
            for copy in copies:
                copy.wait()


def load_call(images, texts):
    block = pltpu.VMEM(images.shape, images.dtype)
    return pl.pallas_call(
        load_kernel,
        in_specs=[pl.BlockSpec(memory_space=pl.ANY)] * 2,
        out_specs=[vmem_spec()] * 2,
        out_shape=[block, block],
        scratch_shapes=[pltpu.SemaphoreType.DMA((2,))],
        compiler_params=params(),
        cost_estimate=cost(0, images.shape[0], images.shape[1], 1, 32),
        name="load",
    )(images, texts)


def own_kernel(mine, yours, got_images, got_texts, own, other):
    rows = mine.shape[0]
    own[:rows] = mine[...]
    other[rows:] = yours[...]
    for c, (low, top) in enumerate(((got_images, got_texts), (got_texts, got_images))):

        @pl.when(lax.axis_index("core") == c)
        def _():
            own[rows:] = low[...]
            other[:rows] = top[...]


def own_call(*parts):
    rows, features = parts[0].shape
    block = pltpu.VMEM((2 * rows, features), parts[0].dtype)
    return pl.pallas_call(
        own_kernel,
        in_specs=[vmem_spec()] * 4,
        out_specs=[vmem_spec()] * 2,
        out_shape=[block, block],
        compiler_params=params(),
        cost_estimate=cost(0, rows, features, 1, 16),
        name="own",
    )(*parts)


def join_kernel(b0, b1, b2, out0, out1):
    rows = b0.shape[0]
    cut = rows // 2
    out0[:rows] = b0[...]
    out0[rows:] = b1[:cut]
    out1[:cut] = b1[cut:]
    out1[cut:] = b2[...]


def join_call(*parts):
    rows, features = parts[0].shape
    out = jax.ShapeDtypeStruct((3 * rows // 2, features), parts[0].dtype)
    return pl.pallas_call(
        join_kernel,
        in_specs=[vmem_spec()] * 3,
        out_specs=[vmem_spec()] * 2,
        out_shape=[out, out],
        compiler_params=params(),
        cost_estimate=cost(0, 3 * rows, features, 1, 4),
        name="join",
    )(*parts)


def take_half(core, halves, shift, out):
    for c in range(2):

        @pl.when(core == c)
        def _():
            at = 0
            for part in halves[c ^ shift]:
                out[at : at + part.shape[0], :] = part[...]
                at += part.shape[0]


def a_halves(refs):
    return refs[:4], refs[4:8]


def b_halves(refs):
    return refs[:3], refs[3:7]


def scores_kernel(scale, *refs):
    a_refs, b_refs = refs[:8], b_halves(refs[8:15])
    e_ref, a_stat, b_stat, flags, a_cat, b_cat, col_m, col_s = refs[15:]
    rows = a_refs[0].shape[0]
    half = 4 * rows
    core = lax.axis_index("core")
    for q in range(2):
        take_half(core, b_refs, q, b_cat.at[q])

    def quadrant(q):
        b_half = b_cat[q]
        sums = []
        col = None
        for r in range(4):
            sl = slice(r * rows, (r + 1) * rows)
            e = jnp.exp2(dot_nt(a_refs[4 * q + r][...], b_half) * scale)
            e_ref[q, sl, :] = e
            sums.append(jnp.sum(e, axis=1, keepdims=True))
            part = jnp.sum(e, axis=0, keepdims=True)
            col = part if col is None else col + part
        row_lse = jnp.log2(row_of(jnp.concatenate(sums, axis=0), half))
        col_lse = jnp.log2(col)
        for j in range(4):
            sl = slice(j * rows, (j + 1) * rows)
            a_stat[4 * q + j : 4 * q + j + 1, :] = row_lse[:, sl]
            b_stat[pl.ds((q ^ core) * 4 + j, 1), :] = col_lse[:, sl]
        return jnp.maximum(jnp.abs(row_lse), jnp.abs(col_lse))

    def by_maxima(q):
        for r in range(4):
            a_cat[r * rows : (r + 1) * rows, :] = a_refs[4 * q + r][...]
        col_m[...] = jnp.full_like(col_m, -jnp.inf)
        col_s[...] = jnp.zeros_like(col_s)

        @pl.loop(0, 4)
        def _(r):
            sl = pl.ds(pl.multiple_of(r * rows, 16), rows)
            s = dot_nt(a_cat[sl, :], b_cat[q]) * scale
            e_ref[q, sl, :] = s
            row_m = jnp.max(s, axis=1, keepdims=True)
            row_s = jnp.sum(jnp.exp2(s - row_m), axis=1, keepdims=True)
            a_stat[pl.ds(4 * q + r, 1), :] = row_of(row_m + jnp.log2(row_s), rows)
            blk_m = jnp.max(s, axis=0, keepdims=True)
            blk_s = jnp.sum(jnp.exp2(s - blk_m), axis=0, keepdims=True)
            before = col_m[...]
            top = jnp.maximum(before, blk_m)
            col_s[...] = col_s[...] * jnp.exp2(before - top) + blk_s * jnp.exp2(blk_m - top)
            col_m[...] = top

        lse = col_m[...] + jnp.log2(col_s[...])
        for j in range(4):
            b_stat[pl.ds((q ^ core) * 4 + j, 1), :] = lse[:, j * rows : (j + 1) * rows]

    bad = jnp.logical_not(jnp.max(jnp.maximum(quadrant(0), quadrant(1))) <= RANGE)
    flags[0] = bad.astype(jnp.int32)
    flags[1] = bad.astype(jnp.int32)

    @pl.when(bad)
    def _():
        by_maxima(0)
        by_maxima(1)


def scores_call(a_blocks, b_blocks, scale):
    rows, features = a_blocks[0].shape
    half = 4 * rows
    stat = jax.ShapeDtypeStruct((8, rows), jnp.float32)
    return pl.pallas_call(
        functools.partial(scores_kernel, scale),
        in_specs=[vmem_spec()] * 15,
        out_specs=[vmem_spec()] * 3 + [smem_spec()],
        out_shape=[
            pltpu.VMEM((2, half, half), jnp.float32),
            stat,
            stat,
            jax.ShapeDtypeStruct((2,), jnp.int32),
        ],
        scratch_shapes=[
            pltpu.VMEM((half, features), jnp.bfloat16),
            pltpu.VMEM((2, half, features), jnp.bfloat16),
            pltpu.VMEM((1, half), jnp.float32),
            pltpu.VMEM((1, half), jnp.float32),
        ],
        compiler_params=params(),
        cost_estimate=cost(2, half, half, features),
        name="scores",
    )(*a_blocks, *b_blocks)


def merge_kernel(m, mine_ref, got_ref, out_ref):
    for k in range(8):
        j = PLACE[ORDER[k] ^ m]
        mine, got = mine_ref[k : k + 1, :], got_ref[j : j + 1, :]
        top = jnp.maximum(mine, got)
        out_ref[k : k + 1, :] = top + jnp.log2(jnp.exp2(mine - top) + jnp.exp2(got - top))


def merge_call(mine, got, m):
    return pl.pallas_call(
        functools.partial(merge_kernel, m),
        in_specs=[vmem_spec()] * 2,
        out_specs=vmem_spec(),
        out_shape=jax.ShapeDtypeStruct(mine.shape, jnp.float32),
        compiler_params=pltpu.CompilerParams(vmem_limit_bytes=2 * 1024 * 1024),
        name="merge",
    )(mine, got)


def weights_kernel(flags, e_ref, a_lse, b_lse, *refs):
    a_refs, (w_ref, gb_hi, a_half) = refs[:8], refs[8:]
    rows = a_lse.shape[1]
    half = 4 * rows
    core = lax.axis_index("core")
    take_half(core, a_halves(a_refs), 1, a_half)
    for q in range(2):
        a_row = jnp.concatenate([a_lse[4 * q + j : 4 * q + j + 1, :] for j in range(4)], axis=1)
        b_row = jnp.concatenate([b_lse[pl.ds((q ^ core) * 4 + j, 1), :] for j in range(4)], axis=1)

        @pl.when(flags[q] == 0)
        def _():
            a_col = column_of(jnp.exp2(-a_row), half)
            b_exp = jnp.exp2(-b_row)
            for r in range(4):
                sl = slice(r * rows, (r + 1) * rows)
                w_ref[q, sl, :] = (e_ref[q, sl, :] * (a_col[sl, :] + b_exp)).astype(jnp.bfloat16)

        @pl.when(flags[q] != 0)
        def _():
            a_col = column_of(a_row, half)
            for r in range(4):
                sl = slice(r * rows, (r + 1) * rows)
                s = e_ref[q, sl, :]
                w_ref[q, sl, :] = (jnp.exp2(s - a_col[sl, :]) + jnp.exp2(s - b_row)).astype(jnp.bfloat16)

    gb_hi[...] = (0.5 * dot_tn(w_ref[1 - core], a_half[...])).astype(jnp.bfloat16)


def weights_call(flags, e, a_lse, b_lse, a_blocks):
    rows, features = a_blocks[0].shape
    half = 4 * rows
    return pl.pallas_call(
        weights_kernel,
        in_specs=[smem_spec()] + [vmem_spec()] * 11,
        out_specs=[vmem_spec()] * 2,
        out_shape=[
            pltpu.VMEM((2, half, half), jnp.bfloat16),
            jax.ShapeDtypeStruct((half, features), jnp.bfloat16),
        ],
        scratch_shapes=[pltpu.VMEM((half, features), jnp.bfloat16)],
        compiler_params=params(),
        cost_estimate=cost(1, half, half, features, 12),
        name="weights",
    )(flags, e, a_lse, b_lse, *a_blocks)


def middle_kernel(w_ref, *refs):
    a_refs, b_refs = refs[:8], b_halves(refs[8:15])
    ga_hi, gb_lo, a_half, b_half = refs[15:]
    rows = a_refs[0].shape[0]
    core = lax.axis_index("core")
    take_half(core, a_halves(a_refs), 0, a_half)
    take_half(core, b_refs, 1, b_half)
    g = 0.5 * dot_tn(w_ref[core], a_half[...])
    high = g[:rows].astype(jnp.bfloat16)
    gb_lo[:rows] = high
    gb_lo[rows : 2 * rows] = (g[:rows] - high.astype(jnp.float32)).astype(jnp.bfloat16)
    gb_lo[2 * rows :] = g[rows:].astype(jnp.bfloat16)
    ga_hi[...] = 0.5 * jnp.dot(w_ref[1], b_half[...], preferred_element_type=jnp.float32)


def middle_call(w, a_blocks, b_blocks):
    rows, features = a_blocks[0].shape
    half = 4 * rows
    return pl.pallas_call(
        middle_kernel,
        in_specs=[vmem_spec()] * 16,
        out_specs=[vmem_spec()] * 2,
        out_shape=[
            pltpu.VMEM((half, features), jnp.float32),
            jax.ShapeDtypeStruct((half + rows, features), jnp.bfloat16),
        ],
        scratch_shapes=[pltpu.VMEM((half, features), jnp.bfloat16)] * 2,
        compiler_params=params(),
        cost_estimate=cost(2, half, half, features),
        name="middle",
    )(w, *a_blocks, *b_blocks)


def far_kernel(ga_hi, got, *outs):
    rows = outs[0].shape[0]
    for j in range(4):
        sl = slice(j * rows, (j + 1) * rows)
        outs[j][...] = (ga_hi[sl, :] + got[sl, :].astype(jnp.float32)).astype(jnp.bfloat16)


def far_call(ga_hi, got):
    half, features = ga_hi.shape
    rows = half // 4
    return pl.pallas_call(
        far_kernel,
        in_specs=[vmem_spec()] * 2,
        out_specs=[vmem_spec()] * 4,
        out_shape=[jax.ShapeDtypeStruct((rows, features), jnp.bfloat16)] * 4,
        compiler_params=params(),
        cost_estimate=cost(0, half, features, 1, 8),
        name="far",
    )(ga_hi, got)


def last_kernel(w_ref, *refs):
    b_refs, (ga_lo, b_half) = b_halves(refs[:7]), refs[7:]
    take_half(lax.axis_index("core"), b_refs, 0, b_half)
    ga_lo[...] = 0.5 * jnp.dot(w_ref[0], b_half[...], preferred_element_type=jnp.float32)


def last_call(w, b_blocks):
    rows, features = b_blocks[0].shape
    half = 4 * rows
    return pl.pallas_call(
        last_kernel,
        in_specs=[vmem_spec()] * 8,
        out_specs=vmem_spec(),
        out_shape=pltpu.VMEM((half, features), jnp.float32),
        scratch_shapes=[pltpu.VMEM((half, features), jnp.bfloat16)],
        compiler_params=params(),
        cost_estimate=cost(1, half, half, features),
        name="last",
    )(w, *b_blocks)


def near_kernel(ga_lo, got_lo, r_xy, r_yz, r_xz, p0, p1, p2, p4):
    rows = p0.shape[0]
    wide = lambda a: a.astype(jnp.float32)
    p0[...] = ga_lo[:rows] + (wide(got_lo[:rows]) + wide(got_lo[rows : 2 * rows]))
    part = lambda j: ga_lo[j * rows : (j + 1) * rows, :] + wide(got_lo[(j + 1) * rows : (j + 2) * rows, :])
    p1[...] = (part(1) + wide(r_xz[...])).astype(jnp.bfloat16)
    p2[...] = (part(2) + wide(r_xy[...])).astype(jnp.bfloat16)
    p4[...] = (part(3) + wide(r_yz[...])).astype(jnp.bfloat16)


def near_call(ga_lo, got_lo, *received):
    rows, features = received[0].shape
    narrow = jax.ShapeDtypeStruct((rows, features), jnp.bfloat16)
    return pl.pallas_call(
        near_kernel,
        in_specs=[vmem_spec()] * 5,
        out_specs=[vmem_spec()] * 4,
        out_shape=[pltpu.VMEM((rows, features), jnp.float32)] + [narrow] * 3,
        compiler_params=params(),
        cost_estimate=cost(0, 4 * rows, features, 1, 12),
        name="near",
    )(ga_lo, got_lo, *received)


def body(images, texts):
    rows, features = images.shape
    scale = 4.0 / math.sqrt(features) * LOG2E
    core = lax.axis_index("core")
    first = core == 0
    in_hbm = lambda a: pltpu.with_memory_space_constraint(a, pltpu.HBM)
    got = swap(images), swap(texts)
    own, other = own_call(*load_call(in_hbm(images), in_hbm(texts)), *got)
    near = {m: to_cube(own, m) for m in (4, 2, 1)}
    late = lax.optimization_barrier((own, near[1]))[0]
    far = {7: to_cube(late, 7), 5: to_cube(near[1], 4), 3: to_cube(near[2], 1), 6: to_cube(near[4], 2)}
    blocks = {0: own, **near, **far}
    in_vmem = lambda a: pltpu.with_memory_space_constraint(a, pltpu.VMEM)
    a_blocks = [in_vmem(blocks[m]) for m in ORDER]
    swapped = {m: swap(far[m]) for m in (7, 5, 3)}
    joined = [swap(a) for a in join_call(near[1], near[2], near[4])]
    last, *held = lax.optimization_barrier((far[6], swapped[7], swapped[5], swapped[3], *joined))
    swapped.update(zip((7, 5, 3), held))
    swapped[6] = swap(last)
    b_blocks = [other] + held[3:] + [swapped[m] for m in ORDER[4:]]
    b_blocks = [in_vmem(b) for b in b_blocks]

    e, a_stat, b_stat, flags = scores_call(a_blocks, b_blocks, scale)
    a_lse = merge_call(a_stat, swap(b_stat), 0)
    for m in (1, 2, 4):
        a_lse = merge_call(a_lse, to_cube(a_lse, m), m)
    b_lse = swap(a_lse)

    w, gb_hi = weights_call(flags, e, a_lse, b_lse, a_blocks)
    got_hi = swap(gb_hi)
    ga_hi, gb_lo = middle_call(w, a_blocks, b_blocks)
    got_lo = swap(gb_lo)
    p = dict(zip(ORDER[4:], far_call(ga_hi, got_hi)))
    from_xy = to_cube(p[3], 1)
    from_yz = to_cube(p[6], 2)
    from_xz = to_cube(p[5], 4)
    from_xyz = to_cube(p[7], 7)
    ga_lo = last_call(w, b_blocks)
    p0, p1, p2, p4 = near_call(ga_lo, got_lo, from_xy, from_yz, from_xz)
    wide = lambda a: a.astype(jnp.float32)
    total = p0 + wide(from_xyz) + wide(to_cube(p1, 1)) + wide(to_cube(p2, 2)) + wide(to_cube(p4, 4))
    kept, sent = total[:rows], total[rows:]
    got_sum = swap(sent)
    image_sum = jnp.where(first, kept, got_sum)
    text_sum = jnp.where(first, got_sum, kept)
    return (image_sum - wide(texts), text_sum - wide(images))


def solution(mesh):
    chips = Mesh(mesh.devices.reshape(SIZES), AXES)
    spec = P(AXES, None)
    return jax.shard_map(
        body,
        mesh=chips,
        in_specs=(spec, spec),
        out_specs=(spec, spec),
        check_vma=False,
    )
```

```python
import functools
import math

import jax
import jax.numpy as jnp
from jax import lax
from jax.experimental import pallas as pl
from jax.experimental.pallas import tpu as pltpu
from jax.sharding import Mesh, PartitionSpec as P

AXES = ("y", "core", "x", "z")
SIZES = (4, 2, 4, 4)
ORDER = (0, 1, 2, 4, 3, 5, 6, 7)
PLACE = tuple(ORDER.index(m) for m in range(8))
LOG2E = 1.4426950408889634
VMEM_LIMIT = 12 * 1024 * 1024
RANGE = 80.0


def flat(y, c, x, z):
    return ((y * 2 + c) * 4 + x) * 4 + z


def coords():
    for y in range(4):
        for c in range(2):
            for x in range(4):
                for z in range(4):
                    yield y, c, x, z


def partner(v, wrapped):
    return 3 - v if wrapped else v ^ 1


def across(m):
    pairs = []
    for y, c, x, z in coords():
        target = (
            partner(y, c == 1) if m & 2 else y,
            c,
            partner(x, c == 1) if m & 1 else x,
            partner(z, c == 0) if m & 4 else z,
        )
        pairs.append((flat(y, c, x, z), flat(*target)))
    return pairs


SWAP = [(flat(y, c, x, z), flat(y, 1 - c, x, z)) for y, c, x, z in coords()]


def to_cube(a, m):
    return lax.ppermute(a, AXES, across(m))


def swap(a):
    return lax.ppermute(a, AXES, SWAP)


def column_of(row, rows):
    padded = -(-rows // 128) * 128
    wide = jnp.broadcast_to(row, (128, rows))
    if padded != rows:
        wide = jnp.concatenate([wide, jnp.zeros((128, padded - rows), jnp.float32)], axis=1)
    return wide.T[:rows, :1]


def row_of(column, rows):
    padded = -(-rows // 128) * 128
    wide = jnp.broadcast_to(column, (rows, 128))
    if padded != rows:
        wide = jnp.concatenate([wide, jnp.zeros((padded - rows, 128), jnp.float32)], axis=0)
    return wide.T[:1, :rows]


def vmem_spec():
    return pl.BlockSpec(memory_space=pltpu.VMEM)


def smem_spec():
    return pl.BlockSpec(memory_space=pltpu.SMEM)


def cost(matmuls, rows, cols, depth, passes=0):
    return pl.CostEstimate(
        flops=2 * matmuls * rows * cols * depth, bytes_accessed=passes * rows * cols, transcendentals=0
    )


def params():
    return pltpu.CompilerParams(vmem_limit_bytes=VMEM_LIMIT)


def dot_nt(a, b):
    return lax.dot_general(a, b, (((1,), (1,)), ((), ())), preferred_element_type=jnp.float32)


def dot_tn(a, b):
    return lax.dot_general(a, b, (((0,), (0,)), ((), ())), preferred_element_type=jnp.float32)


def load_kernel(images, texts, mine, yours, sem):
    core = lax.axis_index("core")
    for c, order in enumerate(((mine, yours), (yours, mine))):

        @pl.when(core == c)
        def _():
            copies = [pltpu.make_async_copy(a, o, sem.at[j]) for j, (a, o) in enumerate(zip((images, texts), order))]
            for copy in copies:
                copy.start()
            for copy in copies:
                copy.wait()


def load_call(images, texts):
    block = pltpu.VMEM(images.shape, images.dtype)
    return pl.pallas_call(
        load_kernel,
        in_specs=[pl.BlockSpec(memory_space=pl.ANY)] * 2,
        out_specs=[vmem_spec()] * 2,
        out_shape=[block, block],
        scratch_shapes=[pltpu.SemaphoreType.DMA((2,))],
        compiler_params=params(),
        cost_estimate=cost(0, images.shape[0], images.shape[1], 1, 32),
        name="load",
    )(images, texts)


def own_kernel(mine, yours, got_images, got_texts, own, other):
    rows = mine.shape[0]
    own[:rows] = mine[...]
    other[rows:] = yours[...]
    for c, (low, top) in enumerate(((got_images, got_texts), (got_texts, got_images))):

        @pl.when(lax.axis_index("core") == c)
        def _():
            own[rows:] = low[...]
            other[:rows] = top[...]


def own_call(*parts):
    rows, features = parts[0].shape
    block = pltpu.VMEM((2 * rows, features), parts[0].dtype)
    return pl.pallas_call(
        own_kernel,
        in_specs=[vmem_spec()] * 4,
        out_specs=[vmem_spec()] * 2,
        out_shape=[block, block],
        compiler_params=params(),
        cost_estimate=cost(0, rows, features, 1, 16),
        name="own",
    )(*parts)


def join_kernel(b0, b1, b2, out0, out1):
    rows = b0.shape[0]
    cut = rows // 2
    out0[:rows] = b0[...]
    out0[rows:] = b1[:cut]
    out1[:cut] = b1[cut:]
    out1[cut:] = b2[...]


def join_call(*parts):
    rows, features = parts[0].shape
    out = jax.ShapeDtypeStruct((3 * rows // 2, features), parts[0].dtype)
    return pl.pallas_call(
        join_kernel,
        in_specs=[vmem_spec()] * 3,
        out_specs=[vmem_spec()] * 2,
        out_shape=[out, out],
        compiler_params=params(),
        cost_estimate=cost(0, 3 * rows, features, 1, 4),
        name="join",
    )(*parts)


def take_half(core, halves, shift, out):
    for c in range(2):

        @pl.when(core == c)
        def _():
            at = 0
            for part in halves[c ^ shift]:
                out[at : at + part.shape[0], :] = part[...]
                at += part.shape[0]


def a_halves(refs):
    return refs[:4], refs[4:8]


def b_halves(refs):
    return refs[:3], refs[3:7]


def scores_kernel(scale, *refs):
    a_refs, b_refs = refs[:8], b_halves(refs[8:15])
    e_ref, a_stat, b_stat, flags, a_cat, b_cat, col_m, col_s = refs[15:]
    rows = a_refs[0].shape[0]
    half = 4 * rows
    core = lax.axis_index("core")
    for q in range(2):
        take_half(core, b_refs, q, b_cat.at[q])

    def quadrant(q):
        b_half = b_cat[q]
        sums = []
        col = None
        for r in range(4):
            sl = slice(r * rows, (r + 1) * rows)
            e = jnp.exp2(dot_nt(a_refs[4 * q + r][...], b_half) * scale)
            e_ref[q, sl, :] = e
            sums.append(jnp.sum(e, axis=1, keepdims=True))
            part = jnp.sum(e, axis=0, keepdims=True)
            col = part if col is None else col + part
        row_lse = jnp.log2(row_of(jnp.concatenate(sums, axis=0), half))
        col_lse = jnp.log2(col)
        for j in range(4):
            sl = slice(j * rows, (j + 1) * rows)
            a_stat[4 * q + j : 4 * q + j + 1, :] = row_lse[:, sl]
            b_stat[pl.ds((q ^ core) * 4 + j, 1), :] = col_lse[:, sl]
        return jnp.maximum(jnp.abs(row_lse), jnp.abs(col_lse))

    def by_maxima(q):
        for r in range(4):
            a_cat[r * rows : (r + 1) * rows, :] = a_refs[4 * q + r][...]
        col_m[...] = jnp.full_like(col_m, -jnp.inf)
        col_s[...] = jnp.zeros_like(col_s)

        @pl.loop(0, 4)
        def _(r):
            sl = pl.ds(pl.multiple_of(r * rows, 16), rows)
            s = dot_nt(a_cat[sl, :], b_cat[q]) * scale
            e_ref[q, sl, :] = s
            row_m = jnp.max(s, axis=1, keepdims=True)
            row_s = jnp.sum(jnp.exp2(s - row_m), axis=1, keepdims=True)
            a_stat[pl.ds(4 * q + r, 1), :] = row_of(row_m + jnp.log2(row_s), rows)
            blk_m = jnp.max(s, axis=0, keepdims=True)
            blk_s = jnp.sum(jnp.exp2(s - blk_m), axis=0, keepdims=True)
            before = col_m[...]
            top = jnp.maximum(before, blk_m)
            col_s[...] = col_s[...] * jnp.exp2(before - top) + blk_s * jnp.exp2(blk_m - top)
            col_m[...] = top

        lse = col_m[...] + jnp.log2(col_s[...])
        for j in range(4):
            b_stat[pl.ds((q ^ core) * 4 + j, 1), :] = lse[:, j * rows : (j + 1) * rows]

    bad = jnp.logical_not(jnp.max(jnp.maximum(quadrant(0), quadrant(1))) <= RANGE)
    flags[0] = bad.astype(jnp.int32)
    flags[1] = bad.astype(jnp.int32)

    @pl.when(bad)
    def _():
        by_maxima(0)
        by_maxima(1)


def scores_call(a_blocks, b_blocks, scale):
    rows, features = a_blocks[0].shape
    half = 4 * rows
    stat = jax.ShapeDtypeStruct((8, rows), jnp.float32)
    return pl.pallas_call(
        functools.partial(scores_kernel, scale),
        in_specs=[vmem_spec()] * 15,
        out_specs=[vmem_spec()] * 3 + [smem_spec()],
        out_shape=[
            pltpu.VMEM((2, half, half), jnp.float32),
            stat,
            stat,
            jax.ShapeDtypeStruct((2,), jnp.int32),
        ],
        scratch_shapes=[
            pltpu.VMEM((half, features), jnp.bfloat16),
            pltpu.VMEM((2, half, features), jnp.bfloat16),
            pltpu.VMEM((1, half), jnp.float32),
            pltpu.VMEM((1, half), jnp.float32),
        ],
        compiler_params=params(),
        cost_estimate=cost(2, half, half, features),
        name="scores",
    )(*a_blocks, *b_blocks)


def merge_kernel(m, mine_ref, got_ref, out_ref):
    for k in range(8):
        j = PLACE[ORDER[k] ^ m]
        mine, got = mine_ref[k : k + 1, :], got_ref[j : j + 1, :]
        top = jnp.maximum(mine, got)
        out_ref[k : k + 1, :] = top + jnp.log2(jnp.exp2(mine - top) + jnp.exp2(got - top))


def merge_call(mine, got, m):
    return pl.pallas_call(
        functools.partial(merge_kernel, m),
        in_specs=[vmem_spec()] * 2,
        out_specs=vmem_spec(),
        out_shape=jax.ShapeDtypeStruct(mine.shape, jnp.float32),
        compiler_params=pltpu.CompilerParams(vmem_limit_bytes=2 * 1024 * 1024),
        name="merge",
    )(mine, got)


def weights_kernel(flags, e_ref, a_lse, b_lse, *refs):
    a_refs, (w_ref, gb_hi, a_half) = refs[:8], refs[8:]
    rows = a_lse.shape[1]
    half = 4 * rows
    core = lax.axis_index("core")
    take_half(core, a_halves(a_refs), 1, a_half)
    for q in range(2):
        a_row = jnp.concatenate([a_lse[4 * q + j : 4 * q + j + 1, :] for j in range(4)], axis=1)
        b_row = jnp.concatenate([b_lse[pl.ds((q ^ core) * 4 + j, 1), :] for j in range(4)], axis=1)

        @pl.when(flags[q] == 0)
        def _():
            a_col = column_of(jnp.exp2(-a_row), half)
            b_exp = jnp.exp2(-b_row)
            for r in range(4):
                sl = slice(r * rows, (r + 1) * rows)
                w_ref[q, sl, :] = (e_ref[q, sl, :] * (a_col[sl, :] + b_exp)).astype(jnp.bfloat16)

        @pl.when(flags[q] != 0)
        def _():
            a_col = column_of(a_row, half)
            for r in range(4):
                sl = slice(r * rows, (r + 1) * rows)
                s = e_ref[q, sl, :]
                w_ref[q, sl, :] = (jnp.exp2(s - a_col[sl, :]) + jnp.exp2(s - b_row)).astype(jnp.bfloat16)

    gb_hi[...] = (0.5 * dot_tn(w_ref[1 - core], a_half[...])).astype(jnp.bfloat16)


def weights_call(flags, e, a_lse, b_lse, a_blocks):
    rows, features = a_blocks[0].shape
    half = 4 * rows
    return pl.pallas_call(
        weights_kernel,
        in_specs=[smem_spec()] + [vmem_spec()] * 11,
        out_specs=[vmem_spec()] * 2,
        out_shape=[
            pltpu.VMEM((2, half, half), jnp.bfloat16),
            jax.ShapeDtypeStruct((half, features), jnp.bfloat16),
        ],
        scratch_shapes=[pltpu.VMEM((half, features), jnp.bfloat16)],
        compiler_params=params(),
        cost_estimate=cost(1, half, half, features, 12),
        name="weights",
    )(flags, e, a_lse, b_lse, *a_blocks)


def middle_kernel(w_ref, *refs):
    a_refs, b_refs = refs[:8], b_halves(refs[8:15])
    ga_hi, gb_lo, a_half, b_half = refs[15:]
    rows = a_refs[0].shape[0]
    core = lax.axis_index("core")
    take_half(core, a_halves(a_refs), 0, a_half)
    take_half(core, b_refs, 1, b_half)
    g = 0.5 * dot_tn(w_ref[core], a_half[...])
    high = g[:rows].astype(jnp.bfloat16)
    gb_lo[:rows] = high
    gb_lo[rows : 2 * rows] = (g[:rows] - high.astype(jnp.float32)).astype(jnp.bfloat16)
    gb_lo[2 * rows :] = g[rows:].astype(jnp.bfloat16)
    ga_hi[...] = 0.5 * jnp.dot(w_ref[1], b_half[...], preferred_element_type=jnp.float32)


def middle_call(w, a_blocks, b_blocks):
    rows, features = a_blocks[0].shape
    half = 4 * rows
    return pl.pallas_call(
        middle_kernel,
        in_specs=[vmem_spec()] * 16,
        out_specs=[vmem_spec()] * 2,
        out_shape=[
            pltpu.VMEM((half, features), jnp.float32),
            jax.ShapeDtypeStruct((half + rows, features), jnp.bfloat16),
        ],
        scratch_shapes=[pltpu.VMEM((half, features), jnp.bfloat16)] * 2,
        compiler_params=params(),
        cost_estimate=cost(2, half, half, features),
        name="middle",
    )(w, *a_blocks, *b_blocks)


def far_kernel(ga_hi, got, *outs):
    rows = outs[0].shape[0]
    for j in range(4):
        sl = slice(j * rows, (j + 1) * rows)
        outs[j][...] = (ga_hi[sl, :] + got[sl, :].astype(jnp.float32)).astype(jnp.bfloat16)


def far_call(ga_hi, got):
    half, features = ga_hi.shape
    rows = half // 4
    return pl.pallas_call(
        far_kernel,
        in_specs=[vmem_spec()] * 2,
        out_specs=[vmem_spec()] * 4,
        out_shape=[jax.ShapeDtypeStruct((rows, features), jnp.bfloat16)] * 4,
        compiler_params=params(),
        cost_estimate=cost(0, half, features, 1, 8),
        name="far",
    )(ga_hi, got)


def last_kernel(w_ref, *refs):
    b_refs, (ga_lo, b_half) = b_halves(refs[:7]), refs[7:]
    take_half(lax.axis_index("core"), b_refs, 0, b_half)
    ga_lo[...] = 0.5 * jnp.dot(w_ref[0], b_half[...], preferred_element_type=jnp.float32)


def last_call(w, b_blocks):
    rows, features = b_blocks[0].shape
    half = 4 * rows
    return pl.pallas_call(
        last_kernel,
        in_specs=[vmem_spec()] * 8,
        out_specs=vmem_spec(),
        out_shape=pltpu.VMEM((half, features), jnp.float32),
        scratch_shapes=[pltpu.VMEM((half, features), jnp.bfloat16)],
        compiler_params=params(),
        cost_estimate=cost(1, half, half, features),
        name="last",
    )(w, *b_blocks)


def near_kernel(ga_lo, got_lo, r_xy, r_yz, r_xz, p0, p1, p2, p4):
    rows = p0.shape[0]
    wide = lambda a: a.astype(jnp.float32)
    p0[...] = ga_lo[:rows] + (wide(got_lo[:rows]) + wide(got_lo[rows : 2 * rows]))
    part = lambda j: ga_lo[j * rows : (j + 1) * rows, :] + wide(got_lo[(j + 1) * rows : (j + 2) * rows, :])
    p1[...] = (part(1) + wide(r_xz[...])).astype(jnp.bfloat16)
    p2[...] = (part(2) + wide(r_xy[...])).astype(jnp.bfloat16)
    p4[...] = (part(3) + wide(r_yz[...])).astype(jnp.bfloat16)


def near_call(ga_lo, got_lo, *received):
    rows, features = received[0].shape
    narrow = jax.ShapeDtypeStruct((rows, features), jnp.bfloat16)
    return pl.pallas_call(
        near_kernel,
        in_specs=[vmem_spec()] * 5,
        out_specs=[vmem_spec()] * 4,
        out_shape=[pltpu.VMEM((rows, features), jnp.float32)] + [narrow] * 3,
        compiler_params=params(),
        cost_estimate=cost(0, 4 * rows, features, 1, 12),
        name="near",
    )(ga_lo, got_lo, *received)


def body(images, texts):
    rows, features = images.shape
    scale = 4.0 / math.sqrt(features) * LOG2E
    core = lax.axis_index("core")
    first = core == 0
    in_hbm = lambda a: pltpu.with_memory_space_constraint(a, pltpu.HBM)
    got = swap(images), swap(texts)
    own, other = own_call(*load_call(in_hbm(images), in_hbm(texts)), *got)
    near = {m: to_cube(own, m) for m in (4, 2, 1)}
    late = lax.optimization_barrier((own, near[1]))[0]
    far = {7: to_cube(late, 7), 5: to_cube(near[1], 4), 3: to_cube(near[2], 1), 6: to_cube(near[4], 2)}
    blocks = {0: own, **near, **far}
    in_vmem = lambda a: pltpu.with_memory_space_constraint(a, pltpu.VMEM)
    a_blocks = [in_vmem(blocks[m]) for m in ORDER]
    swapped = {m: swap(far[m]) for m in (7, 5, 3)}
    joined = [swap(a) for a in join_call(near[1], near[2], near[4])]
    last, *held = lax.optimization_barrier((far[6], swapped[7], swapped[5], swapped[3], *joined))
    swapped.update(zip((7, 5, 3), held))
    swapped[6] = swap(last)
    b_blocks = [other] + held[3:] + [swapped[m] for m in ORDER[4:]]
    b_blocks = [in_vmem(b) for b in b_blocks]

    e, a_stat, b_stat, flags = scores_call(a_blocks, b_blocks, scale)
    a_lse = merge_call(a_stat, swap(b_stat), 0)
    for m in (1, 2, 4):
        a_lse = merge_call(a_lse, to_cube(a_lse, m), m)
    b_lse = swap(a_lse)

    w, gb_hi = weights_call(flags, e, a_lse, b_lse, a_blocks)
    got_hi = swap(gb_hi)
    ga_hi, gb_lo = middle_call(w, a_blocks, b_blocks)
    got_lo = swap(gb_lo)
    p = dict(zip(ORDER[4:], far_call(ga_hi, got_hi)))
    from_xy = to_cube(p[3], 1)
    from_yz = to_cube(p[6], 2)
    from_xz = to_cube(p[5], 4)
    from_xyz = to_cube(p[7], 7)
    ga_lo = last_call(w, b_blocks)
    p0, p1, p2, p4 = near_call(ga_lo, got_lo, from_xy, from_yz, from_xz)
    wide = lambda a: a.astype(jnp.float32)
    total = p0 + wide(from_xyz) + wide(to_cube(p1, 1)) + wide(to_cube(p2, 2)) + wide(to_cube(p4, 4))
    kept, sent = total[:rows], total[rows:]
    got_sum = swap(sent)
    image_sum = jnp.where(first, kept, got_sum)
    text_sum = jnp.where(first, got_sum, kept)
    return (image_sum - wide(texts), text_sum - wide(images))


def solution(mesh):
    chips = Mesh(mesh.devices.reshape(SIZES), AXES)
    spec = P(AXES, None)
    return jax.shard_map(
        body,
        mesh=chips,
        in_specs=(spec, spec),
        out_specs=(spec, spec),
        check_vma=False,
    )
```

```python
import functools
import math

import jax
import jax.numpy as jnp
from jax import lax
from jax.experimental import pallas as pl
from jax.experimental.pallas import tpu as pltpu
from jax.sharding import Mesh, PartitionSpec as P

AXES = ("y", "core", "x", "z")
SIZES = (4, 2, 4, 4)
ORDER = (0, 1, 2, 4, 3, 5, 6, 7)
PLACE = tuple(ORDER.index(m) for m in range(8))
LOG2E = 1.4426950408889634
VMEM_LIMIT = 12 * 1024 * 1024
RANGE = 80.0


def flat(y, c, x, z):
    return ((y * 2 + c) * 4 + x) * 4 + z


def coords():
    for y in range(4):
        for c in range(2):
            for x in range(4):
                for z in range(4):
                    yield y, c, x, z


def partner(v, wrapped):
    return 3 - v if wrapped else v ^ 1


def across(m):
    pairs = []
    for y, c, x, z in coords():
        target = (
            partner(y, c == 0) if m & 2 else y,
            c,
            partner(x, c == 1) if m & 1 else x,
            partner(z, c == 1) if m & 4 else z,
        )
        pairs.append((flat(y, c, x, z), flat(*target)))
    return pairs


SWAP = [(flat(y, c, x, z), flat(y, 1 - c, x, z)) for y, c, x, z in coords()]


def to_cube(a, m):
    return lax.ppermute(a, AXES, across(m))


def swap(a):
    return lax.ppermute(a, AXES, SWAP)


def column_of(row, rows):
    padded = -(-rows // 128) * 128
    wide = jnp.broadcast_to(row, (128, rows))
    if padded != rows:
        wide = jnp.concatenate([wide, jnp.zeros((128, padded - rows), jnp.float32)], axis=1)
    return wide.T[:rows, :1]


def row_of(column, rows):
    padded = -(-rows // 128) * 128
    wide = jnp.broadcast_to(column, (rows, 128))
    if padded != rows:
        wide = jnp.concatenate([wide, jnp.zeros((padded - rows, 128), jnp.float32)], axis=0)
    return wide.T[:1, :rows]


def vmem_spec():
    return pl.BlockSpec(memory_space=pltpu.VMEM)


def smem_spec():
    return pl.BlockSpec(memory_space=pltpu.SMEM)


def cost(matmuls, rows, cols, depth, passes=0):
    return pl.CostEstimate(
        flops=2 * matmuls * rows * cols * depth, bytes_accessed=passes * rows * cols, transcendentals=0
    )


def params():
    return pltpu.CompilerParams(vmem_limit_bytes=VMEM_LIMIT)


def dot_nt(a, b):
    return lax.dot_general(a, b, (((1,), (1,)), ((), ())), preferred_element_type=jnp.float32)


def dot_tn(a, b):
    return lax.dot_general(a, b, (((0,), (0,)), ((), ())), preferred_element_type=jnp.float32)


def load_kernel(images, texts, mine, yours, sem):
    core = lax.axis_index("core")
    for c, order in enumerate(((mine, yours), (yours, mine))):

        @pl.when(core == c)
        def _():
            copies = [pltpu.make_async_copy(a, o, sem.at[j]) for j, (a, o) in enumerate(zip((images, texts), order))]
            for copy in copies:
                copy.start()
            for copy in copies:
                copy.wait()


def load_call(images, texts):
    block = pltpu.VMEM(images.shape, images.dtype)
    return pl.pallas_call(
        load_kernel,
        in_specs=[pl.BlockSpec(memory_space=pl.ANY)] * 2,
        out_specs=[vmem_spec()] * 2,
        out_shape=[block, block],
        scratch_shapes=[pltpu.SemaphoreType.DMA((2,))],
        compiler_params=params(),
        cost_estimate=cost(0, images.shape[0], images.shape[1], 1, 32),
        name="load",
    )(images, texts)


def own_kernel(mine, yours, got_images, got_texts, own, other):
    rows = mine.shape[0]
    own[:rows] = mine[...]
    other[rows:] = yours[...]
    for c, (low, top) in enumerate(((got_images, got_texts), (got_texts, got_images))):

        @pl.when(lax.axis_index("core") == c)
        def _():
            own[rows:] = low[...]
            other[:rows] = top[...]


def own_call(*parts):
    rows, features = parts[0].shape
    block = pltpu.VMEM((2 * rows, features), parts[0].dtype)
    return pl.pallas_call(
        own_kernel,
        in_specs=[vmem_spec()] * 4,
        out_specs=[vmem_spec()] * 2,
        out_shape=[block, block],
        compiler_params=params(),
        cost_estimate=cost(0, rows, features, 1, 16),
        name="own",
    )(*parts)


def join_kernel(b0, b1, b2, out0, out1):
    rows = b0.shape[0]
    cut = rows // 2
    out0[:rows] = b0[...]
    out0[rows:] = b1[:cut]
    out1[:cut] = b1[cut:]
    out1[cut:] = b2[...]


def join_call(*parts):
    rows, features = parts[0].shape
    out = jax.ShapeDtypeStruct((3 * rows // 2, features), parts[0].dtype)
    return pl.pallas_call(
        join_kernel,
        in_specs=[vmem_spec()] * 3,
        out_specs=[vmem_spec()] * 2,
        out_shape=[out, out],
        compiler_params=params(),
        cost_estimate=cost(0, 3 * rows, features, 1, 4),
        name="join",
    )(*parts)


def take_half(core, halves, shift, out):
    for c in range(2):

        @pl.when(core == c)
        def _():
            at = 0
            for part in halves[c ^ shift]:
                out[at : at + part.shape[0], :] = part[...]
                at += part.shape[0]


def a_halves(refs):
    return refs[:4], refs[4:8]


def b_halves(refs):
    return refs[:3], refs[3:7]


def scores_kernel(scale, *refs):
    a_refs, b_refs = refs[:8], b_halves(refs[8:15])
    e_ref, a_stat, b_stat, flags, a_cat, b_cat, col_m, col_s = refs[15:]
    rows = a_refs[0].shape[0]
    half = 4 * rows
    core = lax.axis_index("core")
    for q in range(2):
        take_half(core, b_refs, q, b_cat.at[q])

    def quadrant(q):
        b_half = b_cat[q]
        sums = []
        col = None
        for r in range(4):
            sl = slice(r * rows, (r + 1) * rows)
            e = jnp.exp2(dot_nt(a_refs[4 * q + r][...], b_half) * scale)
            e_ref[q, sl, :] = e
            sums.append(jnp.sum(e, axis=1, keepdims=True))
            part = jnp.sum(e, axis=0, keepdims=True)
            col = part if col is None else col + part
        row_lse = jnp.log2(row_of(jnp.concatenate(sums, axis=0), half))
        col_lse = jnp.log2(col)
        for j in range(4):
            sl = slice(j * rows, (j + 1) * rows)
            a_stat[4 * q + j : 4 * q + j + 1, :] = row_lse[:, sl]
            b_stat[pl.ds((q ^ core) * 4 + j, 1), :] = col_lse[:, sl]
        return jnp.maximum(jnp.abs(row_lse), jnp.abs(col_lse))

    def by_maxima(q):
        for r in range(4):
            a_cat[r * rows : (r + 1) * rows, :] = a_refs[4 * q + r][...]
        col_m[...] = jnp.full_like(col_m, -jnp.inf)
        col_s[...] = jnp.zeros_like(col_s)

        @pl.loop(0, 4)
        def _(r):
            sl = pl.ds(pl.multiple_of(r * rows, 16), rows)
            s = dot_nt(a_cat[sl, :], b_cat[q]) * scale
            e_ref[q, sl, :] = s
            row_m = jnp.max(s, axis=1, keepdims=True)
            row_s = jnp.sum(jnp.exp2(s - row_m), axis=1, keepdims=True)
            a_stat[pl.ds(4 * q + r, 1), :] = row_of(row_m + jnp.log2(row_s), rows)
            blk_m = jnp.max(s, axis=0, keepdims=True)
            blk_s = jnp.sum(jnp.exp2(s - blk_m), axis=0, keepdims=True)
            before = col_m[...]
            top = jnp.maximum(before, blk_m)
            col_s[...] = col_s[...] * jnp.exp2(before - top) + blk_s * jnp.exp2(blk_m - top)
            col_m[...] = top

        lse = col_m[...] + jnp.log2(col_s[...])
        for j in range(4):
            b_stat[pl.ds((q ^ core) * 4 + j, 1), :] = lse[:, j * rows : (j + 1) * rows]

    bad = jnp.logical_not(jnp.max(jnp.maximum(quadrant(0), quadrant(1))) <= RANGE)
    flags[0] = bad.astype(jnp.int32)
    flags[1] = bad.astype(jnp.int32)

    @pl.when(bad)
    def _():
        by_maxima(0)
        by_maxima(1)


def scores_call(a_blocks, b_blocks, scale):
    rows, features = a_blocks[0].shape
    half = 4 * rows
    stat = jax.ShapeDtypeStruct((8, rows), jnp.float32)
    return pl.pallas_call(
        functools.partial(scores_kernel, scale),
        in_specs=[vmem_spec()] * 15,
        out_specs=[vmem_spec()] * 3 + [smem_spec()],
        out_shape=[
            pltpu.VMEM((2, half, half), jnp.float32),
            stat,
            stat,
            jax.ShapeDtypeStruct((2,), jnp.int32),
        ],
        scratch_shapes=[
            pltpu.VMEM((half, features), jnp.bfloat16),
            pltpu.VMEM((2, half, features), jnp.bfloat16),
            pltpu.VMEM((1, half), jnp.float32),
            pltpu.VMEM((1, half), jnp.float32),
        ],
        compiler_params=params(),
        cost_estimate=cost(2, half, half, features),
        name="scores",
    )(*a_blocks, *b_blocks)


def merge_kernel(m, mine_ref, got_ref, out_ref):
    for k in range(8):
        j = PLACE[ORDER[k] ^ m]
        mine, got = mine_ref[k : k + 1, :], got_ref[j : j + 1, :]
        top = jnp.maximum(mine, got)
        out_ref[k : k + 1, :] = top + jnp.log2(jnp.exp2(mine - top) + jnp.exp2(got - top))


def merge_call(mine, got, m):
    return pl.pallas_call(
        functools.partial(merge_kernel, m),
        in_specs=[vmem_spec()] * 2,
        out_specs=vmem_spec(),
        out_shape=jax.ShapeDtypeStruct(mine.shape, jnp.float32),
        compiler_params=pltpu.CompilerParams(vmem_limit_bytes=2 * 1024 * 1024),
        name="merge",
    )(mine, got)


def weights_kernel(flags, e_ref, a_lse, b_lse, *refs):
    a_refs, (w_ref, gb_hi, a_half) = refs[:8], refs[8:]
    rows = a_lse.shape[1]
    half = 4 * rows
    core = lax.axis_index("core")
    take_half(core, a_halves(a_refs), 1, a_half)
    for q in range(2):
        a_row = jnp.concatenate([a_lse[4 * q + j : 4 * q + j + 1, :] for j in range(4)], axis=1)
        b_row = jnp.concatenate([b_lse[pl.ds((q ^ core) * 4 + j, 1), :] for j in range(4)], axis=1)

        @pl.when(flags[q] == 0)
        def _():
            a_col = column_of(jnp.exp2(-a_row), half)
            b_exp = jnp.exp2(-b_row)
            for r in range(4):
                sl = slice(r * rows, (r + 1) * rows)
                w_ref[q, sl, :] = (e_ref[q, sl, :] * (a_col[sl, :] + b_exp)).astype(jnp.bfloat16)

        @pl.when(flags[q] != 0)
        def _():
            a_col = column_of(a_row, half)
            for r in range(4):
                sl = slice(r * rows, (r + 1) * rows)
                s = e_ref[q, sl, :]
                w_ref[q, sl, :] = (jnp.exp2(s - a_col[sl, :]) + jnp.exp2(s - b_row)).astype(jnp.bfloat16)

    gb_hi[...] = (0.5 * dot_tn(w_ref[1 - core], a_half[...])).astype(jnp.bfloat16)


def weights_call(flags, e, a_lse, b_lse, a_blocks):
    rows, features = a_blocks[0].shape
    half = 4 * rows
    return pl.pallas_call(
        weights_kernel,
        in_specs=[smem_spec()] + [vmem_spec()] * 11,
        out_specs=[vmem_spec()] * 2,
        out_shape=[
            pltpu.VMEM((2, half, half), jnp.bfloat16),
            jax.ShapeDtypeStruct((half, features), jnp.bfloat16),
        ],
        scratch_shapes=[pltpu.VMEM((half, features), jnp.bfloat16)],
        compiler_params=params(),
        cost_estimate=cost(1, half, half, features, 12),
        name="weights",
    )(flags, e, a_lse, b_lse, *a_blocks)


def middle_kernel(w_ref, *refs):
    a_refs, b_refs = refs[:8], b_halves(refs[8:15])
    ga_hi, gb_lo, a_half, b_half = refs[15:]
    rows = a_refs[0].shape[0]
    core = lax.axis_index("core")
    take_half(core, a_halves(a_refs), 0, a_half)
    take_half(core, b_refs, 1, b_half)
    g = 0.5 * dot_tn(w_ref[core], a_half[...])
    high = g[:rows].astype(jnp.bfloat16)
    gb_lo[:rows] = high
    gb_lo[rows : 2 * rows] = (g[:rows] - high.astype(jnp.float32)).astype(jnp.bfloat16)
    gb_lo[2 * rows :] = g[rows:].astype(jnp.bfloat16)
    ga_hi[...] = 0.5 * jnp.dot(w_ref[1], b_half[...], preferred_element_type=jnp.float32)


def middle_call(w, a_blocks, b_blocks):
    rows, features = a_blocks[0].shape
    half = 4 * rows
    return pl.pallas_call(
        middle_kernel,
        in_specs=[vmem_spec()] * 16,
        out_specs=[vmem_spec()] * 2,
        out_shape=[
            pltpu.VMEM((half, features), jnp.float32),
            jax.ShapeDtypeStruct((half + rows, features), jnp.bfloat16),
        ],
        scratch_shapes=[pltpu.VMEM((half, features), jnp.bfloat16)] * 2,
        compiler_params=params(),
        cost_estimate=cost(2, half, half, features),
        name="middle",
    )(w, *a_blocks, *b_blocks)


def far_kernel(ga_hi, got, *outs):
    rows = outs[0].shape[0]
    for j in range(4):
        sl = slice(j * rows, (j + 1) * rows)
        outs[j][...] = (ga_hi[sl, :] + got[sl, :].astype(jnp.float32)).astype(jnp.bfloat16)


def far_call(ga_hi, got):
    half, features = ga_hi.shape
    rows = half // 4
    return pl.pallas_call(
        far_kernel,
        in_specs=[vmem_spec()] * 2,
        out_specs=[vmem_spec()] * 4,
        out_shape=[jax.ShapeDtypeStruct((rows, features), jnp.bfloat16)] * 4,
        compiler_params=params(),
        cost_estimate=cost(0, half, features, 1, 8),
        name="far",
    )(ga_hi, got)


def last_kernel(w_ref, *refs):
    b_refs, (ga_lo, b_half) = b_halves(refs[:7]), refs[7:]
    take_half(lax.axis_index("core"), b_refs, 0, b_half)
    ga_lo[...] = 0.5 * jnp.dot(w_ref[0], b_half[...], preferred_element_type=jnp.float32)


def last_call(w, b_blocks):
    rows, features = b_blocks[0].shape
    half = 4 * rows
    return pl.pallas_call(
        last_kernel,
        in_specs=[vmem_spec()] * 8,
        out_specs=vmem_spec(),
        out_shape=pltpu.VMEM((half, features), jnp.float32),
        scratch_shapes=[pltpu.VMEM((half, features), jnp.bfloat16)],
        compiler_params=params(),
        cost_estimate=cost(1, half, half, features),
        name="last",
    )(w, *b_blocks)


def near_kernel(ga_lo, got_lo, r_xy, r_yz, r_xz, p0, p1, p2, p4):
    rows = p0.shape[0]
    wide = lambda a: a.astype(jnp.float32)
    p0[...] = ga_lo[:rows] + (wide(got_lo[:rows]) + wide(got_lo[rows : 2 * rows]))
    part = lambda j: ga_lo[j * rows : (j + 1) * rows, :] + wide(got_lo[(j + 1) * rows : (j + 2) * rows, :])
    p1[...] = (part(1) + wide(r_xz[...])).astype(jnp.bfloat16)
    p2[...] = (part(2) + wide(r_xy[...])).astype(jnp.bfloat16)
    p4[...] = (part(3) + wide(r_yz[...])).astype(jnp.bfloat16)


def near_call(ga_lo, got_lo, *received):
    rows, features = received[0].shape
    narrow = jax.ShapeDtypeStruct((rows, features), jnp.bfloat16)
    return pl.pallas_call(
        near_kernel,
        in_specs=[vmem_spec()] * 5,
        out_specs=[vmem_spec()] * 4,
        out_shape=[pltpu.VMEM((rows, features), jnp.float32)] + [narrow] * 3,
        compiler_params=params(),
        cost_estimate=cost(0, 4 * rows, features, 1, 12),
        name="near",
    )(ga_lo, got_lo, *received)


def body(images, texts):
    rows, features = images.shape
    scale = 4.0 / math.sqrt(features) * LOG2E
    core = lax.axis_index("core")
    first = core == 0
    in_hbm = lambda a: pltpu.with_memory_space_constraint(a, pltpu.HBM)
    got = swap(images), swap(texts)
    own, other = own_call(*load_call(in_hbm(images), in_hbm(texts)), *got)
    near = {m: to_cube(own, m) for m in (4, 2, 1)}
    late = lax.optimization_barrier((own, near[1]))[0]
    far = {7: to_cube(late, 7), 5: to_cube(near[1], 4), 3: to_cube(near[2], 1), 6: to_cube(near[4], 2)}
    blocks = {0: own, **near, **far}
    in_vmem = lambda a: pltpu.with_memory_space_constraint(a, pltpu.VMEM)
    a_blocks = [in_vmem(blocks[m]) for m in ORDER]
    swapped = {m: swap(far[m]) for m in (7, 5, 3)}
    joined = [swap(a) for a in join_call(near[1], near[2], near[4])]
    last, *held = lax.optimization_barrier((far[6], swapped[7], swapped[5], swapped[3], *joined))
    swapped.update(zip((7, 5, 3), held))
    swapped[6] = swap(last)
    b_blocks = [other] + held[3:] + [swapped[m] for m in ORDER[4:]]
    b_blocks = [in_vmem(b) for b in b_blocks]

    e, a_stat, b_stat, flags = scores_call(a_blocks, b_blocks, scale)
    a_lse = merge_call(a_stat, swap(b_stat), 0)
    for m in (1, 2, 4):
        a_lse = merge_call(a_lse, to_cube(a_lse, m), m)
    b_lse = swap(a_lse)

    w, gb_hi = weights_call(flags, e, a_lse, b_lse, a_blocks)
    got_hi = swap(gb_hi)
    ga_hi, gb_lo = middle_call(w, a_blocks, b_blocks)
    got_lo = swap(gb_lo)
    p = dict(zip(ORDER[4:], far_call(ga_hi, got_hi)))
    from_xy = to_cube(p[3], 1)
    from_yz = to_cube(p[6], 2)
    from_xz = to_cube(p[5], 4)
    from_xyz = to_cube(p[7], 7)
    ga_lo = last_call(w, b_blocks)
    p0, p1, p2, p4 = near_call(ga_lo, got_lo, from_xy, from_yz, from_xz)
    wide = lambda a: a.astype(jnp.float32)
    parts = (p0, from_xyz, to_cube(p1, 1), to_cube(p2, 2), to_cube(p4, 4))
    add = lambda cut: functools.reduce(jnp.add, [wide(a[cut]) for a in parts])
    sent, kept = add(slice(rows, None)), add(slice(rows))
    got_sum = swap(sent)
    image_sum = jnp.where(first, kept, got_sum)
    text_sum = jnp.where(first, got_sum, kept)
    return (image_sum - wide(texts), text_sum - wide(images))


def solution(mesh):
    chips = Mesh(mesh.devices.reshape(SIZES), AXES)
    spec = P(AXES, None)
    return jax.shard_map(
        body,
        mesh=chips,
        in_specs=(spec, spec),
        out_specs=(spec, spec),
        check_vma=False,
    )
```
